32 devices in a mesh: blk: 8 (over y, x, core), tp: 4 (over z).
Axes of the slice: x: 2, y: 2, z: 4, core: 2. Of those that a mesh axis runs over, the one named last changes fastest.
Arguments:
- hidden_in: bfloat16 [1024, 4, 2048], P('blk'), may hold values from -6 to 6
- block_order: int32 [8], replicated, may hold values from 0 to 7, each once
- seq_labels: int32 [4], replicated, may hold values from 0 to 1
- exit_scales: float32 [2], replicated, may hold values from 0.4 to 2
- attn_gain: bfloat16 [2048], replicated, may hold values from 0.5 to 1.5
- w_query: bfloat16 [2048, 2048], P(None, 'tp'), may hold values from -0.125 to 0.125
- w_key: bfloat16 [2048, 1024], P(None, 'tp'), may hold values from -0.125 to 0.125
- w_value: bfloat16 [2048, 1024], P(None, 'tp'), may hold values from -0.125 to 0.125
- w_out: bfloat16 [2048, 2048], P('tp'), may hold values from -0.5 to 0.5
- mlp_gain: bfloat16 [2048], replicated, may hold values from 0.5 to 1.5
- w_gate: bfloat16 [2048, 5632], P(None, 'tp'), may hold values from -0.125 to 0.125
- w_up: bfloat16 [2048, 5632], P(None, 'tp'), may hold values from -0.125 to 0.125
- w_down: bfloat16 [5632, 2048], P('tp'), may hold values from -0.078125 to 0.078125
- d_out: bfloat16 [1024, 4, 2048], P('blk'), may hold values from -6 to 6
Outputs:
- block_out: bfloat16 [1024, 4, 2048], P('blk')
- d_hidden_in: float32 [1024, 4, 2048], P('blk')
- d_attn_gain: float32 [2048], P('blk')
- d_w_query: float32 [2048, 2048], P('blk', 'tp')
- d_w_key: float32 [2048, 1024], P('blk', 'tp')
- d_w_value: float32 [2048, 1024], P('blk', 'tp')
- d_w_out: float32 [2048, 2048], P('tp', 'blk')
- d_mlp_gain: float32 [2048], P('blk')
- d_w_gate: float32 [2048, 5632], P('blk', 'tp')
- d_w_up: float32 [2048, 5632], P('blk', 'tp')
- d_w_down: float32 [5632, 2048], P('tp', 'blk')
The draws below stay inside these ranges and needn't reach their ends.
Inputs may be any that keep to these rules, and one draw needn't show every extreme that they name: `block_order`: a permutation: each block of a sequence is held by exactly one index of blk.
All inputs are finite; a program needn't handle non-finite values.
Results may differ from the reference program's by a relative error of at most 0.025.
Values may be sent and summed in bfloat16 or wider, within the bound.
No kernel may reach another device: no remote copies, remote signals or barrier semaphores. Data moves between devices by JAX's collectives and lax.ppermute only.
A program may use at most 256 MiB of HBM per device.

```python
import math
from functools import partial
import jax
import jax.numpy as jnp
from jax import lax

D = 2048
HEADS = 16
KV_HEADS = 8
HEAD_DIM = 128
FF = 5632
LOC = 128
SEQS = 4
LENGTH = 1024
N_BLK = 8


def set_ends(entries, stream_key, smallest, largest):
    longest = entries.shape.index(max(entries.shape))
    spots = []
    for shift in (0, 1):
        where = [jax.random.randint(jax.random.fold_in(stream_key, axis), (), 0, length) for axis, length in enumerate(entries.shape)]
        where[longest] = (where[longest] + shift) % entries.shape[longest]
        spots.append(tuple(where))
    return entries.at[spots[0]].set(smallest).at[spots[1]].set(largest)


def raised(values, rng, source, target, shards_of, factor):
    owner, partner = [(jnp.arange(values.shape[position]) // (values.shape[position] // shards_of)).reshape([-1 if axis == position else 1 for axis in range(values.ndim)]) for position in (source, target)]
    chosen = jax.random.permutation(rng, shards_of)[partner]
    strong = (owner == chosen) | (owner == (partner + shards_of // 2) % shards_of)
    return jnp.where(strong, factor * values, values)


def level_of(stream_key, shape, pieces, least, high):
    def one(axis_at, shards_of):
        heights = jax.random.uniform(jax.random.fold_in(jax.random.fold_in(stream_key, 6), axis_at), (shards_of,), jnp.float32, least / len(pieces), high / len(pieces))
        return jnp.repeat(jnp.exp(heights), shape[axis_at] // shards_of).reshape((-1,) + (1,) * (len(shape) - axis_at - 1))

    level = one(*pieces[0])
    for cut in pieces[1:]:
        level = level * one(*cut)
    return level


def scatter_about(own_key, shape, spread, most, pieces=(), kind=jnp.bfloat16):
    array = jax.random.normal(own_key, shape, jnp.float32) * spread
    if len(pieces) > 0:
        array = level_of(own_key, shape, pieces, -0.22, 0.18) * array
    return jnp.clip(array, min=-most, max=most).astype(kind)


def noise_with(rng, dims, spread, most, cuts, heavy, kind=jnp.bfloat16):
    values = spread * jax.random.normal(rng, dims, jnp.float32)
    if cuts:
        values = values * level_of(rng, dims, cuts, -0.22, 0.18)
    return jnp.clip(raised(values, jax.random.fold_in(rng, 3), *heavy), -most, most).astype(kind)


def setup_inputs(seed: int = 0) -> dict:
    seeds = jax.random.split(jax.random.key(seed), 15)
    hidden_in = scatter_about(seeds[0], (LENGTH, SEQS, D), 1.0, 6.0, ((0, 8),))
    block_order = jax.random.permutation(seeds[1], N_BLK).astype(jnp.int32)
    seq_labels = set_ends(jax.random.randint(seeds[2], (SEQS,), 0, 2), jax.random.fold_in(seeds[2], 1), 0, 1).astype(jnp.int32)
    exit_scales = jnp.clip(jnp.exp(jax.random.uniform(seeds[3], (2,), jnp.float32, math.log(0.4), math.log(2.0))), 0.4, 2.0)
    attn_gain = jnp.clip(1.0 + 0.1 * jax.random.normal(seeds[4], (D,), jnp.float32), 0.5, 1.5).astype(jnp.bfloat16)
    w_query = scatter_about(seeds[5], (D, HEADS * HEAD_DIM), D ** -0.5, 0.125, ((1, 4),))
    w_key = scatter_about(seeds[6], (D, KV_HEADS * HEAD_DIM), D ** -0.5, 0.125, ((1, 4),))
    w_value = scatter_about(seeds[7], (D, KV_HEADS * HEAD_DIM), D ** -0.5, 0.125, ((1, 4),))
    w_out = scatter_about(seeds[8], (HEADS * HEAD_DIM, D), HEAD_DIM ** -0.5, 0.5, ((0, 4),))
    mlp_gain = jnp.clip(1.0 + 0.1 * jax.random.normal(seeds[9], (D,), jnp.float32), 0.5, 1.5).astype(jnp.bfloat16)
    w_gate = scatter_about(seeds[10], (D, FF), D ** -0.5, 0.125, ((1, 4),))
    w_up = scatter_about(seeds[11], (D, FF), D ** -0.5, 0.125, ((1, 4),))
    w_down = scatter_about(seeds[12], (FF, D), FF ** -0.5, 0.078125, ((0, 4),))
    d_out = noise_with(seeds[13], (LENGTH, SEQS, D), 1.0, 6.0, ((0, 8),), (0, 2, 8, 2.0))
    return {"hidden_in": hidden_in, "block_order": block_order, "seq_labels": seq_labels, "exit_scales": exit_scales, "attn_gain": attn_gain, "w_query": w_query, "w_key": w_key, "w_value": w_value, "w_out": w_out, "mlp_gain": mlp_gain, "w_gate": w_gate, "w_up": w_up, "w_down": w_down, "d_out": d_out}


HIGH = lax.Precision.HIGHEST
EPS = 1e-05
THETA = 10000.0

@jax.custom_vjp
def low(v):
    return lax.optimization_barrier(v.astype(jnp.bfloat16)).astype(jnp.float32)

@jax.custom_vjp
def low_back(v):
    return v

def low_keep(v):
    return (low(v), None)

def low_pass(kept, grad):
    return (grad,)

def back_keep(v):
    return (v, None)

def back_low(kept, grad):
    return (low(grad),)
low.defvjp(low_keep, low_pass)
low_back.defvjp(back_keep, back_low)

def rope_tables(positions):
    half = HEAD_DIM // 2
    freq = jnp.exp(jnp.arange(half, dtype=jnp.float32) * (-2.0 * math.log(THETA) / HEAD_DIM))
    angles = positions.astype(jnp.float32)[:, None] * freq[None, :]
    return (jnp.cos(angles), jnp.sin(angles))

def rotate(values, cosine, sine):
    half = values.shape[-1] // 2
    first = values[..., :half]
    second = values[..., half:]
    cosine = cosine[:, None, None, :]
    sine = sine[:, None, None, :]
    return jnp.concatenate([first * cosine - second * sine, second * cosine + first * sine], axis=-1)

def rms_norm(values, gain):
    return values * lax.rsqrt(lax.optimization_barrier(jnp.mean(values * values, axis=-1, keepdims=True)) + EPS) * gain

def project(values, weight):
    return jnp.einsum('lsd,de->lse', values, weight, precision=HIGH)

def attend_block(query_block, query_pos, keys, vals, key_pos):
    scale = HEAD_DIM ** (-0.5)
    wide_keys = jnp.repeat(keys, HEADS // KV_HEADS, axis=1)
    wide_vals = jnp.repeat(vals, HEADS // KV_HEADS, axis=1)
    raw = low_back(jnp.einsum('qhd,khd->hqk', query_block, wide_keys, precision=HIGH))
    mask = key_pos[None, None, :] <= query_pos[None, :, None]
    scores = jnp.where(mask, raw * scale, -1e+30)
    top = lax.optimization_barrier(jnp.max(scores, axis=-1, keepdims=True))
    weights = jnp.where(mask, jnp.exp(scores - top), 0.0)
    probs = weights / lax.optimization_barrier(jnp.sum(weights, axis=-1, keepdims=True))
    return jnp.einsum('hqk,khd->qhd', low(probs), wide_vals, precision=HIGH)

def attend_sequence(query_seq, key_seq, val_seq, positions):
    rows = math.gcd(512, LENGTH)
    query_blocks = query_seq.reshape(LENGTH // rows, rows, HEADS, HEAD_DIM)
    pos_blocks = positions.reshape(LENGTH // rows, rows)
    block_fn = jax.checkpoint(attend_block)
    result = lax.map(lambda item: block_fn(item[0], item[1], key_seq, val_seq, positions), (query_blocks, pos_blocks))
    return result.reshape(LENGTH, HEADS, HEAD_DIM)

def forward(positions, cosine, sine, hidden_in, attn_gain, w_query, w_key, w_value, w_out, mlp_gain, w_gate, w_up, w_down):
    normed = low(rms_norm(hidden_in, attn_gain))
    query = low(rotate(low_back(project(normed, w_query)).reshape(LENGTH, SEQS, HEADS, HEAD_DIM), cosine, sine))
    keys = low(rotate(low_back(project(normed, w_key)).reshape(LENGTH, SEQS, KV_HEADS, HEAD_DIM), cosine, sine))
    vals = low(low_back(project(normed, w_value))).reshape(LENGTH, SEQS, KV_HEADS, HEAD_DIM)
    mixed = lax.map(lambda item: attend_sequence(item[0], item[1], item[2], positions), (query.transpose(1, 0, 2, 3), keys.transpose(1, 0, 2, 3), vals.transpose(1, 0, 2, 3)))
    mixed = low(low_back(mixed.transpose(1, 0, 2, 3).reshape(LENGTH, SEQS, HEADS * HEAD_DIM)))
    resid = hidden_in + low_back(project(mixed, w_out))
    normed_m = low(rms_norm(resid, mlp_gain))
    gate = low_back(project(normed_m, w_gate))
    up = low_back(project(normed_m, w_up))
    hidden = low(jax.nn.silu(gate) * up)
    return resid + low_back(project(hidden, w_down))

def reference(hidden_in, block_order, seq_labels, exit_scales, attn_gain, w_query, w_key, w_value, w_out, mlp_gain, w_gate, w_up, w_down, d_out):
    positions = (block_order[:, None] * LOC + jnp.arange(LOC, dtype=jnp.int32)[None, :]).reshape(LENGTH).astype(jnp.int32)
    cosine, sine = rope_tables(positions)
    floats = [a.astype(jnp.float32) for a in (hidden_in, attn_gain, w_query, w_key, w_value, w_out, mlp_gain, w_gate, w_up, w_down)]
    result, pullback = jax.vjp(partial(forward, positions, cosine, sine), *floats)
    scale_rows = jnp.where(seq_labels == 1, exit_scales[1], exit_scales[0])
    cot = d_out.astype(jnp.float32) * scale_rows[None, :, None]
    grads = pullback(cot)
    return (result.astype(jnp.bfloat16), grads[0], grads[1], grads[2], grads[3], grads[4], grads[5], grads[6], grads[7], grads[8], grads[9])
```

```python
import functools
import math

import jax
import jax.numpy as jnp
from jax import lax
from jax.experimental import pallas as pl
from jax.experimental.pallas import tpu as pltpu
from jax.sharding import PartitionSpec as P

HEAD_DIM = 128
EPS = 1e-05
THETA = 10000.0
NEG = -1e30
F32 = jnp.float32
BF16 = jnp.bfloat16
MIB = 1024 * 1024


def dot(left, right):
    return lax.dot_general(left, right, (((1,), (0,)), ((), ())), preferred_element_type=F32)


def dot_rt(left, right):
    return lax.dot_general(left, right, (((1,), (1,)), ((), ())), preferred_element_type=F32)


def dot_lt(left, right):
    return lax.dot_general(left, right, (((0,), (0,)), ((), ())), preferred_element_type=F32)


def params(limit):
    return pltpu.CompilerParams(vmem_limit_bytes=limit * MIB)


def cost(flops, moved):
    return pl.CostEstimate(flops=int(flops), bytes_accessed=int(moved), transcendentals=0)


SMEM = pl.BlockSpec(memory_space=pltpu.SMEM)
VMEM = pl.BlockSpec(memory_space=pltpu.VMEM)


def project_kernel(heads, kv, x_ref, gain_ref, cos_ref, sin_ref, wq_ref, wk_ref, wv_ref, msg_ref, norm_ref):
    group = heads // kv
    seqs, loc, width = x_ref.shape
    gain = gain_ref[...].astype(F32)
    for s in range(seqs):
        x = x_ref[s].astype(F32)
        inv = lax.rsqrt(jnp.mean(x * x, axis=-1, keepdims=True) + EPS)
        norm_ref[s] = (x * inv * gain).astype(BF16)
    normed = norm_ref[...].reshape(seqs * loc, width)
    cosine, sine = cos_ref[...], sin_ref[...]

    def rot(t):
        return (t * cosine + pltpu.roll(t, HEAD_DIM // 2, 1) * sine).astype(BF16)

    def put(res, h, s, n, slot, turn):
        part = res[s * loc:(s + 1) * loc, h * HEAD_DIM:(h + 1) * HEAD_DIM]
        msg_ref[s * kv + n, :, slot * HEAD_DIM:(slot + 1) * HEAD_DIM] = rot(part) if turn else part.astype(BF16)

    query = dot(normed, wq_ref[...])
    for s in range(seqs):
        for h in range(heads):
            put(query, h, s, h // group, h % group, True)
    keys = dot(normed, wk_ref[...])
    for s in range(seqs):
        for n in range(kv):
            put(keys, n, s, n, group, True)
    vals = dot(normed, wv_ref[...])
    for s in range(seqs):
        for n in range(kv):
            put(vals, n, s, n, group + 1, False)


def project(x, gain, cosine, sine, wq, wk, wv):
    seqs, loc, width = x.shape
    heads, kv = wq.shape[1] // HEAD_DIM, wk.shape[1] // HEAD_DIM
    cols = (heads // kv + 2) * HEAD_DIM
    flops = 2 * seqs * loc * width * (wq.shape[1] + 2 * wk.shape[1])
    return pl.pallas_call(
        functools.partial(project_kernel, heads, kv),
        out_shape=(jax.ShapeDtypeStruct((seqs * kv, loc, cols), BF16), jax.ShapeDtypeStruct(x.shape, BF16)),
        in_specs=[VMEM] * 7,
        out_specs=(VMEM, VMEM),
        compiler_params=params(32),
        cost_estimate=cost(flops, 12 * MIB),
    )(x, gain, cosine, sine, wq, wk, wv)


def attend_kernel(group, at_ref, rec_ref, out_ref, full_ref, lse_ref, keys, vals):
    blocks, loc, _ = rec_ref.shape
    base = group * HEAD_DIM
    for p in range(blocks):
        i = at_ref[p]
        keys[p * loc:(p + 1) * loc, :] = rec_ref[i, :, base:base + HEAD_DIM]
        vals[p * loc:(p + 1) * loc, :] = rec_ref[i, :, base + HEAD_DIM:base + 2 * HEAD_DIM]
    rows = lax.broadcasted_iota(jnp.int32, (group * loc, loc), 0) % loc
    cols = lax.broadcasted_iota(jnp.int32, (group * loc, loc), 1)
    keep = cols <= rows
    for p in range(blocks):
        i = at_ref[p]
        count = (p + 1) * loc
        query = jnp.concatenate([rec_ref[i, :, g * HEAD_DIM:(g + 1) * HEAD_DIM] for g in range(group)], axis=0)
        scores = dot_rt(query, keys[:count, :]) * (HEAD_DIM ** -0.5)
        last = jnp.where(keep, scores[:, count - loc:], NEG)
        scores = jnp.concatenate([scores[:, :count - loc], last], axis=1) if p else last
        top = jnp.max(scores, axis=-1, keepdims=True)
        weights = jnp.exp(scores - top)
        total = jnp.sum(weights, axis=-1, keepdims=True)
        mixed = dot(weights.astype(BF16), vals[:count, :]) / total
        lse_ref[p] = jnp.broadcast_to(top + jnp.log(total), (group * loc, HEAD_DIM))
        full_ref[p] = mixed
        for g in range(group):
            out_ref[i, :, g * HEAD_DIM:(g + 1) * HEAD_DIM] = mixed[g * loc:(g + 1) * loc].astype(BF16)


def attend(at, rec, group):
    blocks, loc, _ = rec.shape
    total = blocks * loc
    return pl.pallas_call(
        functools.partial(attend_kernel, group),
        out_shape=(
            jax.ShapeDtypeStruct((blocks, loc, group * HEAD_DIM), BF16),
            jax.ShapeDtypeStruct((blocks, group * loc, HEAD_DIM), F32),
            jax.ShapeDtypeStruct((blocks, group * loc, HEAD_DIM), F32),
        ),
        in_specs=[SMEM, VMEM],
        out_specs=(VMEM,) * 3,
        scratch_shapes=[pltpu.VMEM((total, HEAD_DIM), BF16)] * 2,
        compiler_params=params(32),
        cost_estimate=cost(3 * group * total * total * HEAD_DIM, 4 * MIB),
    )(at, rec)


def attend_back_kernel(group, at_ref, rec_ref, grad_ref, full_ref, lse_ref, cos_ref, sin_ref, out_ref, keys, vals, d_keys, d_vals):
    blocks, loc, _ = rec_ref.shape
    base = group * HEAD_DIM
    scale = HEAD_DIM ** -0.5
    for p in range(blocks):
        i = at_ref[p]
        keys[p * loc:(p + 1) * loc, :] = rec_ref[i, :, base:base + HEAD_DIM]
        vals[p * loc:(p + 1) * loc, :] = rec_ref[i, :, base + HEAD_DIM:base + 2 * HEAD_DIM]
    rows = lax.broadcasted_iota(jnp.int32, (group * loc, loc), 0) % loc
    cols = lax.broadcasted_iota(jnp.int32, (group * loc, loc), 1)
    keep = cols <= rows

    def unrot(t, cosine, sine):
        return (t * cosine - pltpu.roll(t, HEAD_DIM // 2, 1) * sine).astype(BF16)

    for p in reversed(range(blocks)):
        i = at_ref[p]
        count = (p + 1) * loc
        span = slice(p * loc, count)
        query = jnp.concatenate([rec_ref[i, :, g * HEAD_DIM:(g + 1) * HEAD_DIM] for g in range(group)], axis=0)
        grad = jnp.concatenate([grad_ref[i, :, g * HEAD_DIM:(g + 1) * HEAD_DIM] for g in range(group)], axis=0)
        lse = lse_ref[p][:, :1]
        delta = jnp.sum(grad.astype(F32) * full_ref[p], axis=-1, keepdims=True)
        probs = jnp.exp(dot_rt(query, keys[:count, :]) * scale - lse)
        last = jnp.where(keep, probs[:, count - loc:], 0.0)
        probs = jnp.concatenate([probs[:, :count - loc], last], axis=1) if p else last
        d_probs = dot_rt(grad, vals[:count, :])
        g_scores = (probs * (d_probs - delta) * scale).astype(BF16)
        d_query = dot(g_scores, keys[:count, :])
        dk = dot_lt(g_scores, query)
        dv = dot_lt(probs.astype(BF16), grad)
        if p == blocks - 1:
            d_keys[...] = dk
            d_vals[...] = dv
        else:
            d_keys[:count, :] += dk
            d_vals[:count, :] += dv
        cosine, sine = cos_ref[span, :], sin_ref[span, :]
        for g in range(group):
            out_ref[i, :, g * HEAD_DIM:(g + 1) * HEAD_DIM] = unrot(d_query[g * loc:(g + 1) * loc], cosine, sine)
        out_ref[i, :, base:base + HEAD_DIM] = unrot(d_keys[span, :], cosine, sine)
        out_ref[i, :, base + HEAD_DIM:base + 2 * HEAD_DIM] = d_vals[span, :].astype(BF16)


def attend_back(at, rec, grad, full, lse, cosine, sine, group):
    blocks, loc, cols = rec.shape
    total = blocks * loc
    return pl.pallas_call(
        functools.partial(attend_back_kernel, group),
        out_shape=jax.ShapeDtypeStruct((blocks, loc, cols), BF16),
        in_specs=[SMEM] + [VMEM] * 6,
        out_specs=VMEM,
        scratch_shapes=[pltpu.VMEM((total, HEAD_DIM), BF16)] * 2 + [pltpu.VMEM((total, HEAD_DIM), F32)] * 2,
        compiler_params=params(40),
        cost_estimate=cost(7 * group * total * total * HEAD_DIM, 6 * MIB),
    )(at, rec, grad, full, lse, cosine, sine)


def out_kernel(kv, mix_ref, w_ref, cat_ref, *outs):
    cols = mix_ref.shape[2]
    for s, out in enumerate(outs):
        cat_ref[s] = jnp.concatenate([mix_ref[s * kv + n] for n in range(kv)], axis=1)
        out[...] = dot(cat_ref[s], w_ref[...]).astype(BF16)


def out_project(mixed, w_out, seqs):
    units, loc, cols = mixed.shape
    kv = units // seqs
    width = w_out.shape[1]
    res = pl.pallas_call(
        functools.partial(out_kernel, kv),
        out_shape=(jax.ShapeDtypeStruct((seqs, loc, kv * cols), BF16),)
        + (jax.ShapeDtypeStruct((loc, width), BF16),) * seqs,
        in_specs=[VMEM] * 2,
        out_specs=(VMEM,) * (seqs + 1),
        compiler_params=params(24),
        cost_estimate=cost(2 * seqs * loc * kv * cols * width, 5 * MIB),
    )(mixed, w_out)
    return res[0], res[1:]


def rope_tables(positions, head_dim):
    half = head_dim // 2
    freq = jnp.exp(jnp.arange(half, dtype=jnp.float32) * (-2.0 * math.log(THETA) / head_dim))
    angles = positions.astype(jnp.float32)[:, None] * freq[None, :]
    return (jnp.cos(angles), jnp.sin(angles))


def rotate(values, cosine, sine):
    half = values.shape[-1] // 2
    first = values[..., :half]
    second = values[..., half:]
    cosine = cosine[:, None, None, :]
    sine = sine[:, None, None, :]
    return jnp.concatenate(
        [first * cosine - second * sine, second * cosine + first * sine], axis=-1
    )


def inverse_rms(values):
    return lax.rsqrt(jnp.mean(values * values, axis=-1, keepdims=True) + EPS)


def norm_back(values, inverse, gain, grad):
    unit = values * inverse
    scaled = grad * gain
    back = inverse * (scaled - unit * jnp.mean(scaled * unit, axis=-1, keepdims=True))
    return (back, jnp.sum(grad * unit, axis=(0, 1)))


def matmul(values, weight):
    return jnp.einsum("lsd,de->lse", values, weight, preferred_element_type=jnp.float32)


def matmul_back(values, weight):
    return jnp.einsum("lse,de->lsd", values, weight, preferred_element_type=jnp.float32)


def weight_grad(left, right):
    return jnp.einsum("lsd,lse->de", left, right, preferred_element_type=jnp.float32)


def general(
    hidden_in,
    block_order,
    seq_labels,
    exit_scales,
    attn_gain,
    w_query,
    w_key,
    w_value,
    w_out,
    mlp_gain,
    w_gate,
    w_up,
    w_down,
    d_out,
):
    f32 = jnp.float32
    bf16 = jnp.bfloat16
    loc, seqs, width = hidden_in.shape
    head_dim = HEAD_DIM
    q_heads = w_query.shape[1] // head_dim
    kv_heads = w_key.shape[1] // head_dim
    group = q_heads // kv_heads
    scale = head_dim ** (-0.5)
    blocks_all = block_order.shape[0]
    total_rows = loc * lax.axis_size("blk")
    key_rows = math.gcd(512, total_rows)
    block_count = total_rows // key_rows
    kv_width = 2 * kv_heads * head_dim
    positions = block_order[lax.axis_index("blk")] * loc + jnp.arange(loc, dtype=jnp.int32)
    cosine, sine = rope_tables(positions, head_dim)

    def key_positions(start, count):
        index = start + jnp.arange(count, dtype=jnp.int32)
        owner = index // loc
        table = jnp.sum(
            jnp.where(
                owner[:, None] == jnp.arange(blocks_all, dtype=jnp.int32)[None, :],
                block_order[None, :],
                0,
            ),
            axis=1,
        )
        return table * loc + index % loc

    xin = hidden_in.astype(f32)
    inv_a = inverse_rms(xin)
    gain_a = attn_gain.astype(f32)
    normed = (xin * inv_a * gain_a).astype(bf16)
    query_bf = rotate(
        matmul(normed, w_query).reshape(loc, seqs, q_heads, head_dim), cosine, sine
    ).astype(bf16)
    keys_bf = (
        rotate(matmul(normed, w_key).reshape(loc, seqs, kv_heads, head_dim), cosine, sine)
        .astype(bf16)
        .reshape(loc, seqs, kv_heads * head_dim)
    )
    vals_bf = matmul(normed, w_value).astype(bf16)
    query_g = query_bf.reshape(loc, seqs, kv_heads, group, head_dim)
    starts = jnp.arange(block_count, dtype=jnp.int32) * key_rows
    top = jnp.full((seqs, kv_heads, group, loc), NEG, f32)
    key_part = lax.all_gather(keys_bf, "blk", axis=0, tiled=True)
    val_part = lax.all_gather(vals_bf, "blk", axis=0, tiled=True)
    count = key_part.shape[0]
    kk = key_part.reshape(count, seqs, kv_heads, head_dim)
    vv = val_part.reshape(count, seqs, kv_heads, head_dim)
    mask = key_positions(jnp.int32(0), count)[None, :] <= positions[:, None]
    raw = jnp.einsum("lsngd,msnd->snglm", query_g, kk, preferred_element_type=f32)
    scores = jnp.where(mask, raw * scale, NEG)
    new_top = jnp.maximum(top, jnp.max(scores, axis=-1))
    weights = jnp.where(mask, jnp.exp(scores - new_top[..., None]), 0.0)
    total = jnp.sum(weights, axis=-1)
    acc = jnp.einsum("snglm,msnd->sngld", weights.astype(bf16), vv, preferred_element_type=f32)
    top, total, acc = (new_top, total, acc)
    lse = top + jnp.log(total)
    mixed_raw = acc / total[..., None]
    mixed_bf = (
        mixed_raw.transpose(3, 0, 1, 2, 4).reshape(loc, seqs, q_heads * head_dim).astype(bf16)
    )
    resid = xin + lax.psum(matmul(mixed_bf, w_out).astype(jnp.bfloat16), "tp").astype(jnp.float32)
    inv_m = inverse_rms(resid)
    gain_m = mlp_gain.astype(f32)
    normed_m = (resid * inv_m * gain_m).astype(bf16)
    gate = matmul(normed_m, w_gate)
    up = matmul(normed_m, w_up)
    sig = jax.nn.sigmoid(gate)
    silu = gate * sig
    hidden = (silu * up).astype(bf16)
    output = resid + lax.psum(matmul(hidden, w_down).astype(jnp.bfloat16), "tp").astype(jnp.float32)
    block_out = output.astype(bf16)
    scale_rows = jnp.where(seq_labels == 1, exit_scales[1], exit_scales[0])
    cot = d_out.astype(f32) * scale_rows[None, :, None]
    g_down = cot.astype(bf16)
    d_w_down = weight_grad(hidden, g_down)
    d_hidden = matmul_back(g_down, w_down)
    g_up = (d_hidden * silu).astype(bf16)
    g_gate = (d_hidden * up * (sig * (1.0 + gate * (1.0 - sig)))).astype(bf16)
    d_w_gate = weight_grad(normed_m, g_gate)
    d_w_up = weight_grad(normed_m, g_up)
    d_nm = lax.psum(
        (matmul_back(g_gate, w_gate) + matmul_back(g_up, w_up)).astype(jnp.bfloat16), "tp"
    ).astype(jnp.float32)
    d_resid_norm, d_mlp_gain = norm_back(resid, inv_m, gain_m, d_nm)
    d_resid = cot + d_resid_norm
    g_attn = d_resid.astype(bf16)
    d_w_out = weight_grad(mixed_bf, g_attn)
    g_mixed = matmul_back(g_attn, w_out).astype(bf16)
    g_mixed_g = g_mixed.reshape(loc, seqs, kv_heads, group, head_dim)
    delta = jnp.sum(g_mixed_g.astype(f32).transpose(1, 2, 3, 0, 4) * mixed_raw, axis=-1)
    whole_keys, whole_vals = (
        lax.all_gather(keys_bf, "blk", axis=0, tiled=True),
        lax.all_gather(vals_bf, "blk", axis=0, tiled=True),
    )

    def probe(kk, vv, start, count):
        mask = key_positions(start, count)[None, :] <= positions[:, None]
        raw = jnp.einsum("lsngd,msnd->snglm", query_g, kk, preferred_element_type=f32)
        probs = jnp.where(mask, jnp.exp(raw * scale - lse[..., None]), 0.0)
        d_probs = jnp.einsum("lsngd,msnd->snglm", g_mixed_g, vv, preferred_element_type=f32)
        g_scores = (probs * (d_probs - delta[..., None]) * scale).astype(bf16)
        return (g_scores, probs)

    def kv_pair(g_scores, probs, count):
        d_keys = jnp.einsum("snglm,lsngd->msnd", g_scores, query_g, preferred_element_type=f32)
        d_vals = jnp.einsum(
            "snglm,lsngd->msnd", probs.astype(bf16), g_mixed_g, preferred_element_type=f32
        )
        return jnp.concatenate([d_keys, d_vals], axis=2).reshape(count, seqs, kv_width)

    scan_items = (
        whole_keys.reshape(block_count, key_rows, seqs, -1),
        whole_vals.reshape(block_count, key_rows, seqs, -1),
        starts,
    )
    zero_query = jnp.zeros((loc, seqs, kv_heads, group, head_dim), f32)

    def back_step(d_query, item):
        key_part, val_part, start = item
        kk = key_part.reshape(key_rows, seqs, kv_heads, head_dim)
        vv = val_part.reshape(key_rows, seqs, kv_heads, head_dim)
        g_scores, probs = probe(kk, vv, start, key_rows)
        d_query = d_query + jnp.einsum(
            "snglm,msnd->lsngd", g_scores, kk, preferred_element_type=f32
        )
        return (d_query, kv_pair(g_scores, probs, key_rows))

    d_query, kv_terms = lax.scan(back_step, zero_query, scan_items)
    kv_local = lax.psum_scatter(
        kv_terms.reshape(total_rows, seqs, kv_width).astype(jnp.bfloat16),
        "blk",
        scatter_dimension=0,
        tiled=True,
    ).astype(jnp.float32)
    kv_local = kv_local.reshape(loc, seqs, 2, kv_heads, head_dim)
    g_q = (
        rotate(d_query.reshape(loc, seqs, q_heads, head_dim), cosine, -sine)
        .astype(bf16)
        .reshape(loc, seqs, q_heads * head_dim)
    )
    g_k = (
        rotate(kv_local[:, :, 0], cosine, -sine)
        .astype(bf16)
        .reshape(loc, seqs, kv_heads * head_dim)
    )
    g_v = kv_local[:, :, 1].astype(bf16).reshape(loc, seqs, kv_heads * head_dim)
    d_w_query = weight_grad(normed, g_q)
    d_w_key = weight_grad(normed, g_k)
    d_w_value = weight_grad(normed, g_v)
    d_n = lax.psum(
        (matmul_back(g_q, w_query) + matmul_back(g_k, w_key) + matmul_back(g_v, w_value)).astype(
            jnp.bfloat16
        ),
        "tp",
    ).astype(jnp.float32)
    d_in_norm, d_attn_gain = norm_back(xin, inv_a, gain_a, d_n)
    d_hidden_in = d_resid + d_in_norm
    d_attn_gain, d_w_query, d_w_key, d_w_value, d_w_out, d_mlp_gain, d_w_gate, d_w_up, d_w_down = (
        lax.psum_scatter(
            d_attn_gain.astype(jnp.bfloat16), "blk", scatter_dimension=0, tiled=True
        ).astype(jnp.float32),
        lax.psum_scatter(
            d_w_query.astype(jnp.bfloat16), "blk", scatter_dimension=0, tiled=True
        ).astype(jnp.float32),
        lax.psum_scatter(
            d_w_key.astype(jnp.bfloat16), "blk", scatter_dimension=0, tiled=True
        ).astype(jnp.float32),
        lax.psum_scatter(
            d_w_value.astype(jnp.bfloat16), "blk", scatter_dimension=0, tiled=True
        ).astype(jnp.float32),
        lax.psum_scatter(
            d_w_out.astype(jnp.bfloat16), "blk", scatter_dimension=1, tiled=True
        ).astype(jnp.float32),
        lax.psum_scatter(
            d_mlp_gain.astype(jnp.bfloat16), "blk", scatter_dimension=0, tiled=True
        ).astype(jnp.float32),
        lax.psum_scatter(
            d_w_gate.astype(jnp.bfloat16), "blk", scatter_dimension=0, tiled=True
        ).astype(jnp.float32),
        lax.psum_scatter(
            d_w_up.astype(jnp.bfloat16), "blk", scatter_dimension=0, tiled=True
        ).astype(jnp.float32),
        lax.psum_scatter(
            d_w_down.astype(jnp.bfloat16), "blk", scatter_dimension=1, tiled=True
        ).astype(jnp.float32),
    )
    return (
        block_out,
        d_hidden_in,
        d_attn_gain,
        d_w_query,
        d_w_key,
        d_w_value,
        d_w_out,
        d_mlp_gain,
        d_w_gate,
        d_w_up,
        d_w_down,
    )


def send_in(part):
    return part + lax.ppermute(part, "tp", [(0, 1), (3, 2)])


def sum_line(part, middle):
    half = send_in(part)
    total = half + lax.ppermute(half, "tp", [(1, 2), (2, 1)])
    ends = lax.ppermute(total, "tp", [(1, 0), (2, 3)])
    return jnp.where(middle, total, ends)


def partner(bit):
    return [(i, i ^ bit) for i in range(8)]


def pick(parts, index, axis):
    return lax.dynamic_index_in_dim(parts, index, axis, keepdims=False)


def scatter_sum(parts):
    dtype = parts.dtype
    me = lax.axis_index("blk")
    core, east, north = me % 2, (me // 2) % 2, me // 4
    rows = parts.shape[0] // 8
    parts = parts.reshape((2, 2, 2, rows) + parts.shape[1:])

    def step(values, mine, axis, bit):
        got = lax.ppermute(pick(values, 1 - mine, axis), "blk", partner(bit))
        return pick(values, mine, axis).astype(F32) + got.astype(F32)

    parts = step(parts, core, 2, 1).astype(dtype)
    left, right = parts[:, :, :rows // 2], parts[:, :, rows // 2:]
    left = step(left, east, 1, 2).astype(dtype)
    right = step(right, north, 0, 4).astype(dtype)
    left = step(left, north, 0, 4)
    right = step(right, east, 0, 2)
    return jnp.concatenate([left, right], axis=0)


def sum_gain(gains):
    gains = gains + lax.ppermute(gains, "tp", [(0, 1), (1, 0), (2, 3), (3, 2)])
    gains = gains + lax.ppermute(gains, "tp", [(0, 2), (2, 0), (1, 3), (3, 1)])
    return scatter_sum(gains)


def inverse(values):
    return lax.rsqrt(jnp.mean(values * values, axis=-1, keepdims=True) + EPS)


def tables(positions):
    cosine, sine = rope_tables(positions, HEAD_DIM)
    return jnp.concatenate([cosine, cosine], axis=1), jnp.concatenate([-sine, sine], axis=1)


def fast(
    hidden_in,
    block_order,
    seq_labels,
    exit_scales,
    attn_gain,
    w_query,
    w_key,
    w_value,
    w_out,
    mlp_gain,
    w_gate,
    w_up,
    w_down,
    d_out,
):
    loc, seqs, width = hidden_in.shape
    blocks = block_order.shape[0]
    kv = w_key.shape[1] // HEAD_DIM
    group = w_query.shape[1] // w_key.shape[1]
    me = lax.axis_index("blk")
    line = lax.axis_index("tp")
    middle = (line == 1) | (line == 2)
    index = jnp.arange(blocks, dtype=jnp.int32)
    at = jnp.sum(jnp.where(block_order[None, :] == index[:, None], index[None, :], 0), axis=1)
    mine = block_order[me] * loc + jnp.arange(loc, dtype=jnp.int32)

    x = hidden_in.transpose(1, 0, 2)
    cosine, sine = tables(mine)
    messages, normed = project(x, attn_gain[None, :], cosine, sine, w_query, w_key, w_value)
    rec = lax.all_to_all(messages, "blk", 0, 0, tiled=True)
    mixed, full, lse = attend(at, rec, group)
    mixed = lax.all_to_all(mixed, "blk", 0, 0, tiled=True)
    mixed, parts = out_project(mixed, w_out, seqs)
    attn = [sum_line(p, middle) for p in parts]

    scales = jnp.where(seq_labels == 1, exit_scales[1], exit_scales[0])
    cot = d_out.transpose(1, 0, 2).astype(F32) * scales[:, None, None]
    g_down = cot.astype(BF16)
    gain_m = mlp_gain.astype(F32)
    norms, hiddens, gates, ups, grads, gains = [], [], [], [], [], []
    span = 2
    for first in range(0, seqs, span):
        part = slice(first, first + span)
        rows = span * loc
        total = jnp.concatenate(attn[part], axis=0).astype(F32)
        resid = x[part].reshape(rows, width).astype(F32) + total
        unit = resid * inverse(resid)
        norm = (unit * gain_m).astype(BF16)
        gate = dot(norm, w_gate)
        up = dot(norm, w_up)
        sig = jax.nn.sigmoid(gate)
        silu = gate * sig
        d_hidden = dot_rt(g_down[part].reshape(rows, width), w_down)
        g_up = (d_hidden * silu).astype(BF16)
        g_gate = (d_hidden * up * (sig * (1.0 + gate * (1.0 - sig)))).astype(BF16)
        grad = dot_rt(g_gate, w_gate) + dot_rt(g_up, w_up)
        gains.append(jnp.sum(grad * unit, axis=0))
        grad = grad.astype(BF16)
        grads += [grad[i * loc:(i + 1) * loc] for i in range(span)]
        norms.append(norm)
        hiddens.append((silu * up).astype(BF16))
        gates.append(g_gate)
        ups.append(g_up)
    norm = jnp.concatenate(norms, axis=0)
    hidden = jnp.concatenate(hiddens, axis=0)
    d_mlp = gains[0] + gains[1]
    d_norm = [sum_line(g, middle) for g in grads]

    d_w_down = dot_lt(hidden, g_down.reshape(seqs * loc, width)).astype(BF16)
    d_w_down = lax.psum_scatter(d_w_down, "blk", scatter_dimension=1, tiled=True).astype(F32)
    g_both = jnp.concatenate([jnp.concatenate(gates, axis=0), jnp.concatenate(ups, axis=0)], axis=1)
    d_w_both = dot_lt(norm, g_both).astype(BF16)
    d_w_both = lax.psum_scatter(d_w_both, "blk", scatter_dimension=0, tiled=True).astype(F32)
    units = w_gate.shape[1]
    d_w_gate, d_w_up = d_w_both[:, :units], d_w_both[:, units:]

    d_resids, g_attns, sends = [], [], []
    for s in range(seqs):
        resid = x[s].astype(F32) + attn[s].astype(F32)
        inv = inverse(resid)
        unit = resid * inv
        scaled = d_norm[s].astype(F32) * gain_m
        d_resid = cot[s] + inv * (scaled - unit * jnp.mean(scaled * unit, axis=-1, keepdims=True))
        g_attn = d_resid.astype(BF16)
        g_mixed = dot_rt(g_attn, w_out).astype(BF16)
        sends += [g_mixed[:, n * group * HEAD_DIM:(n + 1) * group * HEAD_DIM] for n in range(kv)]
        d_resids.append(d_resid)
        g_attns.append(g_attn)
    g_attn = jnp.stack(g_attns)
    grad = lax.all_to_all(jnp.stack(sends), "blk", 0, 0, tiled=True)
    cosine, sine = tables(jnp.arange(blocks * loc, dtype=jnp.int32))
    back = attend_back(at, rec, grad, full, lse, cosine, sine, group)
    back = lax.all_to_all(back, "blk", 0, 0, tiled=True)
    back = back.reshape(seqs, kv, loc, (group + 2) * HEAD_DIM)

    out_parts = [dot(hidden[s * loc:(s + 1) * loc], w_down).astype(BF16) for s in range(seqs)]
    outs = [sum_line(p, middle) for p in out_parts]
    block_out = jnp.stack(
        [x[s].astype(F32) + attn[s].astype(F32) + outs[s].astype(F32) for s in range(seqs)], axis=1
    ).astype(BF16)

    wide = group * HEAD_DIM
    stacked = jnp.concatenate(
        [w_query.reshape(width, kv, wide), w_key.reshape(width, kv, HEAD_DIM), w_value.reshape(width, kv, HEAD_DIM)],
        axis=2,
    )
    gain_a = attn_gain.astype(F32)
    grads, d_attn = [], 0.0
    for s in range(seqs):
        grad = sum(dot_rt(back[s, n], stacked[:, n]) for n in range(kv))
        xs = x[s].astype(F32)
        d_attn = d_attn + jnp.sum(grad * (xs * inverse(xs)), axis=0)
        grads.append(grad.astype(BF16))
    totals = [sum_line(g, middle) for g in grads]
    d_gains = sum_gain(jnp.stack([d_attn, d_mlp], axis=1))

    d_w_attn = jnp.einsum("srd,snrc->dnc", normed, back, preferred_element_type=F32).astype(BF16)
    d_w_out = jnp.einsum("srd,src->dc", g_attn, mixed, preferred_element_type=F32).astype(BF16)
    packed = jnp.concatenate([d_w_attn.reshape(width, -1), d_w_out], axis=1)
    packed = scatter_sum(packed)
    cut = kv * (group + 2) * HEAD_DIM
    d_w_out = packed[:, cut:].T
    d_w_attn = packed[:, :cut].reshape(-1, kv, (group + 2) * HEAD_DIM)
    d_w_query = d_w_attn[:, :, :wide].reshape(-1, kv * wide)
    d_w_key = d_w_attn[:, :, wide:wide + HEAD_DIM].reshape(-1, kv * HEAD_DIM)
    d_w_value = d_w_attn[:, :, wide + HEAD_DIM:].reshape(-1, kv * HEAD_DIM)

    d_ins = []
    for s in range(seqs):
        xs = x[s].astype(F32)
        inv = inverse(xs)
        unit = xs * inv
        scaled = totals[s].astype(F32) * gain_a
        d_ins.append(d_resids[s] + inv * (scaled - unit * jnp.mean(scaled * unit, axis=-1, keepdims=True)))
    d_hidden_in = jnp.stack(d_ins, axis=1)
    return (
        block_out,
        d_hidden_in,
        d_gains[:, 0],
        d_w_query,
        d_w_key,
        d_w_value,
        d_w_out,
        d_gains[:, 1],
        d_w_gate,
        d_w_up,
        d_w_down,
    )


def per_device(*args):
    seqs = args[0].shape[1]
    kv_heads = args[6].shape[1] // HEAD_DIM
    fits = lax.axis_size("blk") == 8 and lax.axis_size("tp") == 4 and seqs * kv_heads == 8
    return (fast if fits else general)(*args)


def solution(mesh):
    return jax.shard_map(
        per_device,
        mesh=mesh,
        in_specs=(
            P("blk", None, None),
            P(),
            P(),
            P(),
            P(),
            P(None, "tp"),
            P(None, "tp"),
            P(None, "tp"),
            P("tp", None),
            P(),
            P(None, "tp"),
            P(None, "tp"),
            P("tp", None),
            P("blk", None, None),
        ),
        out_specs=(
            P("blk", None, None),
            P("blk", None, None),
            P("blk"),
            P("blk", "tp"),
            P("blk", "tp"),
            P("blk", "tp"),
            P("tp", "blk"),
            P("blk"),
            P("blk", "tp"),
            P("blk", "tp"),
            P("tp", "blk"),
        ),
        check_vma=False,
    )
```

```python
import functools
import math

import jax
import jax.numpy as jnp
from jax import lax
from jax.experimental import pallas as pl
from jax.experimental.pallas import tpu as pltpu
from jax.sharding import PartitionSpec as P

HEAD_DIM = 128
EPS = 1e-05
THETA = 10000.0
NEG = -1e30
F32 = jnp.float32
BF16 = jnp.bfloat16
MIB = 1024 * 1024


def dot(left, right):
    return lax.dot_general(left, right, (((1,), (0,)), ((), ())), preferred_element_type=F32)


def dot_rt(left, right):
    return lax.dot_general(left, right, (((1,), (1,)), ((), ())), preferred_element_type=F32)


def dot_lt(left, right):
    return lax.dot_general(left, right, (((0,), (0,)), ((), ())), preferred_element_type=F32)


def params(limit):
    return pltpu.CompilerParams(vmem_limit_bytes=limit * MIB)


def cost():
    return pl.CostEstimate(flops=5 * 10**9, bytes_accessed=10**6, transcendentals=0)


SMEM = pl.BlockSpec(memory_space=pltpu.SMEM)
VMEM = pl.BlockSpec(memory_space=pltpu.VMEM)


def project_kernel(heads, kv, x_ref, gain_ref, cos_ref, sin_ref, wq_ref, wk_ref, wv_ref, msg_ref, norm_ref):
    group = heads // kv
    seqs, loc, width = x_ref.shape
    gain = gain_ref[...].astype(F32)
    for s in range(seqs):
        x = x_ref[s].astype(F32)
        inv = lax.rsqrt(jnp.mean(x * x, axis=-1, keepdims=True) + EPS)
        norm_ref[s] = (x * inv * gain).astype(BF16)
    normed = norm_ref[...].reshape(seqs * loc, width)
    cosine, sine = cos_ref[...], sin_ref[...]

    def rot(t):
        return (t * cosine + pltpu.roll(t, HEAD_DIM // 2, 1) * sine).astype(BF16)

    def put(res, h, s, n, slot, turn):
        part = res[s * loc:(s + 1) * loc, h * HEAD_DIM:(h + 1) * HEAD_DIM]
        msg_ref[s * kv + n, :, slot * HEAD_DIM:(slot + 1) * HEAD_DIM] = rot(part) if turn else part.astype(BF16)

    query = dot(normed, wq_ref[...])
    for s in range(seqs):
        for h in range(heads):
            put(query, h, s, h // group, h % group, True)
    keys = dot(normed, wk_ref[...])
    for s in range(seqs):
        for n in range(kv):
            put(keys, n, s, n, group, True)
    vals = dot(normed, wv_ref[...])
    for s in range(seqs):
        for n in range(kv):
            put(vals, n, s, n, group + 1, False)


def project(x, gain, cosine, sine, wq, wk, wv):
    seqs, loc, width = x.shape
    heads, kv = wq.shape[1] // HEAD_DIM, wk.shape[1] // HEAD_DIM
    cols = (heads // kv + 2) * HEAD_DIM
    return pl.pallas_call(
        functools.partial(project_kernel, heads, kv),
        out_shape=(jax.ShapeDtypeStruct((seqs * kv, loc, cols), BF16), jax.ShapeDtypeStruct(x.shape, BF16)),
        in_specs=[VMEM] * 7,
        out_specs=(VMEM, VMEM),
        compiler_params=params(32),
        cost_estimate=cost(),
    )(x, gain, cosine, sine, wq, wk, wv)


def attend_kernel(group, at_ref, rec_ref, out_ref, full_ref, lse_ref, keys, vals):
    blocks, loc, _ = rec_ref.shape
    base = group * HEAD_DIM
    for p in range(blocks):
        i = at_ref[p]
        keys[p * loc:(p + 1) * loc, :] = rec_ref[i, :, base:base + HEAD_DIM]
        vals[p * loc:(p + 1) * loc, :] = rec_ref[i, :, base + HEAD_DIM:base + 2 * HEAD_DIM]
    rows = lax.broadcasted_iota(jnp.int32, (group * loc, loc), 0) % loc
    cols = lax.broadcasted_iota(jnp.int32, (group * loc, loc), 1)
    keep = cols <= rows
    for p in range(blocks):
        i = at_ref[p]
        count = (p + 1) * loc
        query = jnp.concatenate([rec_ref[i, :, g * HEAD_DIM:(g + 1) * HEAD_DIM] for g in range(group)], axis=0)
        scores = dot_rt(query, keys[:count, :]) * (HEAD_DIM ** -0.5)
        last = jnp.where(keep, scores[:, count - loc:], NEG)
        scores = jnp.concatenate([scores[:, :count - loc], last], axis=1) if p else last
        top = jnp.max(scores, axis=-1, keepdims=True)
        weights = jnp.exp(scores - top)
        total = jnp.sum(weights, axis=-1, keepdims=True)
        mixed = dot(weights.astype(BF16), vals[:count, :]) / total
        lse_ref[p] = jnp.broadcast_to(top + jnp.log(total), (group * loc, HEAD_DIM))
        full_ref[p] = mixed
        for g in range(group):
            out_ref[i, :, g * HEAD_DIM:(g + 1) * HEAD_DIM] = mixed[g * loc:(g + 1) * loc].astype(BF16)


def attend(at, rec, group):
    blocks, loc, _ = rec.shape
    total = blocks * loc
    return pl.pallas_call(
        functools.partial(attend_kernel, group),
        out_shape=(
            jax.ShapeDtypeStruct((blocks, loc, group * HEAD_DIM), BF16),
            jax.ShapeDtypeStruct((blocks, group * loc, HEAD_DIM), F32),
            jax.ShapeDtypeStruct((blocks, group * loc, HEAD_DIM), F32),
        ),
        in_specs=[SMEM, VMEM],
        out_specs=(VMEM,) * 3,
        scratch_shapes=[pltpu.VMEM((total, HEAD_DIM), BF16)] * 2,
        compiler_params=params(32),
        cost_estimate=cost(),
    )(at, rec)


def attend_back_kernel(group, at_ref, rec_ref, grad_ref, full_ref, lse_ref, cos_ref, sin_ref, out_ref, keys, vals, d_keys, d_vals):
    blocks, loc, _ = rec_ref.shape
    base = group * HEAD_DIM
    scale = HEAD_DIM ** -0.5
    for p in range(blocks):
        i = at_ref[p]
        keys[p * loc:(p + 1) * loc, :] = rec_ref[i, :, base:base + HEAD_DIM]
        vals[p * loc:(p + 1) * loc, :] = rec_ref[i, :, base + HEAD_DIM:base + 2 * HEAD_DIM]
    rows = lax.broadcasted_iota(jnp.int32, (group * loc, loc), 0) % loc
    cols = lax.broadcasted_iota(jnp.int32, (group * loc, loc), 1)
    keep = cols <= rows

    def unrot(t, cosine, sine):
        return (t * cosine - pltpu.roll(t, HEAD_DIM // 2, 1) * sine).astype(BF16)

    for p in reversed(range(blocks)):
        i = at_ref[p]
        count = (p + 1) * loc
        span = slice(p * loc, count)
        query = jnp.concatenate([rec_ref[i, :, g * HEAD_DIM:(g + 1) * HEAD_DIM] for g in range(group)], axis=0)
        grad = jnp.concatenate([grad_ref[i, :, g * HEAD_DIM:(g + 1) * HEAD_DIM] for g in range(group)], axis=0)
        lse = lse_ref[p][:, :1]
        delta = jnp.sum(grad.astype(F32) * full_ref[p], axis=-1, keepdims=True)
        probs = jnp.exp(dot_rt(query, keys[:count, :]) * scale - lse)
        last = jnp.where(keep, probs[:, count - loc:], 0.0)
        probs = jnp.concatenate([probs[:, :count - loc], last], axis=1) if p else last
        d_probs = dot_rt(grad, vals[:count, :])
        g_scores = (probs * (d_probs - delta) * scale).astype(BF16)
        d_query = dot(g_scores, keys[:count, :])
        dk = dot_lt(g_scores, query)
        dv = dot_lt(probs.astype(BF16), grad)
        if p == blocks - 1:
            d_keys[...] = dk
            d_vals[...] = dv
        else:
            d_keys[:count, :] += dk
            d_vals[:count, :] += dv
        cosine, sine = cos_ref[span, :], sin_ref[span, :]
        for g in range(group):
            out_ref[i, :, g * HEAD_DIM:(g + 1) * HEAD_DIM] = unrot(d_query[g * loc:(g + 1) * loc], cosine, sine)
        out_ref[i, :, base:base + HEAD_DIM] = unrot(d_keys[span, :], cosine, sine)
        out_ref[i, :, base + HEAD_DIM:base + 2 * HEAD_DIM] = d_vals[span, :].astype(BF16)


def attend_back(at, rec, grad, full, lse, cosine, sine, group):
    blocks, loc, cols = rec.shape
    total = blocks * loc
    return pl.pallas_call(
        functools.partial(attend_back_kernel, group),
        out_shape=jax.ShapeDtypeStruct((blocks, loc, cols), BF16),
        in_specs=[SMEM] + [VMEM] * 6,
        out_specs=VMEM,
        scratch_shapes=[pltpu.VMEM((total, HEAD_DIM), BF16)] * 2 + [pltpu.VMEM((total, HEAD_DIM), F32)] * 2,
        compiler_params=params(60),
        cost_estimate=cost(),
    )(at, rec, grad, full, lse, cosine, sine)


def out_kernel(kv, mix_ref, w_ref, cat_ref, *outs):
    cols = mix_ref.shape[2]
    for s, out in enumerate(outs):
        cat_ref[s] = jnp.concatenate([mix_ref[s * kv + n] for n in range(kv)], axis=1)
        out[...] = dot(cat_ref[s], w_ref[...]).astype(BF16)


def out_project(mixed, w_out, seqs):
    units, loc, cols = mixed.shape
    kv = units // seqs
    width = w_out.shape[1]
    res = pl.pallas_call(
        functools.partial(out_kernel, kv),
        out_shape=(jax.ShapeDtypeStruct((seqs, loc, kv * cols), BF16),)
        + (jax.ShapeDtypeStruct((loc, width), BF16),) * seqs,
        in_specs=[VMEM] * 2,
        out_specs=(VMEM,) * (seqs + 1),
        compiler_params=params(24),
        cost_estimate=cost(),
    )(mixed, w_out)
    return res[0], res[1:]


def input_grads_kernel(seqs, kv, back_ref, x_ref, wq_ref, wk_ref, wv_ref, *refs):
    gain_refs, outs, (rows_ref, inv_ref, attn_ref) = refs[:seqs], refs[seqs:2 * seqs], refs[2 * seqs:]
    loc, width = x_ref.shape[1], x_ref.shape[2]
    group = wq_ref.shape[1] // (kv * HEAD_DIM)
    gather(back_ref, rows_ref, seqs, kv, group)
    at_k = kv * group * HEAD_DIM
    at_v = at_k + kv * HEAD_DIM
    for s in range(seqs):
        x = x_ref[s].astype(F32)
        inv = lax.rsqrt(jnp.mean(x * x, axis=-1, keepdims=True) + EPS)
        inv_ref[s * loc:(s + 1) * loc, :] = jnp.broadcast_to(inv, (loc, HEAD_DIM))
    tile = 512
    for t in range(width // tile):
        span = slice(t * tile, (t + 1) * tile)
        grad = dot_rt(rows_ref[:, :at_k], wq_ref[span, :])
        grad += dot_rt(rows_ref[:, at_k:at_v], wk_ref[span, :])
        grad += dot_rt(rows_ref[:, at_v:], wv_ref[span, :])
        total = 0.0
        for s in range(seqs):
            part = grad[s * loc:(s + 1) * loc]
            outs[s][:loc, span] = part.astype(BF16)
            unit = x_ref[s, :, span].astype(F32) * inv_ref[s * loc:(s + 1) * loc, :1]
            total = total + jnp.sum(part * unit, axis=0, keepdims=True)
        attn_ref[:, span] = total
    mlp = sum(ref[...] for ref in gain_refs)
    lines = []
    for gain in (attn_ref[...], mlp):
        high = gain.astype(BF16).astype(F32)
        lines += [high, gain - high]
    row = lax.broadcasted_iota(jnp.int32, (16, width), 0)
    extra = jnp.zeros((16, width), F32)
    for i, gain in enumerate(lines):
        extra = jnp.where(row == i, gain, extra)
    outs[0][loc:, :] = extra.astype(BF16)


def gather(back_ref, rows_ref, seqs, kv, group):
    loc = back_ref.shape[1]
    wide = group * HEAD_DIM
    for s in range(seqs):
        for n in range(kv):
            span = slice(s * loc, (s + 1) * loc)
            rows_ref[span, n * wide:(n + 1) * wide] = back_ref[s * kv + n, :, :wide]
            for i in range(2):
                at = kv * wide + (i * kv + n) * HEAD_DIM
                rows_ref[span, at:at + HEAD_DIM] = back_ref[s * kv + n, :, wide + i * HEAD_DIM:wide + (i + 1) * HEAD_DIM]


def input_grads(back, x, wq, wk, wv, gains):
    seqs, loc, width = x.shape
    kv = wk.shape[1] // HEAD_DIM
    cols = wq.shape[1] + 2 * wk.shape[1]
    return pl.pallas_call(
        functools.partial(input_grads_kernel, seqs, kv),
        out_shape=(jax.ShapeDtypeStruct((loc + 16, width), BF16),) + (jax.ShapeDtypeStruct((loc, width), BF16),) * (seqs - 1),
        in_specs=[VMEM] * (5 + seqs),
        out_specs=(VMEM,) * seqs,
        scratch_shapes=[
            pltpu.VMEM((seqs * loc, cols), BF16),
            pltpu.VMEM((seqs * loc, HEAD_DIM), F32),
            pltpu.VMEM((1, width), F32),
        ],
        compiler_params=params(60),
        cost_estimate=cost(),
    )(back, x, wq, wk, wv, *gains)


def shares_call(body, fixed, tall, cols, scratch, core, shares):
    width = tall[0].shape[-1]
    tile = width // shares

    def mine(step, keep, core_ref):
        return 2 * step + jnp.where(keep == 0, 1 - core_ref[0], core_ref[0])

    def tall_spec(a):
        lead = (0,) * (a.ndim - 1)
        return pl.BlockSpec(a.shape[:-1] + (tile,), lambda i, k, c: lead + (mine(i, k, c),))

    out = pl.BlockSpec((1, tile, cols), lambda i, k, c: (i, 0, 0))
    return pl.pallas_call(
        body,
        grid_spec=pltpu.PrefetchScalarGridSpec(
            num_scalar_prefetch=1,
            grid=(shares // 2, 2),
            in_specs=[pl.BlockSpec(a.shape, lambda i, k, c, n=a.ndim: (0,) * n) for a in fixed] + [tall_spec(a) for a in tall],
            out_specs=(out, out),
            scratch_shapes=scratch,
        ),
        out_shape=(jax.ShapeDtypeStruct((shares // 2, tile, cols), BF16),) * 2,
        compiler_params=params(48),
        cost_estimate=cost(),
    )(core, *fixed, *tall)


def put_share(send_ref, keep_ref, pieces):
    def store(ref):
        at = 0
        for piece in pieces:
            ref[0, :, at:at + piece.shape[1]] = piece.astype(BF16)
            at += piece.shape[1]

    @pl.when(pl.program_id(1) == 0)
    def _():
        store(send_ref)

    @pl.when(pl.program_id(1) == 1)
    def _():
        store(keep_ref)


def attn_grads_kernel(seqs, kv, group, core_ref, back_ref, mix_ref, norm_ref, *refs):
    grad_refs, (send_ref, keep_ref, rows_ref) = refs[:seqs], refs[seqs:]

    @pl.when((pl.program_id(0) == 0) & (pl.program_id(1) == 0))
    def _():
        gather(back_ref, rows_ref, seqs, kv, group)

    rows = rows_ref.shape[0]
    left = norm_ref[...].reshape(rows, norm_ref.shape[2])
    grad = jnp.concatenate([ref[...] for ref in grad_refs], axis=0)
    mixed = mix_ref[...].reshape(rows, mix_ref.shape[2])
    put_share(send_ref, keep_ref, [dot_lt(left, rows_ref[...]), dot_lt(grad, mixed)])


def attn_grads(core, back, mixed, normed, g_attns, kv, shares):
    seqs, loc, width = normed.shape
    group = back.shape[2] // HEAD_DIM - 2
    cols = kv * back.shape[2]
    scratch = [pltpu.VMEM((seqs * loc, cols), BF16)]
    body = functools.partial(attn_grads_kernel, seqs, kv, group)
    return shares_call(body, (back, mixed), (normed,) + tuple(g_attns), cols + mixed.shape[2], scratch, core, shares)


def ffn_grads_kernel(seqs, core_ref, *refs):
    fixed, refs = refs[:3 * seqs], refs[3 * seqs:]
    down_ref, norm_refs, (send_ref, keep_ref), scratch = refs[0], refs[1:seqs + 1], refs[seqs + 1:seqs + 3], refs[seqs + 3:]

    @pl.when((pl.program_id(0) == 0) & (pl.program_id(1) == 0))
    def _():
        loc = fixed[0].shape[0]
        for i, whole in enumerate(scratch):
            for s in range(seqs):
                whole[s * loc:(s + 1) * loc, :] = fixed[i * seqs + s][...]

    gate_ref, up_ref, hid_ref = scratch
    norm = jnp.concatenate([ref[...] for ref in norm_refs], axis=0)
    put_share(
        send_ref,
        keep_ref,
        [dot_lt(norm, gate_ref[...]), dot_lt(norm, up_ref[...]), dot_lt(down_ref[...], hid_ref[...])],
    )


def ffn_grads(core, gates, ups, hiddens, g_down, norms, shares):
    loc, units = gates[0].shape
    scratch = [pltpu.VMEM((len(gates) * loc, units), BF16)] * 3
    body = functools.partial(ffn_grads_kernel, len(gates))
    fixed = tuple(gates) + tuple(ups) + tuple(hiddens)
    return shares_call(body, fixed, (g_down,) + tuple(norms), 3 * units, scratch, core, shares)


def fold_two_kernel(place_ref, *refs):
    keeps, gots, outs = refs[:4], refs[4:8], refs[8:]
    for keep, got, out in zip(keeps, gots, outs):
        out[0] = (keep[0, 0].astype(F32) + got[0, 0].astype(F32)).astype(BF16)


def fold_two(place, keep, got):
    _, rows, cols = keep.shape
    half = rows // 2
    keep, got = keep.reshape(2, 2, rows, cols), got.reshape(2, 2, rows, cols)
    tile = half // 2
    ins = []
    for own in (0, 1):
        ins.append(pl.BlockSpec((1, 1, tile, cols), lambda i, j, p, own=own: (i, jnp.where(own == 1, p[0], 1 - p[0]), j, 0)))
    for own in (0, 1):
        ins.append(pl.BlockSpec((1, 1, tile, cols), lambda i, j, p, own=own: (jnp.where(own == 1, p[1], 1 - p[1]), i, j + 2, 0)))
    return pl.pallas_call(
        fold_two_kernel,
        grid_spec=pltpu.PrefetchScalarGridSpec(
            num_scalar_prefetch=1,
            grid=(2, 2),
            in_specs=ins + ins,
            out_specs=(pl.BlockSpec((1, tile, cols), lambda i, j, p: (i, j, 0)),) * 4,
        ),
        out_shape=(jax.ShapeDtypeStruct((2, half, cols), BF16),) * 4,
        compiler_params=params(40),
        cost_estimate=cost(),
    )(place, keep, keep, keep, keep, got, got, got, got)


def fold_three(place, upper, upper_got, lower, lower_got):
    _, half, cols = upper.shape
    tile = half // 2
    ins = []
    for axis in (1, 0):
        for own in (0, 1):
            ins.append(pl.BlockSpec((1, 1, tile, cols), lambda j, p, own=own, axis=axis: (0, jnp.where(own == 1, p[axis], 1 - p[axis]), j, 0)))
    flat = pl.BlockSpec((1, tile, cols), lambda j, p: (0, j, 0))
    u, ug, l, lg = (a[None] for a in (upper, upper_got, lower, lower_got))
    res = pl.pallas_call(
        fold_two_kernel,
        grid_spec=pltpu.PrefetchScalarGridSpec(
            num_scalar_prefetch=1, grid=(2,), in_specs=ins + ins, out_specs=(flat,) * 4
        ),
        out_shape=(jax.ShapeDtypeStruct((1, half, cols), BF16),) * 4,
        compiler_params=params(40),
        cost_estimate=cost(),
    )(place, u, u, l, l, ug, ug, lg, lg)
    return [a[0] for a in res]


def fold_four_kernel(widths, upper, upper_got, lower, lower_got, *outs):
    half = upper.shape[0]
    for at, (one, two) in enumerate(((upper, upper_got), (lower, lower_got))):
        start = 0
        for out, width in zip(outs, widths):
            part = one[:, start:start + width].astype(F32) + two[:, start:start + width].astype(F32)
            if out is outs[-1]:
                out[:, at * half:(at + 1) * half] = part.T
            else:
                out[at * half:(at + 1) * half, :] = part
            start += width


def fold_four(widths, upper, upper_got, lower, lower_got):
    rows = 2 * upper.shape[0]
    shapes = [(rows, w) for w in widths[:-1]] + [(widths[-1], rows)]
    return pl.pallas_call(
        functools.partial(fold_four_kernel, widths),
        out_shape=tuple(jax.ShapeDtypeStruct(shape, F32) for shape in shapes),
        in_specs=[VMEM] * 4,
        out_specs=(VMEM,) * len(widths),
        compiler_params=params(40),
        cost_estimate=cost(),
    )(upper, upper_got, lower, lower_got)


def finish_kernel(seqs, mid_ref, x_ref, gain_ref, *refs):
    inner, ends, resids, out_ref = refs[:seqs], refs[seqs:2 * seqs], refs[2 * seqs:3 * seqs], refs[3 * seqs]
    gain = gain_ref[...].astype(F32)
    for s in range(seqs):
        grad = jnp.where(mid_ref[0] == 1, inner[s][...].astype(F32), ends[s][...].astype(F32))
        x = x_ref[s].astype(F32)
        inv = lax.rsqrt(jnp.mean(x * x, axis=-1, keepdims=True) + EPS)
        unit = x * inv
        scaled = grad * gain
        back = inv * (scaled - unit * jnp.mean(scaled * unit, axis=-1, keepdims=True))
        out_ref[:, s, :] = resids[s][...] + back


def finish(mid, x, gain, inner, ends, resids):
    seqs, loc, width = x.shape
    tile = 32
    flat = pl.BlockSpec((tile, width), lambda i: (i, 0))
    return pl.pallas_call(
        functools.partial(finish_kernel, seqs),
        grid=(loc // tile,),
        out_shape=jax.ShapeDtypeStruct((loc, seqs, width), F32),
        in_specs=[SMEM, pl.BlockSpec((seqs, tile, width), lambda i: (0, i, 0)), pl.BlockSpec((1, width), lambda i: (0, 0))]
        + [flat] * (3 * seqs),
        out_specs=pl.BlockSpec((tile, seqs, width), lambda i: (i, 0, 0)),
        compiler_params=params(32),
        cost_estimate=cost(),
    )(mid, x, gain, *inner, *ends, *resids)


def output_kernel(seqs, mid_ref, x_ref, *refs):
    attn, inner, ends, out_ref, wide = refs[:seqs], refs[seqs:2 * seqs], refs[2 * seqs:3 * seqs], refs[3 * seqs], refs[3 * seqs + 1]
    for s in range(seqs):
        down = jnp.where(mid_ref[0] == 1, inner[s][...].astype(F32), ends[s][...].astype(F32))
        wide[:, s, :] = x_ref[s].astype(F32) + attn[s][...].astype(F32) + down
    out_ref[...] = wide[...].astype(BF16)


def block_output(mid, x, attn, inner, ends):
    seqs, loc, width = x.shape
    tile = 32
    flat = pl.BlockSpec((tile, width), lambda i: (i, 0))
    parts = []
    for group in (inner, ends):
        per = seqs // len(group)
        for s in range(seqs):
            parts.append((group[s // per], pl.BlockSpec((tile, width), lambda i, at=(s % per) * (loc // tile): (i + at, 0))))
    return pl.pallas_call(
        functools.partial(output_kernel, seqs),
        grid=(loc // tile,),
        out_shape=jax.ShapeDtypeStruct((loc, seqs, width), BF16),
        in_specs=[SMEM, pl.BlockSpec((seqs, tile, width), lambda i: (0, i, 0))] + [flat] * seqs + [spec for _, spec in parts],
        out_specs=pl.BlockSpec((tile, seqs, width), lambda i: (i, 0, 0)),
        scratch_shapes=[pltpu.VMEM((tile, seqs, width), F32)],
        compiler_params=params(32),
        cost_estimate=cost(),
    )(mid, x, *attn, *(a for a, _ in parts))


def add_kernel(left, right, out):
    out[...] = (left[...].astype(F32) + right[...].astype(F32)).astype(BF16)


def add(left, right):
    return pl.pallas_call(
        add_kernel,
        out_shape=jax.ShapeDtypeStruct(left.shape, BF16),
        in_specs=[VMEM, VMEM],
        out_specs=VMEM,
        compiler_params=params(16),
        cost_estimate=cost(),
    )(left, right)


def rope_tables(positions, head_dim):
    half = head_dim // 2
    freq = jnp.exp(jnp.arange(half, dtype=jnp.float32) * (-2.0 * math.log(THETA) / head_dim))
    angles = positions.astype(jnp.float32)[:, None] * freq[None, :]
    return (jnp.cos(angles), jnp.sin(angles))


def rotate(values, cosine, sine):
    half = values.shape[-1] // 2
    first = values[..., :half]
    second = values[..., half:]
    cosine = cosine[:, None, None, :]
    sine = sine[:, None, None, :]
    return jnp.concatenate(
        [first * cosine - second * sine, second * cosine + first * sine], axis=-1
    )


def inverse_rms(values):
    return lax.rsqrt(jnp.mean(values * values, axis=-1, keepdims=True) + EPS)


def norm_back(values, inverse, gain, grad):
    unit = values * inverse
    scaled = grad * gain
    back = inverse * (scaled - unit * jnp.mean(scaled * unit, axis=-1, keepdims=True))
    return (back, jnp.sum(grad * unit, axis=(0, 1)))


def matmul(values, weight):
    return jnp.einsum("lsd,de->lse", values, weight, preferred_element_type=jnp.float32)


def matmul_back(values, weight):
    return jnp.einsum("lse,de->lsd", values, weight, preferred_element_type=jnp.float32)


def weight_grad(left, right):
    return jnp.einsum("lsd,lse->de", left, right, preferred_element_type=jnp.float32)


def general(
    hidden_in,
    block_order,
    seq_labels,
    exit_scales,
    attn_gain,
    w_query,
    w_key,
    w_value,
    w_out,
    mlp_gain,
    w_gate,
    w_up,
    w_down,
    d_out,
):
    f32 = jnp.float32
    bf16 = jnp.bfloat16
    loc, seqs, width = hidden_in.shape
    head_dim = HEAD_DIM
    q_heads = w_query.shape[1] // head_dim
    kv_heads = w_key.shape[1] // head_dim
    group = q_heads // kv_heads
    scale = head_dim ** (-0.5)
    blocks_all = block_order.shape[0]
    total_rows = loc * lax.axis_size("blk")
    key_rows = math.gcd(512, total_rows)
    block_count = total_rows // key_rows
    kv_width = 2 * kv_heads * head_dim
    positions = block_order[lax.axis_index("blk")] * loc + jnp.arange(loc, dtype=jnp.int32)
    cosine, sine = rope_tables(positions, head_dim)

    def key_positions(start, count):
        index = start + jnp.arange(count, dtype=jnp.int32)
        owner = index // loc
        table = jnp.sum(
            jnp.where(
                owner[:, None] == jnp.arange(blocks_all, dtype=jnp.int32)[None, :],
                block_order[None, :],
                0,
            ),
            axis=1,
        )
        return table * loc + index % loc

    xin = hidden_in.astype(f32)
    inv_a = inverse_rms(xin)
    gain_a = attn_gain.astype(f32)
    normed = (xin * inv_a * gain_a).astype(bf16)
    query_bf = rotate(
        matmul(normed, w_query).reshape(loc, seqs, q_heads, head_dim), cosine, sine
    ).astype(bf16)
    keys_bf = (
        rotate(matmul(normed, w_key).reshape(loc, seqs, kv_heads, head_dim), cosine, sine)
        .astype(bf16)
        .reshape(loc, seqs, kv_heads * head_dim)
    )
    vals_bf = matmul(normed, w_value).astype(bf16)
    query_g = query_bf.reshape(loc, seqs, kv_heads, group, head_dim)
    starts = jnp.arange(block_count, dtype=jnp.int32) * key_rows
    top = jnp.full((seqs, kv_heads, group, loc), NEG, f32)
    key_part = lax.all_gather(keys_bf, "blk", axis=0, tiled=True)
    val_part = lax.all_gather(vals_bf, "blk", axis=0, tiled=True)
    count = key_part.shape[0]
    kk = key_part.reshape(count, seqs, kv_heads, head_dim)
    vv = val_part.reshape(count, seqs, kv_heads, head_dim)
    mask = key_positions(jnp.int32(0), count)[None, :] <= positions[:, None]
    raw = jnp.einsum("lsngd,msnd->snglm", query_g, kk, preferred_element_type=f32)
    scores = jnp.where(mask, raw * scale, NEG)
    new_top = jnp.maximum(top, jnp.max(scores, axis=-1))
    weights = jnp.where(mask, jnp.exp(scores - new_top[..., None]), 0.0)
    total = jnp.sum(weights, axis=-1)
    acc = jnp.einsum("snglm,msnd->sngld", weights.astype(bf16), vv, preferred_element_type=f32)
    top, total, acc = (new_top, total, acc)
    lse = top + jnp.log(total)
    mixed_raw = acc / total[..., None]
    mixed_bf = (
        mixed_raw.transpose(3, 0, 1, 2, 4).reshape(loc, seqs, q_heads * head_dim).astype(bf16)
    )
    resid = xin + lax.psum(matmul(mixed_bf, w_out).astype(jnp.bfloat16), "tp").astype(jnp.float32)
    inv_m = inverse_rms(resid)
    gain_m = mlp_gain.astype(f32)
    normed_m = (resid * inv_m * gain_m).astype(bf16)
    gate = matmul(normed_m, w_gate)
    up = matmul(normed_m, w_up)
    sig = jax.nn.sigmoid(gate)
    silu = gate * sig
    hidden = (silu * up).astype(bf16)
    output = resid + lax.psum(matmul(hidden, w_down).astype(jnp.bfloat16), "tp").astype(jnp.float32)
    block_out = output.astype(bf16)
    scale_rows = jnp.where(seq_labels == 1, exit_scales[1], exit_scales[0])
    cot = d_out.astype(f32) * scale_rows[None, :, None]
    g_down = cot.astype(bf16)
    d_w_down = weight_grad(hidden, g_down)
    d_hidden = matmul_back(g_down, w_down)
    g_up = (d_hidden * silu).astype(bf16)
    g_gate = (d_hidden * up * (sig * (1.0 + gate * (1.0 - sig)))).astype(bf16)
    d_w_gate = weight_grad(normed_m, g_gate)
    d_w_up = weight_grad(normed_m, g_up)
    d_nm = lax.psum(
        (matmul_back(g_gate, w_gate) + matmul_back(g_up, w_up)).astype(jnp.bfloat16), "tp"
    ).astype(jnp.float32)
    d_resid_norm, d_mlp_gain = norm_back(resid, inv_m, gain_m, d_nm)
    d_resid = cot + d_resid_norm
    g_attn = d_resid.astype(bf16)
    d_w_out = weight_grad(mixed_bf, g_attn)
    g_mixed = matmul_back(g_attn, w_out).astype(bf16)
    g_mixed_g = g_mixed.reshape(loc, seqs, kv_heads, group, head_dim)
    delta = jnp.sum(g_mixed_g.astype(f32).transpose(1, 2, 3, 0, 4) * mixed_raw, axis=-1)
    whole_keys, whole_vals = (
        lax.all_gather(keys_bf, "blk", axis=0, tiled=True),
        lax.all_gather(vals_bf, "blk", axis=0, tiled=True),
    )

    def probe(kk, vv, start, count):
        mask = key_positions(start, count)[None, :] <= positions[:, None]
        raw = jnp.einsum("lsngd,msnd->snglm", query_g, kk, preferred_element_type=f32)
        probs = jnp.where(mask, jnp.exp(raw * scale - lse[..., None]), 0.0)
        d_probs = jnp.einsum("lsngd,msnd->snglm", g_mixed_g, vv, preferred_element_type=f32)
        g_scores = (probs * (d_probs - delta[..., None]) * scale).astype(bf16)
        return (g_scores, probs)

    def kv_pair(g_scores, probs, count):
        d_keys = jnp.einsum("snglm,lsngd->msnd", g_scores, query_g, preferred_element_type=f32)
        d_vals = jnp.einsum(
            "snglm,lsngd->msnd", probs.astype(bf16), g_mixed_g, preferred_element_type=f32
        )
        return jnp.concatenate([d_keys, d_vals], axis=2).reshape(count, seqs, kv_width)

    scan_items = (
        whole_keys.reshape(block_count, key_rows, seqs, -1),
        whole_vals.reshape(block_count, key_rows, seqs, -1),
        starts,
    )
    zero_query = jnp.zeros((loc, seqs, kv_heads, group, head_dim), f32)

    def back_step(d_query, item):
        key_part, val_part, start = item
        kk = key_part.reshape(key_rows, seqs, kv_heads, head_dim)
        vv = val_part.reshape(key_rows, seqs, kv_heads, head_dim)
        g_scores, probs = probe(kk, vv, start, key_rows)
        d_query = d_query + jnp.einsum(
            "snglm,msnd->lsngd", g_scores, kk, preferred_element_type=f32
        )
        return (d_query, kv_pair(g_scores, probs, key_rows))

    d_query, kv_terms = lax.scan(back_step, zero_query, scan_items)
    kv_local = lax.psum_scatter(
        kv_terms.reshape(total_rows, seqs, kv_width).astype(jnp.bfloat16),
        "blk",
        scatter_dimension=0,
        tiled=True,
    ).astype(jnp.float32)
    kv_local = kv_local.reshape(loc, seqs, 2, kv_heads, head_dim)
    g_q = (
        rotate(d_query.reshape(loc, seqs, q_heads, head_dim), cosine, -sine)
        .astype(bf16)
        .reshape(loc, seqs, q_heads * head_dim)
    )
    g_k = (
        rotate(kv_local[:, :, 0], cosine, -sine)
        .astype(bf16)
        .reshape(loc, seqs, kv_heads * head_dim)
    )
    g_v = kv_local[:, :, 1].astype(bf16).reshape(loc, seqs, kv_heads * head_dim)
    d_w_query = weight_grad(normed, g_q)
    d_w_key = weight_grad(normed, g_k)
    d_w_value = weight_grad(normed, g_v)
    d_n = lax.psum(
        (matmul_back(g_q, w_query) + matmul_back(g_k, w_key) + matmul_back(g_v, w_value)).astype(
            jnp.bfloat16
        ),
        "tp",
    ).astype(jnp.float32)
    d_in_norm, d_attn_gain = norm_back(xin, inv_a, gain_a, d_n)
    d_hidden_in = d_resid + d_in_norm
    d_attn_gain, d_w_query, d_w_key, d_w_value, d_w_out, d_mlp_gain, d_w_gate, d_w_up, d_w_down = (
        lax.psum_scatter(
            d_attn_gain.astype(jnp.bfloat16), "blk", scatter_dimension=0, tiled=True
        ).astype(jnp.float32),
        lax.psum_scatter(
            d_w_query.astype(jnp.bfloat16), "blk", scatter_dimension=0, tiled=True
        ).astype(jnp.float32),
        lax.psum_scatter(
            d_w_key.astype(jnp.bfloat16), "blk", scatter_dimension=0, tiled=True
        ).astype(jnp.float32),
        lax.psum_scatter(
            d_w_value.astype(jnp.bfloat16), "blk", scatter_dimension=0, tiled=True
        ).astype(jnp.float32),
        lax.psum_scatter(
            d_w_out.astype(jnp.bfloat16), "blk", scatter_dimension=1, tiled=True
        ).astype(jnp.float32),
        lax.psum_scatter(
            d_mlp_gain.astype(jnp.bfloat16), "blk", scatter_dimension=0, tiled=True
        ).astype(jnp.float32),
        lax.psum_scatter(
            d_w_gate.astype(jnp.bfloat16), "blk", scatter_dimension=0, tiled=True
        ).astype(jnp.float32),
        lax.psum_scatter(
            d_w_up.astype(jnp.bfloat16), "blk", scatter_dimension=0, tiled=True
        ).astype(jnp.float32),
        lax.psum_scatter(
            d_w_down.astype(jnp.bfloat16), "blk", scatter_dimension=1, tiled=True
        ).astype(jnp.float32),
    )
    return (
        block_out,
        d_hidden_in,
        d_attn_gain,
        d_w_query,
        d_w_key,
        d_w_value,
        d_w_out,
        d_mlp_gain,
        d_w_gate,
        d_w_up,
        d_w_down,
    )


class Steps:
    def __init__(self):
        self.last = None

    def enter(self, *values):
        if self.last is not None:
            values, _ = lax.optimization_barrier((values, self.last))
        return values if len(values) > 1 else values[0]

    def leave(self, value):
        self.last = value
        return value


class Line:
    def __init__(self, steps, middle, parts):
        self.steps, self.middle, self.parts = steps, middle, list(parts)
        count = len(self.parts)
        self.first, self.half, self.second, self.total, self.third, self.done = ([None] * count for _ in range(6))

    def one(self, c):
        self.first[c] = lax.ppermute(self.parts[c], "tp", [(0, 1), (3, 2)])

    def two(self, c):
        part, got = self.steps.enter(self.parts[c], self.first[c])
        self.half[c] = self.steps.leave(add(part, got))
        self.second[c] = lax.ppermute(self.half[c], "tp", [(1, 2), (2, 1)])

    def three(self, c):
        half, got = self.steps.enter(self.half[c], self.second[c])
        self.total[c] = self.steps.leave(add(half, got))
        self.third[c] = lax.ppermute(self.total[c], "tp", [(1, 0), (2, 3)])

    def four(self, c):
        total, got = self.steps.enter(self.total[c], self.third[c])
        self.done[c] = self.steps.leave(jnp.where(self.middle, total, got))

    def five(self, c):
        self.third[c] = self.steps.leave(self.steps.enter(self.third[c]))


def partner(bit):
    return [(i, i ^ bit) for i in range(8)]


class Scatter:
    def __init__(self, steps, place, send, keep):
        self.steps, self.place, self.keep = steps, place, keep
        self.got = lax.ppermute(send, "blk", partner(1))

    def two(self):
        keep, got = self.steps.enter(self.keep, self.got)
        away, self.upper, off, self.lower = fold_two(self.place, keep, got)
        self.steps.leave(self.upper)
        self.upper_got = lax.ppermute(away, "blk", partner(2))
        self.lower_got = lax.ppermute(off, "blk", partner(4))

    def three(self):
        values = self.steps.enter(self.upper, self.upper_got, self.lower, self.lower_got)
        away, self.upper, off, self.lower = fold_three(self.place, *values)
        self.steps.leave(self.upper)
        self.upper_got = lax.ppermute(away, "blk", partner(4))
        self.lower_got = lax.ppermute(off, "blk", partner(2))

    def four(self, widths):
        values = self.steps.enter(self.upper, self.upper_got, self.lower, self.lower_got)
        res = fold_four(widths, *values)
        self.steps.leave(res[0])
        return res


def inverse(values):
    return lax.rsqrt(jnp.mean(values * values, axis=-1, keepdims=True) + EPS)


def tables(positions):
    cosine, sine = rope_tables(positions, HEAD_DIM)
    return jnp.concatenate([cosine, cosine], axis=1), jnp.concatenate([-sine, sine], axis=1)


def fast(
    hidden_in,
    block_order,
    seq_labels,
    exit_scales,
    attn_gain,
    w_query,
    w_key,
    w_value,
    w_out,
    mlp_gain,
    w_gate,
    w_up,
    w_down,
    d_out,
):
    loc, seqs, width = hidden_in.shape
    blocks = block_order.shape[0]
    rows = seqs * loc
    units = w_gate.shape[1]
    kv = w_key.shape[1] // HEAD_DIM
    group = w_query.shape[1] // w_key.shape[1]
    wide = group * HEAD_DIM
    me = lax.axis_index("blk")
    line = lax.axis_index("tp")
    middle = (line == 1) | (line == 2)
    index = jnp.arange(blocks, dtype=jnp.int32)
    at = jnp.sum(jnp.where(block_order[None, :] == index[:, None], index[None, :], 0), axis=1)
    mine = block_order[me] * loc + jnp.arange(loc, dtype=jnp.int32)
    steps = Steps()
    enter, leave = steps.enter, steps.leave

    x = hidden_in.transpose(1, 0, 2)
    cosine, sine = tables(mine)
    messages, normed = project(x, attn_gain[None, :], cosine, sine, w_query, w_key, w_value)
    leave(messages)
    rec = lax.all_to_all(messages, "blk", 0, 0, tiled=True)
    scales = jnp.where(seq_labels == 1, exit_scales[1], exit_scales[0])
    cot = enter(d_out).transpose(1, 0, 2).astype(F32) * scales[:, None, None]
    g_down = leave(cot.astype(BF16).reshape(rows, width))
    d_hidden = leave(dot_rt(g_down, w_down).astype(BF16))
    mixed, full, lse = attend(at, enter(rec), group)
    leave(mixed)
    mixed = lax.all_to_all(mixed, "blk", 0, 0, tiled=True)
    all_cosine, all_sine = tables(enter(jnp.arange(blocks * loc, dtype=jnp.int32)))
    leave(all_cosine)
    mixed, parts = out_project(enter(mixed), w_out, seqs)
    leave(mixed)

    gain_m = mlp_gain.astype(F32)
    attn = Line(steps, middle, parts)
    back = Line(steps, middle, [None] * seqs)
    norms, hiddens, gates, ups, gains = ([None] * seqs for _ in range(5))

    def feed(s):
        total = attn.done[s]
        resid = x[s].astype(F32) + total.astype(F32)
        unit = resid * inverse(resid)
        norm = (unit * gain_m).astype(BF16)
        gate = dot(norm, w_gate)
        up = dot(norm, w_up)
        sig = jax.nn.sigmoid(gate)
        silu = gate * sig
        grad_h = d_hidden[s * loc:(s + 1) * loc].astype(F32)
        g_up = (grad_h * silu).astype(BF16)
        g_gate = (grad_h * up * (sig * (1.0 + gate * (1.0 - sig)))).astype(BF16)
        grad = dot_rt(g_gate, w_gate) + dot_rt(g_up, w_up)
        gains[s] = jnp.sum(grad * unit, axis=0)
        back.parts[s] = leave(grad.astype(BF16))
        norms[s], gates[s], ups[s] = norm, g_gate, g_up
        hiddens[s] = (silu * up).astype(BF16)

    d_resids, g_attns, sends = ([None] * seqs for _ in range(3))

    def norm_back(s):
        resid = x[s].astype(F32) + attn.done[s].astype(F32)
        inv = inverse(resid)
        unit = resid * inv
        scaled = back.done[s].astype(F32) * gain_m
        d_resids[s] = cot[s] + inv * (scaled - unit * jnp.mean(scaled * unit, axis=-1, keepdims=True))
        g_attns[s] = d_resids[s].astype(BF16)
        sends[s] = leave(dot_rt(g_attns[s], w_out).astype(BF16))

    def run(lines, text):
        for word in text.split():
            name, c = word[:-1], int(word[-1])
            if name == "F":
                feed(c)
            elif name == "N":
                norm_back(c)
            else:
                obj = lines[name[0]]
                (obj.one, obj.two, obj.three, obj.four, obj.five)[int(name[1]) - 1](c)

    lines = {"a": attn, "b": back}
    core = (me % 2).astype(jnp.int32)[None]
    place = jnp.stack([(me // 2) % 2, me // 4]).astype(jnp.int32)
    run(lines, "a10 a11 a12 a13 a20 a21 a30 a22 a31 a40 F0 b10 a23 a32 a41 F1 b11")
    run(lines, "a33 a42 F2 b12 b20 a43 F3 b13 b21 b30")
    hidden = [enter(jnp.concatenate(hiddens[i:i + 2], axis=0)) for i in range(0, seqs, 2)]
    outs = Line(steps, middle, [leave(dot(h, w_down).astype(BF16)) for h in hidden])
    lines["c"] = outs
    run(lines, "c10 c11 b22 b31 b40 N0 b23 b32 b41 N1 b33 c20 b42 N2 b43 N3")
    send = jnp.stack(sends).reshape(seqs, loc, kv, wide).transpose(0, 2, 1, 3).reshape(seqs * kv, loc, wide)
    grad = lax.all_to_all(send, "blk", 0, 0, tiled=True)
    send, keep = ffn_grads(*enter(core, gates, ups, hiddens, g_down, norms), blocks)
    leave(keep)
    ffn_sum = Scatter(steps, place, send, keep)
    grads = leave(attend_back(at, rec, enter(grad), full, lse, all_cosine, all_sine, group))
    grads = lax.all_to_all(grads, "blk", 0, 0, tiled=True)
    run(lines, "c21 c30")

    grads = enter(grads)
    ins = Line(steps, middle, input_grads(grads, x, w_query, w_key, w_value, [g[None, :] for g in gains]))
    leave(ins.parts[0])
    lines["d"] = ins
    run(lines, "d10 d11 d12 d13")
    ffn_sum.two()
    run(lines, "c31 d20 d21 d30 c50")
    send, keep = attn_grads(*enter(core, grads, mixed, normed, g_attns), kv, blocks)
    leave(keep)
    attn_sum = Scatter(steps, place, send, keep)
    run(lines, "d22 d31 c51")
    mid = middle.astype(jnp.int32)[None]
    block_out = leave(block_output(mid, x, attn.done, enter(outs.total), outs.third))
    attn_sum.two()
    run(lines, "d40")
    extra = ins.done[0][loc:loc + 4].astype(F32)
    both = (extra[0::2] + extra[1::2]).reshape(2, 8, width // 8)
    both = leave(both + lax.ppermute(both, "blk", partner(1)))
    others = [lax.ppermute(both, "blk", partner(bit)) for bit in (2, 4, 6)]
    run(lines, "d23 d32 d51")
    ffn_sum.three()
    run(lines, "d33 d52")
    attn_sum.three()
    d_w_gate, d_w_up, d_w_down = ffn_sum.four((units, units, units))
    d_w_query, d_w_key, d_w_value, d_w_out = attn_sum.four((kv * wide, kv * HEAD_DIM, kv * HEAD_DIM, kv * wide))
    others = enter(others)
    both = both + others[0] + others[1] + others[2]
    both = leave(lax.dynamic_index_in_dim(both, me, 1, keepdims=False))
    ends = enter(ins.third[-1])
    d_hidden_in = finish(
        mid,
        x,
        attn_gain[None, :],
        ins.total,
        ins.third[:-1] + [ends],
        d_resids,
    )
    return (
        block_out,
        d_hidden_in,
        both[0],
        d_w_query,
        d_w_key,
        d_w_value,
        d_w_out,
        both[1],
        d_w_gate,
        d_w_up,
        d_w_down,
    )


def per_device(*args):
    seqs = args[0].shape[1]
    kv_heads = args[6].shape[1] // HEAD_DIM
    fits = lax.axis_size("blk") == 8 and lax.axis_size("tp") == 4 and seqs * kv_heads == 8
    return (fast if fits else general)(*args)


def solution(mesh):
    return jax.shard_map(
        per_device,
        mesh=mesh,
        in_specs=(
            P("blk", None, None),
            P(),
            P(),
            P(),
            P(),
            P(None, "tp"),
            P(None, "tp"),
            P(None, "tp"),
            P("tp", None),
            P(),
            P(None, "tp"),
            P(None, "tp"),
            P("tp", None),
            P("blk", None, None),
        ),
        out_specs=(
            P("blk", None, None),
            P("blk", None, None),
            P("blk"),
            P("blk", "tp"),
            P("blk", "tp"),
            P("blk", "tp"),
            P("tp", "blk"),
            P("blk"),
            P("blk", "tp"),
            P("blk", "tp"),
            P("tp", "blk"),
        ),
        check_vma=False,
    )
```

```python
import functools
import math

import jax
import jax.numpy as jnp
from jax import lax
from jax.experimental import pallas as pl
from jax.experimental.pallas import tpu as pltpu
from jax.sharding import PartitionSpec as P

HEAD_DIM = 128
EPS = 1e-05
THETA = 10000.0
NEG = -1e30
F32 = jnp.float32
BF16 = jnp.bfloat16
MIB = 1024 * 1024


def dot(left, right):
    return lax.dot_general(left, right, (((1,), (0,)), ((), ())), preferred_element_type=F32)


def dot_rt(left, right):
    return lax.dot_general(left, right, (((1,), (1,)), ((), ())), preferred_element_type=F32)


def dot_lt(left, right):
    return lax.dot_general(left, right, (((0,), (0,)), ((), ())), preferred_element_type=F32)


def params(limit):
    return pltpu.CompilerParams(vmem_limit_bytes=limit * MIB)


def cost():
    return pl.CostEstimate(flops=10**9, bytes_accessed=10**6, transcendentals=0)


SMEM = pl.BlockSpec(memory_space=pltpu.SMEM)
VMEM = pl.BlockSpec(memory_space=pltpu.VMEM)


def project_kernel(heads, kv, x_ref, gain_ref, cos_ref, sin_ref, wq_ref, wk_ref, wv_ref, msg_ref, norm_ref):
    group = heads // kv
    seqs, loc, width = x_ref.shape
    gain = gain_ref[...].astype(F32)
    for s in range(seqs):
        x = x_ref[s].astype(F32)
        inv = lax.rsqrt(jnp.mean(x * x, axis=-1, keepdims=True) + EPS)
        norm_ref[s] = (x * inv * gain).astype(BF16)
    normed = norm_ref[...].reshape(seqs * loc, width)
    cosine, sine = cos_ref[...], sin_ref[...]

    def rot(t):
        return (t * cosine + pltpu.roll(t, HEAD_DIM // 2, 1) * sine).astype(BF16)

    def put(res, h, s, n, slot, turn):
        part = res[s * loc:(s + 1) * loc, h * HEAD_DIM:(h + 1) * HEAD_DIM]
        msg_ref[s * kv + n, :, slot * HEAD_DIM:(slot + 1) * HEAD_DIM] = rot(part) if turn else part.astype(BF16)

    query = dot(normed, wq_ref[...])
    for s in range(seqs):
        for h in range(heads):
            put(query, h, s, h // group, h % group, True)
    keys = dot(normed, wk_ref[...])
    for s in range(seqs):
        for n in range(kv):
            put(keys, n, s, n, group, True)
    vals = dot(normed, wv_ref[...])
    for s in range(seqs):
        for n in range(kv):
            put(vals, n, s, n, group + 1, False)


def project(x, gain, cosine, sine, wq, wk, wv):
    seqs, loc, width = x.shape
    heads, kv = wq.shape[1] // HEAD_DIM, wk.shape[1] // HEAD_DIM
    cols = (heads // kv + 2) * HEAD_DIM
    return pl.pallas_call(
        functools.partial(project_kernel, heads, kv),
        out_shape=(jax.ShapeDtypeStruct((seqs * kv, loc, cols), BF16), jax.ShapeDtypeStruct(x.shape, BF16)),
        in_specs=[VMEM] * 7,
        out_specs=(VMEM, VMEM),
        compiler_params=params(32),
        cost_estimate=cost(),
    )(x, gain, cosine, sine, wq, wk, wv)


def attend_kernel(group, at_ref, rec_ref, out_ref, full_ref, lse_ref, keys, vals):
    blocks, loc, _ = rec_ref.shape
    base = group * HEAD_DIM
    for p in range(blocks):
        i = at_ref[p]
        keys[p * loc:(p + 1) * loc, :] = rec_ref[i, :, base:base + HEAD_DIM]
        vals[p * loc:(p + 1) * loc, :] = rec_ref[i, :, base + HEAD_DIM:base + 2 * HEAD_DIM]
    rows = lax.broadcasted_iota(jnp.int32, (group * loc, loc), 0) % loc
    cols = lax.broadcasted_iota(jnp.int32, (group * loc, loc), 1)
    keep = cols <= rows
    for p in range(blocks):
        i = at_ref[p]
        count = (p + 1) * loc
        query = jnp.concatenate([rec_ref[i, :, g * HEAD_DIM:(g + 1) * HEAD_DIM] for g in range(group)], axis=0)
        scores = dot_rt(query, keys[:count, :]) * (HEAD_DIM ** -0.5)
        last = jnp.where(keep, scores[:, count - loc:], NEG)
        scores = jnp.concatenate([scores[:, :count - loc], last], axis=1) if p else last
        top = jnp.max(scores, axis=-1, keepdims=True)
        weights = jnp.exp(scores - top)
        total = jnp.sum(weights, axis=-1, keepdims=True)
        mixed = dot(weights.astype(BF16), vals[:count, :]) / total
        lse_ref[p] = jnp.broadcast_to(top + jnp.log(total), (group * loc, HEAD_DIM))
        full_ref[p] = mixed
        for g in range(group):
            out_ref[i, :, g * HEAD_DIM:(g + 1) * HEAD_DIM] = mixed[g * loc:(g + 1) * loc].astype(BF16)


def attend(at, rec, group):
    blocks, loc, _ = rec.shape
    total = blocks * loc
    return pl.pallas_call(
        functools.partial(attend_kernel, group),
        out_shape=(
            jax.ShapeDtypeStruct((blocks, loc, group * HEAD_DIM), BF16),
            jax.ShapeDtypeStruct((blocks, group * loc, HEAD_DIM), F32),
            jax.ShapeDtypeStruct((blocks, group * loc, HEAD_DIM), F32),
        ),
        in_specs=[SMEM, VMEM],
        out_specs=(VMEM,) * 3,
        scratch_shapes=[pltpu.VMEM((total, HEAD_DIM), BF16)] * 2,
        compiler_params=params(32),
        cost_estimate=cost(),
    )(at, rec)


def attend_back_kernel(group, at_ref, rec_ref, grad_ref, full_ref, lse_ref, cos_ref, sin_ref, out_ref, keys, vals, d_keys, d_vals):
    blocks, loc, _ = rec_ref.shape
    base = group * HEAD_DIM
    scale = HEAD_DIM ** -0.5
    for p in range(blocks):
        i = at_ref[p]
        keys[p * loc:(p + 1) * loc, :] = rec_ref[i, :, base:base + HEAD_DIM]
        vals[p * loc:(p + 1) * loc, :] = rec_ref[i, :, base + HEAD_DIM:base + 2 * HEAD_DIM]
    rows = lax.broadcasted_iota(jnp.int32, (group * loc, loc), 0) % loc
    cols = lax.broadcasted_iota(jnp.int32, (group * loc, loc), 1)
    keep = cols <= rows

    def unrot(t, cosine, sine):
        return (t * cosine - pltpu.roll(t, HEAD_DIM // 2, 1) * sine).astype(BF16)

    for p in reversed(range(blocks)):
        i = at_ref[p]
        count = (p + 1) * loc
        span = slice(p * loc, count)
        query = jnp.concatenate([rec_ref[i, :, g * HEAD_DIM:(g + 1) * HEAD_DIM] for g in range(group)], axis=0)
        grad = jnp.concatenate([grad_ref[i, :, g * HEAD_DIM:(g + 1) * HEAD_DIM] for g in range(group)], axis=0)
        lse = lse_ref[p][:, :1]
        delta = jnp.sum(grad.astype(F32) * full_ref[p], axis=-1, keepdims=True)
        probs = jnp.exp(dot_rt(query, keys[:count, :]) * scale - lse)
        last = jnp.where(keep, probs[:, count - loc:], 0.0)
        probs = jnp.concatenate([probs[:, :count - loc], last], axis=1) if p else last
        d_probs = dot_rt(grad, vals[:count, :])
        g_scores = (probs * (d_probs - delta) * scale).astype(BF16)
        d_query = dot(g_scores, keys[:count, :])
        dk = dot_lt(g_scores, query)
        dv = dot_lt(probs.astype(BF16), grad)
        if p == blocks - 1:
            d_keys[...] = dk
            d_vals[...] = dv
        else:
            d_keys[:count, :] += dk
            d_vals[:count, :] += dv
        cosine, sine = cos_ref[span, :], sin_ref[span, :]
        for g in range(group):
            out_ref[i, :, g * HEAD_DIM:(g + 1) * HEAD_DIM] = unrot(d_query[g * loc:(g + 1) * loc], cosine, sine)
        out_ref[i, :, base:base + HEAD_DIM] = unrot(d_keys[span, :], cosine, sine)
        out_ref[i, :, base + HEAD_DIM:base + 2 * HEAD_DIM] = d_vals[span, :].astype(BF16)


def attend_back(at, rec, grad, full, lse, cosine, sine, group):
    blocks, loc, cols = rec.shape
    total = blocks * loc
    return pl.pallas_call(
        functools.partial(attend_back_kernel, group),
        out_shape=jax.ShapeDtypeStruct((blocks, loc, cols), BF16),
        in_specs=[SMEM] + [VMEM] * 6,
        out_specs=VMEM,
        scratch_shapes=[pltpu.VMEM((total, HEAD_DIM), BF16)] * 2 + [pltpu.VMEM((total, HEAD_DIM), F32)] * 2,
        compiler_params=params(60),
        cost_estimate=cost(),
    )(at, rec, grad, full, lse, cosine, sine)


def out_kernel(kv, mix_ref, w_ref, cat_ref, *outs):
    cols = mix_ref.shape[2]
    for s, out in enumerate(outs):
        cat_ref[s] = jnp.concatenate([mix_ref[s * kv + n] for n in range(kv)], axis=1)
        out[...] = dot(cat_ref[s], w_ref[...]).astype(BF16)


def out_project(mixed, w_out, seqs):
    units, loc, cols = mixed.shape
    kv = units // seqs
    width = w_out.shape[1]
    res = pl.pallas_call(
        functools.partial(out_kernel, kv),
        out_shape=(jax.ShapeDtypeStruct((seqs, loc, kv * cols), BF16),)
        + (jax.ShapeDtypeStruct((loc, width), BF16),) * seqs,
        in_specs=[VMEM] * 2,
        out_specs=(VMEM,) * (seqs + 1),
        compiler_params=params(24),
        cost_estimate=cost(),
    )(mixed, w_out)
    return res[0], res[1:]


def input_grads_kernel(seqs, kv, groups, back_ref, x_ref, wq_ref, wk_ref, wv_ref, *refs):
    gain_refs, outs, (rows_ref, inv_ref, attn_ref) = refs[:seqs], refs[seqs:seqs + groups], refs[seqs + groups:]
    per = seqs // groups
    loc, width = x_ref.shape[1], x_ref.shape[2]
    group = wq_ref.shape[1] // (kv * HEAD_DIM)
    gather(back_ref, rows_ref, seqs, kv, group)
    at_k = kv * group * HEAD_DIM
    at_v = at_k + kv * HEAD_DIM
    for s in range(seqs):
        x = x_ref[s].astype(F32)
        inv = lax.rsqrt(jnp.mean(x * x, axis=-1, keepdims=True) + EPS)
        inv_ref[s * loc:(s + 1) * loc, :] = jnp.broadcast_to(inv, (loc, HEAD_DIM))
    tile = 512
    for t in range(width // tile):
        span = slice(t * tile, (t + 1) * tile)
        grad = dot_rt(rows_ref[:, :at_k], wq_ref[span, :])
        grad += dot_rt(rows_ref[:, at_k:at_v], wk_ref[span, :])
        grad += dot_rt(rows_ref[:, at_v:], wv_ref[span, :])
        total = 0.0
        for s in range(seqs):
            part = grad[s * loc:(s + 1) * loc]
            at = (s % per) * loc
            outs[s // per][at:at + loc, span] = part.astype(BF16)
            unit = x_ref[s, :, span].astype(F32) * inv_ref[s * loc:(s + 1) * loc, :1]
            total = total + jnp.sum(part * unit, axis=0, keepdims=True)
        attn_ref[:, span] = total
    mlp = sum(ref[...] for ref in gain_refs)
    lines = []
    for gain in (attn_ref[...], mlp):
        high = gain.astype(BF16).astype(F32)
        lines += [high, gain - high]
    row = lax.broadcasted_iota(jnp.int32, (16, width), 0)
    extra = jnp.zeros((16, width), F32)
    for i, gain in enumerate(lines):
        extra = jnp.where(row == i, gain, extra)
    outs[0][per * loc:, :] = extra.astype(BF16)


def gather(back_ref, rows_ref, seqs, kv, group):
    loc = back_ref.shape[1]
    wide = group * HEAD_DIM
    for s in range(seqs):
        for n in range(kv):
            span = slice(s * loc, (s + 1) * loc)
            rows_ref[span, n * wide:(n + 1) * wide] = back_ref[s * kv + n, :, :wide]
            for i in range(2):
                at = kv * wide + (i * kv + n) * HEAD_DIM
                rows_ref[span, at:at + HEAD_DIM] = back_ref[s * kv + n, :, wide + i * HEAD_DIM:wide + (i + 1) * HEAD_DIM]


def input_grads(back, x, wq, wk, wv, gains, groups):
    seqs, loc, width = x.shape
    kv = wk.shape[1] // HEAD_DIM
    cols = wq.shape[1] + 2 * wk.shape[1]
    rows = seqs * loc // groups
    return pl.pallas_call(
        functools.partial(input_grads_kernel, seqs, kv, groups),
        out_shape=(jax.ShapeDtypeStruct((rows + 16, width), BF16),) + (jax.ShapeDtypeStruct((rows, width), BF16),) * (groups - 1),
        in_specs=[VMEM] * (5 + seqs),
        out_specs=(VMEM,) * groups,
        scratch_shapes=[
            pltpu.VMEM((seqs * loc, cols), BF16),
            pltpu.VMEM((seqs * loc, HEAD_DIM), F32),
            pltpu.VMEM((1, width), F32),
        ],
        compiler_params=params(60),
        cost_estimate=cost(),
    )(back, x, wq, wk, wv, *gains)


def shares_call(body, fixed, tall, cols, scratch, core, shares):
    width = tall[0].shape[-1]
    tile = width // shares

    def mine(step, keep, core_ref):
        return 2 * step + jnp.where(keep == 0, 1 - core_ref[0], core_ref[0])

    def tall_spec(a):
        lead = (0,) * (a.ndim - 1)
        return pl.BlockSpec(a.shape[:-1] + (tile,), lambda i, k, c: lead + (mine(i, k, c),))

    out = pl.BlockSpec((1, tile, cols), lambda i, k, c: (i, 0, 0))
    return pl.pallas_call(
        body,
        grid_spec=pltpu.PrefetchScalarGridSpec(
            num_scalar_prefetch=1,
            grid=(shares // 2, 2),
            in_specs=[pl.BlockSpec(a.shape, lambda i, k, c, n=a.ndim: (0,) * n) for a in fixed] + [tall_spec(a) for a in tall],
            out_specs=(out, out),
            scratch_shapes=scratch,
        ),
        out_shape=(jax.ShapeDtypeStruct((shares // 2, tile, cols), BF16),) * 2,
        compiler_params=params(60),
        cost_estimate=cost(),
    )(core, *fixed, *tall)


def put_share(send_ref, keep_ref, pieces):
    def store(ref):
        at = 0
        for piece in pieces:
            ref[0, :, at:at + piece.shape[1]] = piece.astype(BF16)
            at += piece.shape[1]

    @pl.when(pl.program_id(1) == 0)
    def _():
        store(send_ref)

    @pl.when(pl.program_id(1) == 1)
    def _():
        store(keep_ref)


def attn_grads_kernel(seqs, kv, group, core_ref, back_ref, mix_ref, norm_ref, *refs):
    grad_refs, (send_ref, keep_ref, rows_ref) = refs[:seqs], refs[seqs:]

    @pl.when((pl.program_id(0) == 0) & (pl.program_id(1) == 0))
    def _():
        gather(back_ref, rows_ref, seqs, kv, group)

    rows = rows_ref.shape[0]
    left = norm_ref[...].reshape(rows, norm_ref.shape[2])
    grad = jnp.concatenate([ref[...] for ref in grad_refs], axis=0)
    mixed = mix_ref[...].reshape(rows, mix_ref.shape[2])
    put_share(send_ref, keep_ref, [dot_lt(left, rows_ref[...]), dot_lt(grad, mixed)])


def attn_grads(core, back, mixed, normed, g_attns, kv, shares):
    seqs, loc, width = normed.shape
    group = back.shape[2] // HEAD_DIM - 2
    cols = kv * back.shape[2]
    scratch = [pltpu.VMEM((seqs * loc, cols), BF16)]
    body = functools.partial(attn_grads_kernel, seqs, kv, group)
    return shares_call(body, (back, mixed), (normed,) + tuple(g_attns), cols + mixed.shape[2], scratch, core, shares)


def ffn_grads_kernel(seqs, core_ref, *refs):
    fixed, refs = refs[:3 * seqs], refs[3 * seqs:]
    down_ref, norm_refs, (send_ref, keep_ref), scratch = refs[0], refs[1:seqs + 1], refs[seqs + 1:seqs + 3], refs[seqs + 3:]

    @pl.when((pl.program_id(0) == 0) & (pl.program_id(1) == 0))
    def _():
        loc = fixed[0].shape[0]
        for i, whole in enumerate(scratch):
            for s in range(seqs):
                whole[s * loc:(s + 1) * loc, :] = fixed[i * seqs + s][...]

    gate_ref, up_ref, hid_ref = scratch
    norm = jnp.concatenate([ref[...] for ref in norm_refs], axis=0)
    put_share(
        send_ref,
        keep_ref,
        [dot_lt(norm, gate_ref[...]), dot_lt(norm, up_ref[...]), dot_lt(down_ref[...], hid_ref[...])],
    )


def ffn_grads(core, gates, ups, hiddens, g_down, norms, shares):
    loc, units = gates[0].shape
    scratch = [pltpu.VMEM((len(gates) * loc, units), BF16)] * 3
    body = functools.partial(ffn_grads_kernel, len(gates))
    fixed = tuple(gates) + tuple(ups) + tuple(hiddens)
    return shares_call(body, fixed, (g_down,) + tuple(norms), 3 * units, scratch, core, shares)


def fold_two_kernel(place_ref, *refs):
    keeps, gots, outs = refs[:4], refs[4:8], refs[8:]
    for keep, got, out in zip(keeps, gots, outs):
        out[0] = (keep[0, 0].astype(F32) + got[0, 0].astype(F32)).astype(BF16)


def fold_two(place, keep, got):
    _, rows, cols = keep.shape
    half = rows // 2
    keep, got = keep.reshape(2, 2, rows, cols), got.reshape(2, 2, rows, cols)
    tile = half // 2
    ins = []
    for own in (0, 1):
        ins.append(pl.BlockSpec((1, 1, tile, cols), lambda i, j, p, own=own: (i, jnp.where(own == 1, p[0], 1 - p[0]), j, 0)))
    for own in (0, 1):
        ins.append(pl.BlockSpec((1, 1, tile, cols), lambda i, j, p, own=own: (jnp.where(own == 1, p[1], 1 - p[1]), i, j + 2, 0)))
    return pl.pallas_call(
        fold_two_kernel,
        grid_spec=pltpu.PrefetchScalarGridSpec(
            num_scalar_prefetch=1,
            grid=(2, 2),
            in_specs=ins + ins,
            out_specs=(pl.BlockSpec((1, tile, cols), lambda i, j, p: (i, j, 0)),) * 4,
        ),
        out_shape=(jax.ShapeDtypeStruct((2, half, cols), BF16),) * 4,
        compiler_params=params(40),
        cost_estimate=cost(),
    )(place, keep, keep, keep, keep, got, got, got, got)


def fold_three(place, upper, upper_got, lower, lower_got):
    _, half, cols = upper.shape
    tile = half // 2
    ins = []
    for axis in (1, 0):
        for own in (0, 1):
            ins.append(pl.BlockSpec((1, 1, tile, cols), lambda j, p, own=own, axis=axis: (0, jnp.where(own == 1, p[axis], 1 - p[axis]), j, 0)))
    flat = pl.BlockSpec((1, tile, cols), lambda j, p: (0, j, 0))
    u, ug, l, lg = (a[None] for a in (upper, upper_got, lower, lower_got))
    res = pl.pallas_call(
        fold_two_kernel,
        grid_spec=pltpu.PrefetchScalarGridSpec(
            num_scalar_prefetch=1, grid=(2,), in_specs=ins + ins, out_specs=(flat,) * 4
        ),
        out_shape=(jax.ShapeDtypeStruct((1, half, cols), BF16),) * 4,
        compiler_params=params(40),
        cost_estimate=cost(),
    )(place, u, u, l, l, ug, ug, lg, lg)
    return [a[0] for a in res]


def fold_four_kernel(widths, upper, upper_got, lower, lower_got, *outs):
    half = upper.shape[0]
    for at, (one, two) in enumerate(((upper, upper_got), (lower, lower_got))):
        start = 0
        for out, width in zip(outs, widths):
            part = one[:, start:start + width].astype(F32) + two[:, start:start + width].astype(F32)
            if out is outs[-1]:
                out[:, at * half:(at + 1) * half] = part.T
            else:
                out[at * half:(at + 1) * half, :] = part
            start += width


def fold_four(widths, upper, upper_got, lower, lower_got):
    rows = 2 * upper.shape[0]
    shapes = [(rows, w) for w in widths[:-1]] + [(widths[-1], rows)]
    return pl.pallas_call(
        functools.partial(fold_four_kernel, widths),
        out_shape=tuple(jax.ShapeDtypeStruct(shape, F32) for shape in shapes),
        in_specs=[VMEM] * 4,
        out_specs=(VMEM,) * len(widths),
        compiler_params=params(40),
        cost_estimate=cost(),
    )(upper, upper_got, lower, lower_got)


def finish_kernel(seqs, mid_ref, x_ref, gain_ref, *refs):
    inner, ends, resids, out_ref = refs[:seqs], refs[seqs:2 * seqs], refs[2 * seqs:3 * seqs], refs[3 * seqs]
    gain = gain_ref[...].astype(F32)
    for s in range(seqs):
        grad = jnp.where(mid_ref[0] == 1, inner[s][...].astype(F32), ends[s][...].astype(F32))
        x = x_ref[s].astype(F32)
        inv = lax.rsqrt(jnp.mean(x * x, axis=-1, keepdims=True) + EPS)
        unit = x * inv
        scaled = grad * gain
        back = inv * (scaled - unit * jnp.mean(scaled * unit, axis=-1, keepdims=True))
        out_ref[:, s, :] = resids[s][...] + back


def by_seq(group, seqs, loc, tile):
    per = seqs // len(group)
    return [
        (group[s // per], pl.BlockSpec((tile, group[0].shape[1]), lambda i, at=(s % per) * (loc // tile): (i + at, 0)))
        for s in range(seqs)
    ]


def finish(mid, x, gain, inner, ends, resids):
    seqs, loc, width = x.shape
    tile = 32
    parts = by_seq(inner, seqs, loc, tile) + by_seq(ends, seqs, loc, tile) + by_seq(resids, seqs, loc, tile)
    return pl.pallas_call(
        functools.partial(finish_kernel, seqs),
        grid=(loc // tile,),
        out_shape=jax.ShapeDtypeStruct((loc, seqs, width), F32),
        in_specs=[SMEM, pl.BlockSpec((seqs, tile, width), lambda i: (0, i, 0)), pl.BlockSpec((1, width), lambda i: (0, 0))]
        + [spec for _, spec in parts],
        out_specs=pl.BlockSpec((tile, seqs, width), lambda i: (i, 0, 0)),
        compiler_params=params(60),
        cost_estimate=cost(),
    )(mid, x, gain, *(a for a, _ in parts))


def output_kernel(seqs, mid_ref, x_ref, *refs):
    attn, inner, ends, out_ref, wide = refs[:seqs], refs[seqs:2 * seqs], refs[2 * seqs:3 * seqs], refs[3 * seqs], refs[3 * seqs + 1]
    for s in range(seqs):
        down = jnp.where(mid_ref[0] == 1, inner[s][...].astype(F32), ends[s][...].astype(F32))
        wide[:, s, :] = x_ref[s].astype(F32) + attn[s][...].astype(F32) + down
    out_ref[...] = wide[...].astype(BF16)


def block_output(mid, x, attn, inner, ends):
    seqs, loc, width = x.shape
    tile = 32
    parts = by_seq(attn, seqs, loc, tile) + by_seq(inner, seqs, loc, tile) + by_seq(ends, seqs, loc, tile)
    return pl.pallas_call(
        functools.partial(output_kernel, seqs),
        grid=(loc // tile,),
        out_shape=jax.ShapeDtypeStruct((loc, seqs, width), BF16),
        in_specs=[SMEM, pl.BlockSpec((seqs, tile, width), lambda i: (0, i, 0))] + [spec for _, spec in parts],
        out_specs=pl.BlockSpec((tile, seqs, width), lambda i: (i, 0, 0)),
        scratch_shapes=[pltpu.VMEM((tile, seqs, width), F32)],
        compiler_params=params(32),
        cost_estimate=cost(),
    )(mid, x, *(a for a, _ in parts))


def add_kernel(left, right, out):
    out[...] = (left[...].astype(F32) + right[...].astype(F32)).astype(BF16)


def add(left, right):
    return pl.pallas_call(
        add_kernel,
        out_shape=jax.ShapeDtypeStruct(left.shape, BF16),
        in_specs=[VMEM, VMEM],
        out_specs=VMEM,
        compiler_params=params(16),
        cost_estimate=cost(),
    )(left, right)


def rope_tables(positions, head_dim):
    half = head_dim // 2
    freq = jnp.exp(jnp.arange(half, dtype=jnp.float32) * (-2.0 * math.log(THETA) / head_dim))
    angles = positions.astype(jnp.float32)[:, None] * freq[None, :]
    return (jnp.cos(angles), jnp.sin(angles))


def rotate(values, cosine, sine):
    half = values.shape[-1] // 2
    first = values[..., :half]
    second = values[..., half:]
    cosine = cosine[:, None, None, :]
    sine = sine[:, None, None, :]
    return jnp.concatenate(
        [first * cosine - second * sine, second * cosine + first * sine], axis=-1
    )


def inverse_rms(values):
    return lax.rsqrt(jnp.mean(values * values, axis=-1, keepdims=True) + EPS)


def norm_back(values, inverse, gain, grad):
    unit = values * inverse
    scaled = grad * gain
    back = inverse * (scaled - unit * jnp.mean(scaled * unit, axis=-1, keepdims=True))
    return (back, jnp.sum(grad * unit, axis=(0, 1)))


def matmul(values, weight):
    return jnp.einsum("lsd,de->lse", values, weight, preferred_element_type=jnp.float32)


def matmul_back(values, weight):
    return jnp.einsum("lse,de->lsd", values, weight, preferred_element_type=jnp.float32)


def weight_grad(left, right):
    return jnp.einsum("lsd,lse->de", left, right, preferred_element_type=jnp.float32)


def general(
    hidden_in,
    block_order,
    seq_labels,
    exit_scales,
    attn_gain,
    w_query,
    w_key,
    w_value,
    w_out,
    mlp_gain,
    w_gate,
    w_up,
    w_down,
    d_out,
):
    f32 = jnp.float32
    bf16 = jnp.bfloat16
    loc, seqs, width = hidden_in.shape
    head_dim = HEAD_DIM
    q_heads = w_query.shape[1] // head_dim
    kv_heads = w_key.shape[1] // head_dim
    group = q_heads // kv_heads
    scale = head_dim ** (-0.5)
    blocks_all = block_order.shape[0]
    total_rows = loc * lax.axis_size("blk")
    key_rows = math.gcd(512, total_rows)
    block_count = total_rows // key_rows
    kv_width = 2 * kv_heads * head_dim
    positions = block_order[lax.axis_index("blk")] * loc + jnp.arange(loc, dtype=jnp.int32)
    cosine, sine = rope_tables(positions, head_dim)

    def key_positions(start, count):
        index = start + jnp.arange(count, dtype=jnp.int32)
        owner = index // loc
        table = jnp.sum(
            jnp.where(
                owner[:, None] == jnp.arange(blocks_all, dtype=jnp.int32)[None, :],
                block_order[None, :],
                0,
            ),
            axis=1,
        )
        return table * loc + index % loc

    xin = hidden_in.astype(f32)
    inv_a = inverse_rms(xin)
    gain_a = attn_gain.astype(f32)
    normed = (xin * inv_a * gain_a).astype(bf16)
    query_bf = rotate(
        matmul(normed, w_query).reshape(loc, seqs, q_heads, head_dim), cosine, sine
    ).astype(bf16)
    keys_bf = (
        rotate(matmul(normed, w_key).reshape(loc, seqs, kv_heads, head_dim), cosine, sine)
        .astype(bf16)
        .reshape(loc, seqs, kv_heads * head_dim)
    )
    vals_bf = matmul(normed, w_value).astype(bf16)
    query_g = query_bf.reshape(loc, seqs, kv_heads, group, head_dim)
    starts = jnp.arange(block_count, dtype=jnp.int32) * key_rows
    top = jnp.full((seqs, kv_heads, group, loc), NEG, f32)
    key_part = lax.all_gather(keys_bf, "blk", axis=0, tiled=True)
    val_part = lax.all_gather(vals_bf, "blk", axis=0, tiled=True)
    count = key_part.shape[0]
    kk = key_part.reshape(count, seqs, kv_heads, head_dim)
    vv = val_part.reshape(count, seqs, kv_heads, head_dim)
    mask = key_positions(jnp.int32(0), count)[None, :] <= positions[:, None]
    raw = jnp.einsum("lsngd,msnd->snglm", query_g, kk, preferred_element_type=f32)
    scores = jnp.where(mask, raw * scale, NEG)
    new_top = jnp.maximum(top, jnp.max(scores, axis=-1))
    weights = jnp.where(mask, jnp.exp(scores - new_top[..., None]), 0.0)
    total = jnp.sum(weights, axis=-1)
    acc = jnp.einsum("snglm,msnd->sngld", weights.astype(bf16), vv, preferred_element_type=f32)
    top, total, acc = (new_top, total, acc)
    lse = top + jnp.log(total)
    mixed_raw = acc / total[..., None]
    mixed_bf = (
        mixed_raw.transpose(3, 0, 1, 2, 4).reshape(loc, seqs, q_heads * head_dim).astype(bf16)
    )
    resid = xin + lax.psum(matmul(mixed_bf, w_out).astype(jnp.bfloat16), "tp").astype(jnp.float32)
    inv_m = inverse_rms(resid)
    gain_m = mlp_gain.astype(f32)
    normed_m = (resid * inv_m * gain_m).astype(bf16)
    gate = matmul(normed_m, w_gate)
    up = matmul(normed_m, w_up)
    sig = jax.nn.sigmoid(gate)
    silu = gate * sig
    hidden = (silu * up).astype(bf16)
    output = resid + lax.psum(matmul(hidden, w_down).astype(jnp.bfloat16), "tp").astype(jnp.float32)
    block_out = output.astype(bf16)
    scale_rows = jnp.where(seq_labels == 1, exit_scales[1], exit_scales[0])
    cot = d_out.astype(f32) * scale_rows[None, :, None]
    g_down = cot.astype(bf16)
    d_w_down = weight_grad(hidden, g_down)
    d_hidden = matmul_back(g_down, w_down)
    g_up = (d_hidden * silu).astype(bf16)
    g_gate = (d_hidden * up * (sig * (1.0 + gate * (1.0 - sig)))).astype(bf16)
    d_w_gate = weight_grad(normed_m, g_gate)
    d_w_up = weight_grad(normed_m, g_up)
    d_nm = lax.psum(
        (matmul_back(g_gate, w_gate) + matmul_back(g_up, w_up)).astype(jnp.bfloat16), "tp"
    ).astype(jnp.float32)
    d_resid_norm, d_mlp_gain = norm_back(resid, inv_m, gain_m, d_nm)
    d_resid = cot + d_resid_norm
    g_attn = d_resid.astype(bf16)
    d_w_out = weight_grad(mixed_bf, g_attn)
    g_mixed = matmul_back(g_attn, w_out).astype(bf16)
    g_mixed_g = g_mixed.reshape(loc, seqs, kv_heads, group, head_dim)
    delta = jnp.sum(g_mixed_g.astype(f32).transpose(1, 2, 3, 0, 4) * mixed_raw, axis=-1)
    whole_keys, whole_vals = (
        lax.all_gather(keys_bf, "blk", axis=0, tiled=True),
        lax.all_gather(vals_bf, "blk", axis=0, tiled=True),
    )

    def probe(kk, vv, start, count):
        mask = key_positions(start, count)[None, :] <= positions[:, None]
        raw = jnp.einsum("lsngd,msnd->snglm", query_g, kk, preferred_element_type=f32)
        probs = jnp.where(mask, jnp.exp(raw * scale - lse[..., None]), 0.0)
        d_probs = jnp.einsum("lsngd,msnd->snglm", g_mixed_g, vv, preferred_element_type=f32)
        g_scores = (probs * (d_probs - delta[..., None]) * scale).astype(bf16)
        return (g_scores, probs)

    def kv_pair(g_scores, probs, count):
        d_keys = jnp.einsum("snglm,lsngd->msnd", g_scores, query_g, preferred_element_type=f32)
        d_vals = jnp.einsum(
            "snglm,lsngd->msnd", probs.astype(bf16), g_mixed_g, preferred_element_type=f32
        )
        return jnp.concatenate([d_keys, d_vals], axis=2).reshape(count, seqs, kv_width)

    scan_items = (
        whole_keys.reshape(block_count, key_rows, seqs, -1),
        whole_vals.reshape(block_count, key_rows, seqs, -1),
        starts,
    )
    zero_query = jnp.zeros((loc, seqs, kv_heads, group, head_dim), f32)

    def back_step(d_query, item):
        key_part, val_part, start = item
        kk = key_part.reshape(key_rows, seqs, kv_heads, head_dim)
        vv = val_part.reshape(key_rows, seqs, kv_heads, head_dim)
        g_scores, probs = probe(kk, vv, start, key_rows)
        d_query = d_query + jnp.einsum(
            "snglm,msnd->lsngd", g_scores, kk, preferred_element_type=f32
        )
        return (d_query, kv_pair(g_scores, probs, key_rows))

    d_query, kv_terms = lax.scan(back_step, zero_query, scan_items)
    kv_local = lax.psum_scatter(
        kv_terms.reshape(total_rows, seqs, kv_width).astype(jnp.bfloat16),
        "blk",
        scatter_dimension=0,
        tiled=True,
    ).astype(jnp.float32)
    kv_local = kv_local.reshape(loc, seqs, 2, kv_heads, head_dim)
    g_q = (
        rotate(d_query.reshape(loc, seqs, q_heads, head_dim), cosine, -sine)
        .astype(bf16)
        .reshape(loc, seqs, q_heads * head_dim)
    )
    g_k = (
        rotate(kv_local[:, :, 0], cosine, -sine)
        .astype(bf16)
        .reshape(loc, seqs, kv_heads * head_dim)
    )
    g_v = kv_local[:, :, 1].astype(bf16).reshape(loc, seqs, kv_heads * head_dim)
    d_w_query = weight_grad(normed, g_q)
    d_w_key = weight_grad(normed, g_k)
    d_w_value = weight_grad(normed, g_v)
    d_n = lax.psum(
        (matmul_back(g_q, w_query) + matmul_back(g_k, w_key) + matmul_back(g_v, w_value)).astype(
            jnp.bfloat16
        ),
        "tp",
    ).astype(jnp.float32)
    d_in_norm, d_attn_gain = norm_back(xin, inv_a, gain_a, d_n)
    d_hidden_in = d_resid + d_in_norm
    d_attn_gain, d_w_query, d_w_key, d_w_value, d_w_out, d_mlp_gain, d_w_gate, d_w_up, d_w_down = (
        lax.psum_scatter(
            d_attn_gain.astype(jnp.bfloat16), "blk", scatter_dimension=0, tiled=True
        ).astype(jnp.float32),
        lax.psum_scatter(
            d_w_query.astype(jnp.bfloat16), "blk", scatter_dimension=0, tiled=True
        ).astype(jnp.float32),
        lax.psum_scatter(
            d_w_key.astype(jnp.bfloat16), "blk", scatter_dimension=0, tiled=True
        ).astype(jnp.float32),
        lax.psum_scatter(
            d_w_value.astype(jnp.bfloat16), "blk", scatter_dimension=0, tiled=True
        ).astype(jnp.float32),
        lax.psum_scatter(
            d_w_out.astype(jnp.bfloat16), "blk", scatter_dimension=1, tiled=True
        ).astype(jnp.float32),
        lax.psum_scatter(
            d_mlp_gain.astype(jnp.bfloat16), "blk", scatter_dimension=0, tiled=True
        ).astype(jnp.float32),
        lax.psum_scatter(
            d_w_gate.astype(jnp.bfloat16), "blk", scatter_dimension=0, tiled=True
        ).astype(jnp.float32),
        lax.psum_scatter(
            d_w_up.astype(jnp.bfloat16), "blk", scatter_dimension=0, tiled=True
        ).astype(jnp.float32),
        lax.psum_scatter(
            d_w_down.astype(jnp.bfloat16), "blk", scatter_dimension=1, tiled=True
        ).astype(jnp.float32),
    )
    return (
        block_out,
        d_hidden_in,
        d_attn_gain,
        d_w_query,
        d_w_key,
        d_w_value,
        d_w_out,
        d_mlp_gain,
        d_w_gate,
        d_w_up,
        d_w_down,
    )


class Steps:
    def __init__(self):
        self.last = None

    def enter(self, *values):
        if self.last is not None:
            values, _ = lax.optimization_barrier((values, self.last))
        return values if len(values) > 1 else values[0]

    def leave(self, value):
        self.last = value
        return value


class Line:
    def __init__(self, steps, middle, parts):
        self.steps, self.middle, self.parts = steps, middle, list(parts)
        count = len(self.parts)
        self.first, self.half, self.second, self.total, self.third, self.done = ([None] * count for _ in range(6))

    def one(self, c):
        self.first[c] = lax.ppermute(self.parts[c], "tp", [(0, 1), (3, 2)])

    def two(self, c):
        part, got = self.steps.enter(self.parts[c], self.first[c])
        self.half[c] = self.steps.leave(add(part, got))
        self.second[c] = lax.ppermute(self.half[c], "tp", [(1, 2), (2, 1)])

    def three(self, c):
        half, got = self.steps.enter(self.half[c], self.second[c])
        self.total[c] = self.steps.leave(add(half, got))
        self.third[c] = lax.ppermute(self.total[c], "tp", [(1, 0), (2, 3)])

    def four(self, c):
        total, got = self.steps.enter(self.total[c], self.third[c])
        self.done[c] = self.steps.leave(jnp.where(self.middle, total, got))

    def five(self, c):
        self.third[c] = self.steps.leave(self.steps.enter(self.third[c]))


def partner(bit):
    return [(i, i ^ bit) for i in range(8)]


class Scatter:
    def __init__(self, steps, place, send, keep):
        self.steps, self.place, self.send, self.keep = steps, place, send, keep

    def one_go(self):
        self.got = lax.ppermute(self.steps.enter(self.send), "blk", partner(1))

    def two(self):
        keep, got = self.steps.enter(self.keep, self.got)
        self.away, self.upper, self.off, self.lower = fold_two(self.place, keep, got)
        self.steps.leave(self.upper)

    def two_go(self, first=2, second=4):
        away, off = self.steps.enter(self.away, self.off)
        self.upper_got = lax.ppermute(away, "blk", partner(first))
        self.lower_got = lax.ppermute(off, "blk", partner(second))

    def three(self):
        values = self.steps.enter(self.upper, self.upper_got, self.lower, self.lower_got)
        self.away, self.upper, self.off, self.lower = fold_three(self.place, *values)
        self.steps.leave(self.upper)

    def three_go(self):
        self.two_go(4, 2)

    def four(self, widths):
        values = self.steps.enter(self.upper, self.upper_got, self.lower, self.lower_got)
        res = fold_four(widths, *values)
        self.steps.leave(res[0])
        return res


def inverse(values):
    return lax.rsqrt(jnp.mean(values * values, axis=-1, keepdims=True) + EPS)


def tables(positions):
    cosine, sine = rope_tables(positions, HEAD_DIM)
    return jnp.concatenate([cosine, cosine], axis=1), jnp.concatenate([-sine, sine], axis=1)


def fast(
    hidden_in,
    block_order,
    seq_labels,
    exit_scales,
    attn_gain,
    w_query,
    w_key,
    w_value,
    w_out,
    mlp_gain,
    w_gate,
    w_up,
    w_down,
    d_out,
):
    loc, seqs, width = hidden_in.shape
    blocks = block_order.shape[0]
    rows = seqs * loc
    units = w_gate.shape[1]
    kv = w_key.shape[1] // HEAD_DIM
    group = w_query.shape[1] // w_key.shape[1]
    wide = group * HEAD_DIM
    me = lax.axis_index("blk")
    line = lax.axis_index("tp")
    middle = (line == 1) | (line == 2)
    index = jnp.arange(blocks, dtype=jnp.int32)
    at = jnp.sum(jnp.where(block_order[None, :] == index[:, None], index[None, :], 0), axis=1)
    mine = block_order[me] * loc + jnp.arange(loc, dtype=jnp.int32)
    steps = Steps()
    enter, leave = steps.enter, steps.leave

    x = hidden_in.transpose(1, 0, 2)
    cosine, sine = tables(mine)
    messages, normed = project(x, attn_gain[None, :], cosine, sine, w_query, w_key, w_value)
    leave(messages)
    rec = lax.all_to_all(messages, "blk", 0, 0, tiled=True)
    scales = jnp.where(seq_labels == 1, exit_scales[1], exit_scales[0])
    cot = enter(d_out).transpose(1, 0, 2).astype(F32) * scales[:, None, None]
    g_down = leave(cot.astype(BF16).reshape(rows, width))
    d_hidden = leave(dot_rt(g_down, w_down).astype(BF16))
    mixed, full, lse = attend(at, enter(rec), group)
    leave(mixed)
    mixed = lax.all_to_all(mixed, "blk", 0, 0, tiled=True)
    all_cosine, all_sine = tables(enter(jnp.arange(blocks * loc, dtype=jnp.int32)))
    leave(all_cosine)
    mixed, parts = out_project(enter(mixed), w_out, seqs)
    leave(mixed)

    gain_m = mlp_gain.astype(F32)
    attn = Line(steps, middle, parts)
    back = Line(steps, middle, [None] * seqs)
    norms, hiddens, gates, ups, gains = ([None] * seqs for _ in range(5))

    def feed(s):
        total = attn.done[s]
        resid = x[s].astype(F32) + total.astype(F32)
        unit = resid * inverse(resid)
        norm = (unit * gain_m).astype(BF16)
        gate = dot(norm, w_gate)
        up = dot(norm, w_up)
        sig = jax.nn.sigmoid(gate)
        silu = gate * sig
        grad_h = d_hidden[s * loc:(s + 1) * loc].astype(F32)
        g_up = (grad_h * silu).astype(BF16)
        g_gate = (grad_h * up * (sig * (1.0 + gate * (1.0 - sig)))).astype(BF16)
        grad = dot_rt(g_gate, w_gate) + dot_rt(g_up, w_up)
        gains[s] = jnp.sum(grad * unit, axis=0)
        back.parts[s] = leave(grad.astype(BF16))
        norms[s], gates[s], ups[s] = norm, g_gate, g_up
        hiddens[s] = (silu * up).astype(BF16)

    d_resids, g_attns, sends = ([None] * seqs for _ in range(3))

    def norm_back(s):
        resid = x[s].astype(F32) + attn.done[s].astype(F32)
        inv = inverse(resid)
        unit = resid * inv
        scaled = back.done[s].astype(F32) * gain_m
        d_resids[s] = cot[s] + inv * (scaled - unit * jnp.mean(scaled * unit, axis=-1, keepdims=True))
        g_attns[s] = d_resids[s].astype(BF16)
        sends[s] = leave(dot_rt(g_attns[s], w_out).astype(BF16))

    def run(lines, *texts):
        for word in " ".join(texts).split():
            name, c = word[:-1], int(word[-1])
            if name == "F":
                feed(c)
            elif name == "N":
                norm_back(c)
            elif name == "O":
                hidden = jnp.concatenate(enter(hiddens[2 * c:2 * c + 2]), axis=0)
                outs.parts[c] = leave(dot(hidden, w_down).astype(BF16))
            else:
                obj = lines[name[0]]
                (obj.one, obj.two, obj.three, obj.four, obj.five)[int(name[1]) - 1](c)

    outs = Line(steps, middle, [None] * 2)
    lines = {"a": attn, "b": back, "c": outs}
    core = (me % 2).astype(jnp.int32)[None]
    place = jnp.stack([(me // 2) % 2, me // 4]).astype(jnp.int32)
    run(
        lines,
        "a10 a11 a12 a13",
        "a20 a21 a30 a22",
        "a31 a40 F0 b10",
        "a23 a32 a41 F1",
        "b11",
    )
    run(
        lines,
        "a33 a42 F2 b12",
        "b20 a43 F3 b13",
        "b21 b30",
    )
    run(
        lines,
        "O0 O1 b22 b31",
        "b40 N0 b23 b32",
        "b41 N1 b33 b42",
        "N2 b43 N3",
    )
    send = jnp.stack(enter(sends)).reshape(seqs, loc, kv, wide).transpose(0, 2, 1, 3).reshape(seqs * kv, loc, wide)
    grad = lax.all_to_all(send, "blk", 0, 0, tiled=True)
    send, keep = ffn_grads(*enter(core, gates, ups, hiddens, g_down, norms), blocks)
    leave(keep)
    ffn_sum = Scatter(steps, place, send, keep)
    run(lines, "c10 c11 c20")
    grads = leave(attend_back(at, rec, enter(grad), full, lse, all_cosine, all_sine, group))
    grads = lax.all_to_all(grads, "blk", 0, 0, tiled=True)
    ffn_sum.one_go()

    grads = enter(grads)
    parts = input_grads(grads, x, w_query, w_key, w_value, [g[None, :] for g in gains], 2)
    ins = Line(steps, middle, parts)
    leave(ins.parts[0])
    lines["d"] = ins
    run(lines, "d10 d11 c21")
    ffn_sum.two()
    ffn_sum.two_go()
    send, keep = attn_grads(*enter(core, grads, mixed, normed, g_attns), kv, blocks)
    leave(keep)
    attn_sum = Scatter(steps, place, send, keep)
    run(lines, "c30 c31 d20")
    attn_sum.one_go()
    run(lines, "c50 d21")
    attn_sum.two()
    ffn_sum.three()
    run(lines, "d30")
    ffn_sum.three_go()
    attn_sum.two_go()
    run(lines, "c51 d31")
    mid = middle.astype(jnp.int32)[None]
    block_out = leave(block_output(mid, x, attn.done, enter(outs.total), outs.third))
    attn_sum.three()
    attn_sum.three_go()
    run(lines, "d40")
    extra = ins.done[0][2 * loc:2 * loc + 4].astype(F32)
    both = (extra[0::2] + extra[1::2]).reshape(2, 8, width // 8)
    both = leave(both + lax.ppermute(both, "blk", partner(1)))
    others = [lax.ppermute(enter(both), "blk", partner(bit)) for bit in (2, 4, 6)]
    d_w_gate, d_w_up, d_w_down = ffn_sum.four((units, units, units))
    run(lines, "d51")
    d_hidden_in = finish(
        mid,
        x,
        attn_gain[None, :],
        ins.total,
        ins.third,
        d_resids,
    )
    leave(d_hidden_in)
    d_w_query, d_w_key, d_w_value, d_w_out = attn_sum.four((kv * wide, kv * HEAD_DIM, kv * HEAD_DIM, kv * wide))
    others = enter(others)
    both = both + others[0] + others[1] + others[2]
    both = lax.dynamic_index_in_dim(both, me, 1, keepdims=False)
    return (
        block_out,
        d_hidden_in,
        both[0],
        d_w_query,
        d_w_key,
        d_w_value,
        d_w_out,
        both[1],
        d_w_gate,
        d_w_up,
        d_w_down,
    )


def per_device(*args):
    seqs = args[0].shape[1]
    kv_heads = args[6].shape[1] // HEAD_DIM
    fits = lax.axis_size("blk") == 8 and lax.axis_size("tp") == 4 and seqs * kv_heads == 8
    return (fast if fits else general)(*args)


def solution(mesh):
    return jax.shard_map(
        per_device,
        mesh=mesh,
        in_specs=(
            P("blk", None, None),
            P(),
            P(),
            P(),
            P(),
            P(None, "tp"),
            P(None, "tp"),
            P(None, "tp"),
            P("tp", None),
            P(),
            P(None, "tp"),
            P(None, "tp"),
            P("tp", None),
            P("blk", None, None),
        ),
        out_specs=(
            P("blk", None, None),
            P("blk", None, None),
            P("blk"),
            P("blk", "tp"),
            P("blk", "tp"),
            P("blk", "tp"),
            P("tp", "blk"),
            P("blk"),
            P("blk", "tp"),
            P("blk", "tp"),
            P("tp", "blk"),
        ),
        check_vma=False,
    )
```

```python
import functools
import math

import jax
import jax.numpy as jnp
from jax import lax
from jax.experimental import pallas as pl
from jax.experimental.pallas import tpu as pltpu
from jax.sharding import PartitionSpec as P

HEAD_DIM = 128
EPS = 1e-05
THETA = 10000.0
NEG = -1e30
F32 = jnp.float32
BF16 = jnp.bfloat16
MIB = 1024 * 1024


def dot(left, right):
    return lax.dot_general(left, right, (((1,), (0,)), ((), ())), preferred_element_type=F32)


def dot_rt(left, right):
    return lax.dot_general(left, right, (((1,), (1,)), ((), ())), preferred_element_type=F32)


def dot_lt(left, right):
    return lax.dot_general(left, right, (((0,), (0,)), ((), ())), preferred_element_type=F32)


def params(limit):
    return pltpu.CompilerParams(vmem_limit_bytes=limit * MIB)


def cost():
    return pl.CostEstimate(flops=10**9, bytes_accessed=10**6, transcendentals=0)


SMEM = pl.BlockSpec(memory_space=pltpu.SMEM)
VMEM = pl.BlockSpec(memory_space=pltpu.VMEM)


def project_kernel(heads, kv, x_ref, gain_ref, cos_ref, sin_ref, wq_ref, wk_ref, wv_ref, msg_ref, norm_ref):
    group = heads // kv
    seqs, loc, width = x_ref.shape
    gain = gain_ref[...].astype(F32)
    for s in range(seqs):
        x = x_ref[s].astype(F32)
        inv = lax.rsqrt(jnp.mean(x * x, axis=-1, keepdims=True) + EPS)
        norm_ref[s] = (x * inv * gain).astype(BF16)
    normed = norm_ref[...].reshape(seqs * loc, width)
    cosine, sine = cos_ref[...], sin_ref[...]

    def rot(t):
        return (t * cosine + pltpu.roll(t, HEAD_DIM // 2, 1) * sine).astype(BF16)

    def put(res, h, s, n, slot, turn):
        part = res[s * loc:(s + 1) * loc, h * HEAD_DIM:(h + 1) * HEAD_DIM]
        msg_ref[s * kv + n, :, slot * HEAD_DIM:(slot + 1) * HEAD_DIM] = rot(part) if turn else part.astype(BF16)

    query = dot(normed, wq_ref[...])
    for s in range(seqs):
        for h in range(heads):
            put(query, h, s, h // group, h % group, True)
    keys = dot(normed, wk_ref[...])
    for s in range(seqs):
        for n in range(kv):
            put(keys, n, s, n, group, True)
    vals = dot(normed, wv_ref[...])
    for s in range(seqs):
        for n in range(kv):
            put(vals, n, s, n, group + 1, False)


def project(x, gain, cosine, sine, wq, wk, wv):
    seqs, loc, width = x.shape
    heads, kv = wq.shape[1] // HEAD_DIM, wk.shape[1] // HEAD_DIM
    cols = (heads // kv + 2) * HEAD_DIM
    return pl.pallas_call(
        functools.partial(project_kernel, heads, kv),
        out_shape=(jax.ShapeDtypeStruct((seqs * kv, loc, cols), BF16), jax.ShapeDtypeStruct(x.shape, BF16)),
        in_specs=[VMEM] * 7,
        out_specs=(VMEM, VMEM),
        compiler_params=params(32),
        cost_estimate=cost(),
    )(x, gain, cosine, sine, wq, wk, wv)


def attend_kernel(group, at_ref, rec_ref, out_ref, full_ref, lse_ref, keys, vals):
    blocks, loc, _ = rec_ref.shape
    base = group * HEAD_DIM
    for p in range(blocks):
        i = at_ref[p]
        keys[p * loc:(p + 1) * loc, :] = rec_ref[i, :, base:base + HEAD_DIM]
        vals[p * loc:(p + 1) * loc, :] = rec_ref[i, :, base + HEAD_DIM:base + 2 * HEAD_DIM]
    rows = lax.broadcasted_iota(jnp.int32, (group * loc, loc), 0) % loc
    cols = lax.broadcasted_iota(jnp.int32, (group * loc, loc), 1)
    keep = cols <= rows
    for p in range(blocks):
        i = at_ref[p]
        count = (p + 1) * loc
        query = jnp.concatenate([rec_ref[i, :, g * HEAD_DIM:(g + 1) * HEAD_DIM] for g in range(group)], axis=0)
        scores = dot_rt(query, keys[:count, :]) * (HEAD_DIM ** -0.5)
        last = jnp.where(keep, scores[:, count - loc:], NEG)
        scores = jnp.concatenate([scores[:, :count - loc], last], axis=1) if p else last
        top = jnp.max(scores, axis=-1, keepdims=True)
        weights = jnp.exp(scores - top)
        total = jnp.sum(weights, axis=-1, keepdims=True)
        mixed = dot(weights.astype(BF16), vals[:count, :]) / total
        lse_ref[p] = jnp.broadcast_to(top + jnp.log(total), (group * loc, HEAD_DIM))
        full_ref[p] = mixed
        for g in range(group):
            out_ref[i, :, g * HEAD_DIM:(g + 1) * HEAD_DIM] = mixed[g * loc:(g + 1) * loc].astype(BF16)


def attend(at, rec, group):
    blocks, loc, _ = rec.shape
    total = blocks * loc
    return pl.pallas_call(
        functools.partial(attend_kernel, group),
        out_shape=(
            jax.ShapeDtypeStruct((blocks, loc, group * HEAD_DIM), BF16),
            jax.ShapeDtypeStruct((blocks, group * loc, HEAD_DIM), F32),
            jax.ShapeDtypeStruct((blocks, group * loc, HEAD_DIM), F32),
        ),
        in_specs=[SMEM, VMEM],
        out_specs=(VMEM,) * 3,
        scratch_shapes=[pltpu.VMEM((total, HEAD_DIM), BF16)] * 2,
        compiler_params=params(60),
        cost_estimate=cost(),
    )(at, rec)


def attend_back_kernel(group, at_ref, rec_ref, grad_ref, full_ref, lse_ref, cos_ref, sin_ref, out_ref, keys, vals, d_keys, d_vals):
    blocks, loc, _ = rec_ref.shape
    base = group * HEAD_DIM
    scale = HEAD_DIM ** -0.5
    for p in range(blocks):
        i = at_ref[p]
        keys[p * loc:(p + 1) * loc, :] = rec_ref[i, :, base:base + HEAD_DIM]
        vals[p * loc:(p + 1) * loc, :] = rec_ref[i, :, base + HEAD_DIM:base + 2 * HEAD_DIM]
    rows = lax.broadcasted_iota(jnp.int32, (group * loc, loc), 0) % loc
    cols = lax.broadcasted_iota(jnp.int32, (group * loc, loc), 1)
    keep = cols <= rows

    def unrot(t, cosine, sine):
        return (t * cosine - pltpu.roll(t, HEAD_DIM // 2, 1) * sine).astype(BF16)

    for p in reversed(range(blocks)):
        i = at_ref[p]
        count = (p + 1) * loc
        span = slice(p * loc, count)
        query = jnp.concatenate([rec_ref[i, :, g * HEAD_DIM:(g + 1) * HEAD_DIM] for g in range(group)], axis=0)
        grad = jnp.concatenate([grad_ref[i, :, g * HEAD_DIM:(g + 1) * HEAD_DIM] for g in range(group)], axis=0)
        lse = lse_ref[p][:, :1]
        delta = jnp.sum(grad.astype(F32) * full_ref[p], axis=-1, keepdims=True)
        probs = jnp.exp(dot_rt(query, keys[:count, :]) * scale - lse)
        last = jnp.where(keep, probs[:, count - loc:], 0.0)
        probs = jnp.concatenate([probs[:, :count - loc], last], axis=1) if p else last
        d_probs = dot_rt(grad, vals[:count, :])
        g_scores = (probs * (d_probs - delta) * scale).astype(BF16)
        d_query = dot(g_scores, keys[:count, :])
        dk = dot_lt(g_scores, query)
        dv = dot_lt(probs.astype(BF16), grad)
        if p == blocks - 1:
            d_keys[...] = dk
            d_vals[...] = dv
        else:
            d_keys[:count, :] += dk
            d_vals[:count, :] += dv
        cosine, sine = cos_ref[span, :], sin_ref[span, :]
        for g in range(group):
            out_ref[i, :, g * HEAD_DIM:(g + 1) * HEAD_DIM] = unrot(d_query[g * loc:(g + 1) * loc], cosine, sine)
        out_ref[i, :, base:base + HEAD_DIM] = unrot(d_keys[span, :], cosine, sine)
        out_ref[i, :, base + HEAD_DIM:base + 2 * HEAD_DIM] = d_vals[span, :].astype(BF16)


def attend_back(at, rec, grad, full, lse, cosine, sine, group):
    blocks, loc, cols = rec.shape
    total = blocks * loc
    return pl.pallas_call(
        functools.partial(attend_back_kernel, group),
        out_shape=jax.ShapeDtypeStruct((blocks, loc, cols), BF16),
        in_specs=[SMEM] + [VMEM] * 6,
        out_specs=VMEM,
        scratch_shapes=[pltpu.VMEM((total, HEAD_DIM), BF16)] * 2 + [pltpu.VMEM((total, HEAD_DIM), F32)] * 2,
        compiler_params=params(60),
        cost_estimate=cost(),
    )(at, rec, grad, full, lse, cosine, sine)


def out_kernel(kv, mix_ref, w_ref, cat_ref, *outs):
    cols = mix_ref.shape[2]
    for s, out in enumerate(outs):
        cat_ref[s] = jnp.concatenate([mix_ref[s * kv + n] for n in range(kv)], axis=1)
        out[...] = dot(cat_ref[s], w_ref[...]).astype(BF16)


def out_project(mixed, w_out, seqs):
    units, loc, cols = mixed.shape
    kv = units // seqs
    width = w_out.shape[1]
    res = pl.pallas_call(
        functools.partial(out_kernel, kv),
        out_shape=(jax.ShapeDtypeStruct((seqs, loc, kv * cols), BF16),)
        + (jax.ShapeDtypeStruct((loc, width), BF16),) * seqs,
        in_specs=[VMEM] * 2,
        out_specs=(VMEM,) * (seqs + 1),
        compiler_params=params(24),
        cost_estimate=cost(),
    )(mixed, w_out)
    return res[0], res[1:]


def input_grads_kernel(seqs, kv, groups, back_ref, x_ref, wq_ref, wk_ref, wv_ref, *refs):
    gain_refs, outs, (rows_ref, inv_ref, attn_ref) = refs[:seqs], refs[seqs:seqs + groups], refs[seqs + groups:]
    per = seqs // groups
    loc, width = x_ref.shape[1], x_ref.shape[2]
    group = wq_ref.shape[1] // (kv * HEAD_DIM)
    gather(back_ref, rows_ref, seqs, kv, group)
    at_k = kv * group * HEAD_DIM
    at_v = at_k + kv * HEAD_DIM
    for s in range(seqs):
        x = x_ref[s].astype(F32)
        inv = lax.rsqrt(jnp.mean(x * x, axis=-1, keepdims=True) + EPS)
        inv_ref[s * loc:(s + 1) * loc, :] = jnp.broadcast_to(inv, (loc, HEAD_DIM))
    tile = 512
    for t in range(width // tile):
        span = slice(t * tile, (t + 1) * tile)
        grad = dot_rt(rows_ref[:, :at_k], wq_ref[span, :])
        grad += dot_rt(rows_ref[:, at_k:at_v], wk_ref[span, :])
        grad += dot_rt(rows_ref[:, at_v:], wv_ref[span, :])
        total = 0.0
        for s in range(seqs):
            part = grad[s * loc:(s + 1) * loc]
            at = (s % per) * loc
            outs[s // per][at:at + loc, span] = part.astype(BF16)
            unit = x_ref[s, :, span].astype(F32) * inv_ref[s * loc:(s + 1) * loc, :1]
            total = total + jnp.sum(part * unit, axis=0, keepdims=True)
        attn_ref[:, span] = total
    mlp = sum(ref[...] for ref in gain_refs)
    lines = []
    for gain in (attn_ref[...], mlp):
        high = gain.astype(BF16).astype(F32)
        lines += [high, gain - high]
    row = lax.broadcasted_iota(jnp.int32, (16, width), 0)
    extra = jnp.zeros((16, width), F32)
    for i, gain in enumerate(lines):
        extra = jnp.where(row == i, gain, extra)
    outs[0][per * loc:, :] = extra.astype(BF16)


def gather(back_ref, rows_ref, seqs, kv, group):
    loc = back_ref.shape[1]
    wide = group * HEAD_DIM
    for s in range(seqs):
        for n in range(kv):
            span = slice(s * loc, (s + 1) * loc)
            rows_ref[span, n * wide:(n + 1) * wide] = back_ref[s * kv + n, :, :wide]
            for i in range(2):
                at = kv * wide + (i * kv + n) * HEAD_DIM
                rows_ref[span, at:at + HEAD_DIM] = back_ref[s * kv + n, :, wide + i * HEAD_DIM:wide + (i + 1) * HEAD_DIM]


def input_grads(back, x, wq, wk, wv, gains, groups):
    seqs, loc, width = x.shape
    kv = wk.shape[1] // HEAD_DIM
    cols = wq.shape[1] + 2 * wk.shape[1]
    rows = seqs * loc // groups
    return pl.pallas_call(
        functools.partial(input_grads_kernel, seqs, kv, groups),
        out_shape=(jax.ShapeDtypeStruct((rows + 16, width), BF16),) + (jax.ShapeDtypeStruct((rows, width), BF16),) * (groups - 1),
        in_specs=[VMEM] * (5 + seqs),
        out_specs=(VMEM,) * groups,
        scratch_shapes=[
            pltpu.VMEM((seqs * loc, cols), BF16),
            pltpu.VMEM((seqs * loc, HEAD_DIM), F32),
            pltpu.VMEM((1, width), F32),
        ],
        compiler_params=params(60),
        cost_estimate=cost(),
    )(back, x, wq, wk, wv, *gains)


def shares_call(body, fixed, tall, cols, scratch, core, shares):
    width = tall[0].shape[-1]
    tile = width // shares

    def mine(step, keep, core_ref):
        return 2 * step + jnp.where(keep == 0, 1 - core_ref[0], core_ref[0])

    def tall_spec(a):
        lead = (0,) * (a.ndim - 1)
        return pl.BlockSpec(a.shape[:-1] + (tile,), lambda i, k, c: lead + (mine(i, k, c),))

    out = pl.BlockSpec((1, tile, cols), lambda i, k, c: (i, 0, 0))
    return pl.pallas_call(
        body,
        grid_spec=pltpu.PrefetchScalarGridSpec(
            num_scalar_prefetch=1,
            grid=(shares // 2, 2),
            in_specs=[pl.BlockSpec(a.shape, lambda i, k, c, n=a.ndim: (0,) * n) for a in fixed] + [tall_spec(a) for a in tall],
            out_specs=(out, out),
            scratch_shapes=scratch,
        ),
        out_shape=(jax.ShapeDtypeStruct((shares // 2, tile, cols), BF16),) * 2,
        compiler_params=params(60),
        cost_estimate=cost(),
    )(core, *fixed, *tall)


def put_share(send_ref, keep_ref, pieces):
    def store(ref):
        at = 0
        for piece in pieces:
            ref[0, :, at:at + piece.shape[1]] = piece.astype(BF16)
            at += piece.shape[1]

    @pl.when(pl.program_id(1) == 0)
    def _():
        store(send_ref)

    @pl.when(pl.program_id(1) == 1)
    def _():
        store(keep_ref)


def attn_grads_kernel(seqs, kv, group, core_ref, back_ref, mix_ref, norm_ref, *refs):
    grad_refs, (send_ref, keep_ref, rows_ref) = refs[:seqs], refs[seqs:]

    @pl.when((pl.program_id(0) == 0) & (pl.program_id(1) == 0))
    def _():
        gather(back_ref, rows_ref, seqs, kv, group)

    rows = rows_ref.shape[0]
    left = norm_ref[...].reshape(rows, norm_ref.shape[2])
    grad = jnp.concatenate([ref[...] for ref in grad_refs], axis=0)
    mixed = mix_ref[...].reshape(rows, mix_ref.shape[2])
    put_share(send_ref, keep_ref, [dot_lt(left, rows_ref[...]), dot_lt(grad, mixed)])


def attn_grads(core, back, mixed, normed, g_attns, kv, shares):
    seqs, loc, width = normed.shape
    group = back.shape[2] // HEAD_DIM - 2
    cols = kv * back.shape[2]
    scratch = [pltpu.VMEM((seqs * loc, cols), BF16)]
    body = functools.partial(attn_grads_kernel, seqs, kv, group)
    return shares_call(body, (back, mixed), (normed,) + tuple(g_attns), cols + mixed.shape[2], scratch, core, shares)


def ffn_grads_kernel(seqs, count, core_ref, *refs):
    rights, lefts = refs[:count * seqs], refs[count * seqs:-3]
    send_ref, keep_ref, right_ref = refs[-3:]
    lefts = [ref for ref in lefts if len(ref.shape) == 2 and ref.shape[1] < right_ref.shape[2]]

    @pl.when((pl.program_id(0) == 0) & (pl.program_id(1) == 0))
    def _():
        loc = rights[0].shape[0]
        for i in range(count):
            for s in range(seqs):
                right_ref[i, s * loc:(s + 1) * loc, :] = rights[i * seqs + s][...]

    left = jnp.concatenate([ref[...] for ref in lefts], axis=0)
    put_share(send_ref, keep_ref, [dot_lt(left, right_ref[i]) for i in range(count)])


def ffn_grads(core, rights, lefts, before, total, shares):
    seqs, count = len(rights[0]), len(rights)
    loc, units = rights[0][0].shape
    width = lefts[0].shape[1]
    tile = width // shares
    start = total - count if before else 0
    fixed = sum((tuple(r) for r in rights), ())
    left = [pl.BlockSpec((a.shape[0], tile), lambda i, k, c: (0, 2 * i + jnp.where(k == 0, 1 - c[0], c[0]))) for a in lefts]
    out = pl.BlockSpec((1, tile, count * units), lambda i, k, c: (i, 0, start // count))
    args = fixed + tuple(lefts) + tuple(before)
    return pl.pallas_call(
        functools.partial(ffn_grads_kernel, seqs, count),
        grid_spec=pltpu.PrefetchScalarGridSpec(
            num_scalar_prefetch=1,
            grid=(shares // 2, 2),
            in_specs=[pl.BlockSpec((loc, units), lambda i, k, c: (0, 0))] * len(fixed)
            + left
            + [pl.BlockSpec(memory_space=pl.ANY)] * len(before),
            out_specs=(out, out),
            scratch_shapes=[pltpu.VMEM((count, seqs * loc, units), BF16)],
        ),
        out_shape=(jax.ShapeDtypeStruct((shares // 2, tile, total * units), BF16),) * 2,
        input_output_aliases={len(args) - 1: 0, len(args): 1} if before else {},
        compiler_params=params(60),
        cost_estimate=cost(),
    )(core, *args)


def fold_two_kernel(place_ref, *refs):
    keeps, gots, outs = refs[:4], refs[4:8], refs[8:]
    for keep, got, out in zip(keeps, gots, outs):
        out[0] = (keep[0, 0].astype(F32) + got[0, 0].astype(F32)).astype(BF16)


def fold_two(place, keep, got):
    _, rows, cols = keep.shape
    half = rows // 2
    keep, got = keep.reshape(2, 2, rows, cols), got.reshape(2, 2, rows, cols)
    tile = half // 2
    ins = []
    for own in (0, 1):
        ins.append(pl.BlockSpec((1, 1, tile, cols), lambda i, j, p, own=own: (i, jnp.where(own == 1, p[0], 1 - p[0]), j, 0)))
    for own in (0, 1):
        ins.append(pl.BlockSpec((1, 1, tile, cols), lambda i, j, p, own=own: (jnp.where(own == 1, p[1], 1 - p[1]), i, j + 2, 0)))
    return pl.pallas_call(
        fold_two_kernel,
        grid_spec=pltpu.PrefetchScalarGridSpec(
            num_scalar_prefetch=1,
            grid=(2, 2),
            in_specs=ins + ins,
            out_specs=(pl.BlockSpec((1, tile, cols), lambda i, j, p: (i, j, 0)),) * 4,
        ),
        out_shape=(jax.ShapeDtypeStruct((2, half, cols), BF16),) * 4,
        compiler_params=params(40),
        cost_estimate=cost(),
    )(place, keep, keep, keep, keep, got, got, got, got)


def fold_three(place, upper, upper_got, lower, lower_got):
    _, half, cols = upper.shape
    tile = half // 2
    ins = []
    for axis in (1, 0):
        for own in (0, 1):
            ins.append(pl.BlockSpec((1, 1, tile, cols), lambda j, p, own=own, axis=axis: (0, jnp.where(own == 1, p[axis], 1 - p[axis]), j, 0)))
    flat = pl.BlockSpec((1, tile, cols), lambda j, p: (0, j, 0))
    u, ug, l, lg = (a[None] for a in (upper, upper_got, lower, lower_got))
    res = pl.pallas_call(
        fold_two_kernel,
        grid_spec=pltpu.PrefetchScalarGridSpec(
            num_scalar_prefetch=1, grid=(2,), in_specs=ins + ins, out_specs=(flat,) * 4
        ),
        out_shape=(jax.ShapeDtypeStruct((1, half, cols), BF16),) * 4,
        compiler_params=params(40),
        cost_estimate=cost(),
    )(place, u, u, l, l, ug, ug, lg, lg)
    return [a[0] for a in res]


def fold_four_kernel(widths, upper, upper_got, lower, lower_got, *outs):
    half = upper.shape[0]
    for at, (one, two) in enumerate(((upper, upper_got), (lower, lower_got))):
        start = 0
        for out, width in zip(outs, widths):
            part = one[:, start:start + width].astype(F32) + two[:, start:start + width].astype(F32)
            if out is outs[-1]:
                out[:, at * half:(at + 1) * half] = part.T
            else:
                out[at * half:(at + 1) * half, :] = part
            start += width


def fold_four(widths, upper, upper_got, lower, lower_got):
    rows = 2 * upper.shape[0]
    shapes = [(rows, w) for w in widths[:-1]] + [(widths[-1], rows)]
    return pl.pallas_call(
        functools.partial(fold_four_kernel, widths),
        out_shape=tuple(jax.ShapeDtypeStruct(shape, F32) for shape in shapes),
        in_specs=[VMEM] * 4,
        out_specs=(VMEM,) * len(widths),
        compiler_params=params(40),
        cost_estimate=cost(),
    )(upper, upper_got, lower, lower_got)


def finish_kernel(seqs, mid_ref, x_ref, gain_ref, *refs):
    inner, ends, resids, out_ref = refs[:seqs], refs[seqs:2 * seqs], refs[2 * seqs:3 * seqs], refs[3 * seqs]
    gain = gain_ref[...].astype(F32)
    for s in range(seqs):
        grad = jnp.where(mid_ref[0] == 1, inner[s][...].astype(F32), ends[s][...].astype(F32))
        x = x_ref[s].astype(F32)
        inv = lax.rsqrt(jnp.mean(x * x, axis=-1, keepdims=True) + EPS)
        unit = x * inv
        scaled = grad * gain
        back = inv * (scaled - unit * jnp.mean(scaled * unit, axis=-1, keepdims=True))
        out_ref[:, s, :] = resids[s][...] + back


def by_seq(group, seqs, loc, tile):
    per = seqs // len(group)
    return [
        (group[s // per], pl.BlockSpec((tile, group[0].shape[1]), lambda i, at=(s % per) * (loc // tile): (i + at, 0)))
        for s in range(seqs)
    ]


def finish(mid, x, gain, inner, ends, resids):
    seqs, loc, width = x.shape
    tile = 32
    parts = by_seq(inner, seqs, loc, tile) + by_seq(ends, seqs, loc, tile) + by_seq(resids, seqs, loc, tile)
    return pl.pallas_call(
        functools.partial(finish_kernel, seqs),
        grid=(loc // tile,),
        out_shape=jax.ShapeDtypeStruct((loc, seqs, width), F32),
        in_specs=[SMEM, pl.BlockSpec((seqs, tile, width), lambda i: (0, i, 0)), pl.BlockSpec((1, width), lambda i: (0, 0))]
        + [spec for _, spec in parts],
        out_specs=pl.BlockSpec((tile, seqs, width), lambda i: (i, 0, 0)),
        compiler_params=params(60),
        cost_estimate=cost(),
    )(mid, x, gain, *(a for a, _ in parts))


def output_kernel(seqs, mid_ref, x_ref, *refs):
    attn, inner, ends, out_ref, wide = refs[:seqs], refs[seqs:2 * seqs], refs[2 * seqs:3 * seqs], refs[3 * seqs], refs[3 * seqs + 1]
    for s in range(seqs):
        down = jnp.where(mid_ref[0] == 1, inner[s][...].astype(F32), ends[s][...].astype(F32))
        wide[:, s, :] = x_ref[s].astype(F32) + attn[s][...].astype(F32) + down
    out_ref[...] = wide[...].astype(BF16)


def block_output(mid, x, attn, inner, ends):
    seqs, loc, width = x.shape
    tile = 32
    parts = by_seq(attn, seqs, loc, tile) + by_seq(inner, seqs, loc, tile) + by_seq(ends, seqs, loc, tile)
    return pl.pallas_call(
        functools.partial(output_kernel, seqs),
        grid=(loc // tile,),
        out_shape=jax.ShapeDtypeStruct((loc, seqs, width), BF16),
        in_specs=[SMEM, pl.BlockSpec((seqs, tile, width), lambda i: (0, i, 0))] + [spec for _, spec in parts],
        out_specs=pl.BlockSpec((tile, seqs, width), lambda i: (i, 0, 0)),
        scratch_shapes=[pltpu.VMEM((tile, seqs, width), F32)],
        compiler_params=params(32),
        cost_estimate=cost(),
    )(mid, x, *(a for a, _ in parts))


def add_kernel(left, right, out):
    out[...] = (left[...].astype(F32) + right[...].astype(F32)).astype(BF16)


def add(left, right):
    return pl.pallas_call(
        add_kernel,
        out_shape=jax.ShapeDtypeStruct(left.shape, BF16),
        in_specs=[VMEM, VMEM],
        out_specs=VMEM,
        compiler_params=params(16),
        cost_estimate=cost(),
    )(left, right)


def rope_tables(positions, head_dim):
    half = head_dim // 2
    freq = jnp.exp(jnp.arange(half, dtype=jnp.float32) * (-2.0 * math.log(THETA) / head_dim))
    angles = positions.astype(jnp.float32)[:, None] * freq[None, :]
    return (jnp.cos(angles), jnp.sin(angles))


def rotate(values, cosine, sine):
    half = values.shape[-1] // 2
    first = values[..., :half]
    second = values[..., half:]
    cosine = cosine[:, None, None, :]
    sine = sine[:, None, None, :]
    return jnp.concatenate(
        [first * cosine - second * sine, second * cosine + first * sine], axis=-1
    )


def inverse_rms(values):
    return lax.rsqrt(jnp.mean(values * values, axis=-1, keepdims=True) + EPS)


def norm_back(values, inverse, gain, grad):
    unit = values * inverse
    scaled = grad * gain
    back = inverse * (scaled - unit * jnp.mean(scaled * unit, axis=-1, keepdims=True))
    return (back, jnp.sum(grad * unit, axis=(0, 1)))


def matmul(values, weight):
    return jnp.einsum("lsd,de->lse", values, weight, preferred_element_type=jnp.float32)


def matmul_back(values, weight):
    return jnp.einsum("lse,de->lsd", values, weight, preferred_element_type=jnp.float32)


def weight_grad(left, right):
    return jnp.einsum("lsd,lse->de", left, right, preferred_element_type=jnp.float32)


def general(
    hidden_in,
    block_order,
    seq_labels,
    exit_scales,
    attn_gain,
    w_query,
    w_key,
    w_value,
    w_out,
    mlp_gain,
    w_gate,
    w_up,
    w_down,
    d_out,
):
    f32 = jnp.float32
    bf16 = jnp.bfloat16
    loc, seqs, width = hidden_in.shape
    head_dim = HEAD_DIM
    q_heads = w_query.shape[1] // head_dim
    kv_heads = w_key.shape[1] // head_dim
    group = q_heads // kv_heads
    scale = head_dim ** (-0.5)
    blocks_all = block_order.shape[0]
    total_rows = loc * lax.axis_size("blk")
    key_rows = math.gcd(512, total_rows)
    block_count = total_rows // key_rows
    kv_width = 2 * kv_heads * head_dim
    positions = block_order[lax.axis_index("blk")] * loc + jnp.arange(loc, dtype=jnp.int32)
    cosine, sine = rope_tables(positions, head_dim)

    def key_positions(start, count):
        index = start + jnp.arange(count, dtype=jnp.int32)
        owner = index // loc
        table = jnp.sum(
            jnp.where(
                owner[:, None] == jnp.arange(blocks_all, dtype=jnp.int32)[None, :],
                block_order[None, :],
                0,
            ),
            axis=1,
        )
        return table * loc + index % loc

    xin = hidden_in.astype(f32)
    inv_a = inverse_rms(xin)
    gain_a = attn_gain.astype(f32)
    normed = (xin * inv_a * gain_a).astype(bf16)
    query_bf = rotate(
        matmul(normed, w_query).reshape(loc, seqs, q_heads, head_dim), cosine, sine
    ).astype(bf16)
    keys_bf = (
        rotate(matmul(normed, w_key).reshape(loc, seqs, kv_heads, head_dim), cosine, sine)
        .astype(bf16)
        .reshape(loc, seqs, kv_heads * head_dim)
    )
    vals_bf = matmul(normed, w_value).astype(bf16)
    query_g = query_bf.reshape(loc, seqs, kv_heads, group, head_dim)
    starts = jnp.arange(block_count, dtype=jnp.int32) * key_rows
    top = jnp.full((seqs, kv_heads, group, loc), NEG, f32)
    key_part = lax.all_gather(keys_bf, "blk", axis=0, tiled=True)
    val_part = lax.all_gather(vals_bf, "blk", axis=0, tiled=True)
    count = key_part.shape[0]
    kk = key_part.reshape(count, seqs, kv_heads, head_dim)
    vv = val_part.reshape(count, seqs, kv_heads, head_dim)
    mask = key_positions(jnp.int32(0), count)[None, :] <= positions[:, None]
    raw = jnp.einsum("lsngd,msnd->snglm", query_g, kk, preferred_element_type=f32)
    scores = jnp.where(mask, raw * scale, NEG)
    new_top = jnp.maximum(top, jnp.max(scores, axis=-1))
    weights = jnp.where(mask, jnp.exp(scores - new_top[..., None]), 0.0)
    total = jnp.sum(weights, axis=-1)
    acc = jnp.einsum("snglm,msnd->sngld", weights.astype(bf16), vv, preferred_element_type=f32)
    top, total, acc = (new_top, total, acc)
    lse = top + jnp.log(total)
    mixed_raw = acc / total[..., None]
    mixed_bf = (
        mixed_raw.transpose(3, 0, 1, 2, 4).reshape(loc, seqs, q_heads * head_dim).astype(bf16)
    )
    resid = xin + lax.psum(matmul(mixed_bf, w_out).astype(jnp.bfloat16), "tp").astype(jnp.float32)
    inv_m = inverse_rms(resid)
    gain_m = mlp_gain.astype(f32)
    normed_m = (resid * inv_m * gain_m).astype(bf16)
    gate = matmul(normed_m, w_gate)
    up = matmul(normed_m, w_up)
    sig = jax.nn.sigmoid(gate)
    silu = gate * sig
    hidden = (silu * up).astype(bf16)
    output = resid + lax.psum(matmul(hidden, w_down).astype(jnp.bfloat16), "tp").astype(jnp.float32)
    block_out = output.astype(bf16)
    scale_rows = jnp.where(seq_labels == 1, exit_scales[1], exit_scales[0])
    cot = d_out.astype(f32) * scale_rows[None, :, None]
    g_down = cot.astype(bf16)
    d_w_down = weight_grad(hidden, g_down)
    d_hidden = matmul_back(g_down, w_down)
    g_up = (d_hidden * silu).astype(bf16)
    g_gate = (d_hidden * up * (sig * (1.0 + gate * (1.0 - sig)))).astype(bf16)
    d_w_gate = weight_grad(normed_m, g_gate)
    d_w_up = weight_grad(normed_m, g_up)
    d_nm = lax.psum(
        (matmul_back(g_gate, w_gate) + matmul_back(g_up, w_up)).astype(jnp.bfloat16), "tp"
    ).astype(jnp.float32)
    d_resid_norm, d_mlp_gain = norm_back(resid, inv_m, gain_m, d_nm)
    d_resid = cot + d_resid_norm
    g_attn = d_resid.astype(bf16)
    d_w_out = weight_grad(mixed_bf, g_attn)
    g_mixed = matmul_back(g_attn, w_out).astype(bf16)
    g_mixed_g = g_mixed.reshape(loc, seqs, kv_heads, group, head_dim)
    delta = jnp.sum(g_mixed_g.astype(f32).transpose(1, 2, 3, 0, 4) * mixed_raw, axis=-1)
    whole_keys, whole_vals = (
        lax.all_gather(keys_bf, "blk", axis=0, tiled=True),
        lax.all_gather(vals_bf, "blk", axis=0, tiled=True),
    )

    def probe(kk, vv, start, count):
        mask = key_positions(start, count)[None, :] <= positions[:, None]
        raw = jnp.einsum("lsngd,msnd->snglm", query_g, kk, preferred_element_type=f32)
        probs = jnp.where(mask, jnp.exp(raw * scale - lse[..., None]), 0.0)
        d_probs = jnp.einsum("lsngd,msnd->snglm", g_mixed_g, vv, preferred_element_type=f32)
        g_scores = (probs * (d_probs - delta[..., None]) * scale).astype(bf16)
        return (g_scores, probs)

    def kv_pair(g_scores, probs, count):
        d_keys = jnp.einsum("snglm,lsngd->msnd", g_scores, query_g, preferred_element_type=f32)
        d_vals = jnp.einsum(
            "snglm,lsngd->msnd", probs.astype(bf16), g_mixed_g, preferred_element_type=f32
        )
        return jnp.concatenate([d_keys, d_vals], axis=2).reshape(count, seqs, kv_width)

    scan_items = (
        whole_keys.reshape(block_count, key_rows, seqs, -1),
        whole_vals.reshape(block_count, key_rows, seqs, -1),
        starts,
    )
    zero_query = jnp.zeros((loc, seqs, kv_heads, group, head_dim), f32)

    def back_step(d_query, item):
        key_part, val_part, start = item
        kk = key_part.reshape(key_rows, seqs, kv_heads, head_dim)
        vv = val_part.reshape(key_rows, seqs, kv_heads, head_dim)
        g_scores, probs = probe(kk, vv, start, key_rows)
        d_query = d_query + jnp.einsum(
            "snglm,msnd->lsngd", g_scores, kk, preferred_element_type=f32
        )
        return (d_query, kv_pair(g_scores, probs, key_rows))

    d_query, kv_terms = lax.scan(back_step, zero_query, scan_items)
    kv_local = lax.psum_scatter(
        kv_terms.reshape(total_rows, seqs, kv_width).astype(jnp.bfloat16),
        "blk",
        scatter_dimension=0,
        tiled=True,
    ).astype(jnp.float32)
    kv_local = kv_local.reshape(loc, seqs, 2, kv_heads, head_dim)
    g_q = (
        rotate(d_query.reshape(loc, seqs, q_heads, head_dim), cosine, -sine)
        .astype(bf16)
        .reshape(loc, seqs, q_heads * head_dim)
    )
    g_k = (
        rotate(kv_local[:, :, 0], cosine, -sine)
        .astype(bf16)
        .reshape(loc, seqs, kv_heads * head_dim)
    )
    g_v = kv_local[:, :, 1].astype(bf16).reshape(loc, seqs, kv_heads * head_dim)
    d_w_query = weight_grad(normed, g_q)
    d_w_key = weight_grad(normed, g_k)
    d_w_value = weight_grad(normed, g_v)
    d_n = lax.psum(
        (matmul_back(g_q, w_query) + matmul_back(g_k, w_key) + matmul_back(g_v, w_value)).astype(
            jnp.bfloat16
        ),
        "tp",
    ).astype(jnp.float32)
    d_in_norm, d_attn_gain = norm_back(xin, inv_a, gain_a, d_n)
    d_hidden_in = d_resid + d_in_norm
    d_attn_gain, d_w_query, d_w_key, d_w_value, d_w_out, d_mlp_gain, d_w_gate, d_w_up, d_w_down = (
        lax.psum_scatter(
            d_attn_gain.astype(jnp.bfloat16), "blk", scatter_dimension=0, tiled=True
        ).astype(jnp.float32),
        lax.psum_scatter(
            d_w_query.astype(jnp.bfloat16), "blk", scatter_dimension=0, tiled=True
        ).astype(jnp.float32),
        lax.psum_scatter(
            d_w_key.astype(jnp.bfloat16), "blk", scatter_dimension=0, tiled=True
        ).astype(jnp.float32),
        lax.psum_scatter(
            d_w_value.astype(jnp.bfloat16), "blk", scatter_dimension=0, tiled=True
        ).astype(jnp.float32),
        lax.psum_scatter(
            d_w_out.astype(jnp.bfloat16), "blk", scatter_dimension=1, tiled=True
        ).astype(jnp.float32),
        lax.psum_scatter(
            d_mlp_gain.astype(jnp.bfloat16), "blk", scatter_dimension=0, tiled=True
        ).astype(jnp.float32),
        lax.psum_scatter(
            d_w_gate.astype(jnp.bfloat16), "blk", scatter_dimension=0, tiled=True
        ).astype(jnp.float32),
        lax.psum_scatter(
            d_w_up.astype(jnp.bfloat16), "blk", scatter_dimension=0, tiled=True
        ).astype(jnp.float32),
        lax.psum_scatter(
            d_w_down.astype(jnp.bfloat16), "blk", scatter_dimension=1, tiled=True
        ).astype(jnp.float32),
    )
    return (
        block_out,
        d_hidden_in,
        d_attn_gain,
        d_w_query,
        d_w_key,
        d_w_value,
        d_w_out,
        d_mlp_gain,
        d_w_gate,
        d_w_up,
        d_w_down,
    )


class Steps:
    def __init__(self):
        self.last = None

    def enter(self, *values):
        if self.last is not None:
            values, _ = lax.optimization_barrier((values, self.last))
        return values if len(values) > 1 else values[0]

    def leave(self, value):
        self.last = value
        return value


class Line:
    def __init__(self, steps, middle, parts):
        self.steps, self.middle, self.parts = steps, middle, list(parts)
        count = len(self.parts)
        self.first, self.half, self.second, self.total, self.third, self.done = ([None] * count for _ in range(6))

    def one(self, c):
        self.first[c] = lax.ppermute(self.parts[c], "tp", [(0, 1), (3, 2)])

    def two(self, c):
        part, got = self.steps.enter(self.parts[c], self.first[c])
        self.half[c] = self.steps.leave(add(part, got))
        self.second[c] = lax.ppermute(self.half[c], "tp", [(1, 2), (2, 1)])

    def three(self, c):
        half, got = self.steps.enter(self.half[c], self.second[c])
        self.total[c] = self.steps.leave(add(half, got))
        self.third[c] = lax.ppermute(self.total[c], "tp", [(1, 0), (2, 3)])

    def four(self, c):
        total, got = self.steps.enter(self.total[c], self.third[c])
        self.done[c] = self.steps.leave(jnp.where(self.middle, total, got))

    def five(self, c):
        self.third[c] = self.steps.leave(self.steps.enter(self.third[c]))


def partner(bit):
    return [(i, i ^ bit) for i in range(8)]


class Scatter:
    def __init__(self, steps, place, send, keep):
        self.steps, self.place, self.send, self.keep = steps, place, send, keep

    def one_go(self):
        self.got = lax.ppermute(self.steps.enter(self.send), "blk", partner(1))

    def two(self):
        keep, got = self.steps.enter(self.keep, self.got)
        self.away, self.upper, self.off, self.lower = fold_two(self.place, keep, got)
        self.steps.leave(self.upper)

    def two_go(self, first=2, second=4):
        away, off = self.steps.enter(self.away, self.off)
        self.upper_got = lax.ppermute(away, "blk", partner(first))
        self.lower_got = lax.ppermute(off, "blk", partner(second))

    def three(self):
        values = self.steps.enter(self.upper, self.upper_got, self.lower, self.lower_got)
        self.away, self.upper, self.off, self.lower = fold_three(self.place, *values)
        self.steps.leave(self.upper)

    def three_go(self):
        self.two_go(4, 2)

    def four(self, widths):
        values = self.steps.enter(self.upper, self.upper_got, self.lower, self.lower_got)
        res = fold_four(widths, *values)
        self.steps.leave(res[0])
        return res


def inverse(values):
    return lax.rsqrt(jnp.mean(values * values, axis=-1, keepdims=True) + EPS)


def tables(positions):
    cosine, sine = rope_tables(positions, HEAD_DIM)
    return jnp.concatenate([cosine, cosine], axis=1), jnp.concatenate([-sine, sine], axis=1)


def fast(
    hidden_in,
    block_order,
    seq_labels,
    exit_scales,
    attn_gain,
    w_query,
    w_key,
    w_value,
    w_out,
    mlp_gain,
    w_gate,
    w_up,
    w_down,
    d_out,
):
    loc, seqs, width = hidden_in.shape
    blocks = block_order.shape[0]
    rows = seqs * loc
    units = w_gate.shape[1]
    kv = w_key.shape[1] // HEAD_DIM
    group = w_query.shape[1] // w_key.shape[1]
    wide = group * HEAD_DIM
    me = lax.axis_index("blk")
    line = lax.axis_index("tp")
    middle = (line == 1) | (line == 2)
    index = jnp.arange(blocks, dtype=jnp.int32)
    at = jnp.sum(jnp.where(block_order[None, :] == index[:, None], index[None, :], 0), axis=1)
    mine = jnp.sum(jnp.where(index == me, block_order, 0)) * loc + jnp.arange(loc, dtype=jnp.int32)
    steps = Steps()
    enter, leave = steps.enter, steps.leave

    x = hidden_in.transpose(1, 0, 2)
    cosine, sine = tables(mine)
    messages, normed = project(x, attn_gain[None, :], cosine, sine, w_query, w_key, w_value)
    leave(messages)
    rec = lax.all_to_all(messages, "blk", 0, 0, tiled=True)
    scales = jnp.where(seq_labels == 1, exit_scales[1], exit_scales[0])
    cot = enter(d_out).transpose(1, 0, 2).astype(F32) * scales[:, None, None]
    g_down = leave(cot.astype(BF16).reshape(rows, width))
    d_hidden = leave(dot_rt(g_down, w_down).astype(BF16))
    mixed, full, lse = attend(at, enter(rec), group)
    leave(mixed)
    mixed = lax.all_to_all(mixed, "blk", 0, 0, tiled=True)
    all_cosine, all_sine = tables(enter(jnp.arange(blocks * loc, dtype=jnp.int32)))
    leave(all_cosine)
    mixed, parts = out_project(enter(mixed), w_out, seqs)
    leave(mixed)

    gain_m = mlp_gain.astype(F32)
    attn = Line(steps, middle, parts)
    back = Line(steps, middle, [None] * seqs)
    norms, hiddens, gates, ups, gains = ([None] * seqs for _ in range(5))

    def feed(s):
        total = attn.done[s]
        resid = x[s].astype(F32) + total.astype(F32)
        unit = resid * inverse(resid)
        norm = (unit * gain_m).astype(BF16)
        gate = dot(norm, w_gate)
        up = dot(norm, w_up)
        sig = jax.nn.sigmoid(gate)
        silu = gate * sig
        grad_h = d_hidden[s * loc:(s + 1) * loc].astype(F32)
        g_up = (grad_h * silu).astype(BF16)
        g_gate = (grad_h * up * (sig * (1.0 + gate * (1.0 - sig)))).astype(BF16)
        grad = dot_rt(g_gate, w_gate) + dot_rt(g_up, w_up)
        gains[s] = jnp.sum(grad * unit, axis=0)
        back.parts[s] = leave(grad.astype(BF16))
        norms[s], gates[s], ups[s] = norm, g_gate, g_up
        hiddens[s] = (silu * up).astype(BF16)

    d_resids, g_attns, sends = ([None] * seqs for _ in range(3))

    def norm_back(s):
        resid = x[s].astype(F32) + attn.done[s].astype(F32)
        inv = inverse(resid)
        unit = resid * inv
        scaled = back.done[s].astype(F32) * gain_m
        d_resids[s] = cot[s] + inv * (scaled - unit * jnp.mean(scaled * unit, axis=-1, keepdims=True))
        g_attns[s] = d_resids[s].astype(BF16)
        sends[s] = leave(dot_rt(g_attns[s], w_out).astype(BF16))

    def run(lines, *texts):
        for word in " ".join(texts).split():
            name, c = word[:-1], int(word[-1])
            if name == "F":
                feed(c)
            elif name == "N":
                norm_back(c)
            elif name == "O":
                hidden = jnp.concatenate(enter(hiddens[2 * c:2 * c + 2]), axis=0)
                outs.parts[c] = leave(dot(hidden, w_down).astype(BF16))
            else:
                obj = lines[name[0]]
                (obj.one, obj.two, obj.three, obj.four, obj.five)[int(name[1]) - 1](c)

    outs = Line(steps, middle, [None] * 2)
    lines = {"a": attn, "b": back, "c": outs}
    core = (me % 2).astype(jnp.int32)[None]
    place = jnp.stack([(me // 2) % 2, me // 4]).astype(jnp.int32)
    run(
        lines,
        "a10 a11 a12 a13",
        "a20 a21 a30 a22",
        "a31 a40 F0 b10",
        "a23 a32 a41 F1",
        "b11",
    )
    run(
        lines,
        "a33 a42 F2 b12",
        "b20 a43 F3 b13",
        "b21 b30",
    )
    run(
        lines,
        "O0 O1 b22 b31",
        "b40 N0 b23 b32",
        "b41 N1 b33 b42",
        "N2 b43 N3",
    )
    send = jnp.stack(enter(sends)).reshape(seqs, loc, kv, wide).transpose(0, 2, 1, 3).reshape(seqs * kv, loc, wide)
    grad = lax.all_to_all(send, "blk", 0, 0, tiled=True)
    made = leave(ffn_grads(core, *enter([gates, ups], norms), (), 3, blocks))
    run(lines, "c10 c11 c20")
    grads = leave(attend_back(at, rec, enter(grad), full, lse, all_cosine, all_sine, group))
    grads = lax.all_to_all(grads, "blk", 0, 0, tiled=True)
    send, keep = ffn_grads(core, *enter([hiddens], [g_down], made), 3, blocks)
    leave(keep)
    ffn_sum = Scatter(steps, place, send, keep)
    run(lines, "c21 c30")

    grads = enter(grads)
    parts = input_grads(grads, x, w_query, w_key, w_value, [g[None, :] for g in gains], 2)
    ins = Line(steps, middle, parts)
    leave(ins.parts[0])
    lines["d"] = ins
    run(lines, "d10 d11")
    ffn_sum.one_go()
    send, keep = attn_grads(*enter(core, grads, mixed, normed, g_attns), kv, blocks)
    leave(keep)
    attn_sum = Scatter(steps, place, send, keep)
    ffn_sum.two()
    ffn_sum.two_go()
    run(lines, "c31 d20")
    attn_sum.one_go()
    run(lines, "c50 d21")
    attn_sum.two()
    ffn_sum.three()
    run(lines, "d30")
    ffn_sum.three_go()
    attn_sum.two_go()
    run(lines, "c51 d31")
    mid = middle.astype(jnp.int32)[None]
    block_out = leave(block_output(mid, x, attn.done, enter(outs.total), outs.third))
    attn_sum.three()
    attn_sum.three_go()
    run(lines, "d40")
    extra = ins.done[0][2 * loc:2 * loc + 4].astype(F32)
    both = (extra[0::2] + extra[1::2]).reshape(2, 8, width // 8)
    both = leave(both + lax.ppermute(both, "blk", partner(1)))
    others = [lax.ppermute(enter(both), "blk", partner(bit)) for bit in (2, 4, 6)]
    d_w_gate, d_w_up, d_w_down = ffn_sum.four((units, units, units))
    run(lines, "d51")
    d_hidden_in = finish(
        mid,
        x,
        attn_gain[None, :],
        ins.total,
        ins.third,
        d_resids,
    )
    leave(d_hidden_in)
    d_w_query, d_w_key, d_w_value, d_w_out = attn_sum.four((kv * wide, kv * HEAD_DIM, kv * HEAD_DIM, kv * wide))
    others = enter(others)
    both = both + others[0] + others[1] + others[2]
    both = lax.dynamic_index_in_dim(both, me, 1, keepdims=False)
    return (
        block_out,
        d_hidden_in,
        both[0],
        d_w_query,
        d_w_key,
        d_w_value,
        d_w_out,
        both[1],
        d_w_gate,
        d_w_up,
        d_w_down,
    )


def per_device(*args):
    seqs = args[0].shape[1]
    kv_heads = args[6].shape[1] // HEAD_DIM
    fits = lax.axis_size("blk") == 8 and lax.axis_size("tp") == 4 and seqs * kv_heads == 8
    return (fast if fits else general)(*args)


def solution(mesh):
    return jax.shard_map(
        per_device,
        mesh=mesh,
        in_specs=(
            P("blk", None, None),
            P(),
            P(),
            P(),
            P(),
            P(None, "tp"),
            P(None, "tp"),
            P(None, "tp"),
            P("tp", None),
            P(),
            P(None, "tp"),
            P(None, "tp"),
            P("tp", None),
            P("blk", None, None),
        ),
        out_specs=(
            P("blk", None, None),
            P("blk", None, None),
            P("blk"),
            P("blk", "tp"),
            P("blk", "tp"),
            P("blk", "tp"),
            P("tp", "blk"),
            P("blk"),
            P("blk", "tp"),
            P("blk", "tp"),
            P("tp", "blk"),
        ),
        check_vma=False,
    )
```

```python
import functools
import math

import jax
import jax.numpy as jnp
from jax import lax
from jax.experimental import pallas as pl
from jax.experimental.pallas import tpu as pltpu
from jax.sharding import PartitionSpec as P

HEAD_DIM = 128
EPS = 1e-05
THETA = 10000.0
NEG = -1e30
F32 = jnp.float32
BF16 = jnp.bfloat16
MIB = 1024 * 1024


def dot(left, right):
    return lax.dot_general(left, right, (((1,), (0,)), ((), ())), preferred_element_type=F32)


def dot_rt(left, right):
    return lax.dot_general(left, right, (((1,), (1,)), ((), ())), preferred_element_type=F32)


def dot_lt(left, right):
    return lax.dot_general(left, right, (((0,), (0,)), ((), ())), preferred_element_type=F32)


def params(limit):
    return pltpu.CompilerParams(vmem_limit_bytes=limit * MIB)


def cost():
    return pl.CostEstimate(flops=10**9, bytes_accessed=10**6, transcendentals=0)


SMEM = pl.BlockSpec(memory_space=pltpu.SMEM)
VMEM = pl.BlockSpec(memory_space=pltpu.VMEM)


def project_kernel(heads, kv, x_ref, gain_ref, cos_ref, sin_ref, wq_ref, wk_ref, wv_ref, msg_ref, norm_ref):
    group = heads // kv
    seqs, loc, width = x_ref.shape
    gain = gain_ref[...].astype(F32)
    for s in range(seqs):
        x = x_ref[s].astype(F32)
        inv = lax.rsqrt(jnp.mean(x * x, axis=-1, keepdims=True) + EPS)
        norm_ref[s] = (x * inv * gain).astype(BF16)
    normed = norm_ref[...].reshape(seqs * loc, width)
    cosine, sine = cos_ref[...], sin_ref[...]

    def rot(t):
        return (t * cosine + pltpu.roll(t, HEAD_DIM // 2, 1) * sine).astype(BF16)

    def put(res, h, s, n, slot, turn):
        part = res[s * loc:(s + 1) * loc, h * HEAD_DIM:(h + 1) * HEAD_DIM]
        msg_ref[s * kv + n, :, slot * HEAD_DIM:(slot + 1) * HEAD_DIM] = rot(part) if turn else part.astype(BF16)

    query = dot(normed, wq_ref[...])
    for s in range(seqs):
        for h in range(heads):
            put(query, h, s, h // group, h % group, True)
    keys = dot(normed, wk_ref[...])
    for s in range(seqs):
        for n in range(kv):
            put(keys, n, s, n, group, True)
    vals = dot(normed, wv_ref[...])
    for s in range(seqs):
        for n in range(kv):
            put(vals, n, s, n, group + 1, False)


def project(x, gain, cosine, sine, wq, wk, wv):
    seqs, loc, width = x.shape
    heads, kv = wq.shape[1] // HEAD_DIM, wk.shape[1] // HEAD_DIM
    cols = (heads // kv + 2) * HEAD_DIM
    return pl.pallas_call(
        functools.partial(project_kernel, heads, kv),
        out_shape=(jax.ShapeDtypeStruct((seqs * kv, loc, cols), BF16), jax.ShapeDtypeStruct(x.shape, BF16)),
        in_specs=[VMEM] * 7,
        out_specs=(VMEM, VMEM),
        compiler_params=params(32),
        cost_estimate=cost(),
    )(x, gain, cosine, sine, wq, wk, wv)


def attend_kernel(group, at_ref, rec_ref, out_ref, full_ref, lse_ref, keys, vals):
    blocks, loc, _ = rec_ref.shape
    base = group * HEAD_DIM
    for p in range(blocks):
        i = at_ref[p]
        keys[p * loc:(p + 1) * loc, :] = rec_ref[i, :, base:base + HEAD_DIM]
        vals[p * loc:(p + 1) * loc, :] = rec_ref[i, :, base + HEAD_DIM:base + 2 * HEAD_DIM]
    rows = lax.broadcasted_iota(jnp.int32, (group * loc, loc), 0) % loc
    cols = lax.broadcasted_iota(jnp.int32, (group * loc, loc), 1)
    keep = cols <= rows
    for p in range(blocks):
        i = at_ref[p]
        count = (p + 1) * loc
        query = jnp.concatenate([rec_ref[i, :, g * HEAD_DIM:(g + 1) * HEAD_DIM] for g in range(group)], axis=0)
        scores = dot_rt(query, keys[:count, :]) * (HEAD_DIM ** -0.5)
        last = jnp.where(keep, scores[:, count - loc:], NEG)
        scores = jnp.concatenate([scores[:, :count - loc], last], axis=1) if p else last
        top = jnp.max(scores, axis=-1, keepdims=True)
        weights = jnp.exp(scores - top)
        total = jnp.sum(weights, axis=-1, keepdims=True)
        mixed = dot(weights.astype(BF16), vals[:count, :]) / total
        lse_ref[p] = jnp.broadcast_to(top + jnp.log(total), (group * loc, HEAD_DIM))
        full_ref[p] = mixed
        for g in range(group):
            out_ref[i, :, g * HEAD_DIM:(g + 1) * HEAD_DIM] = mixed[g * loc:(g + 1) * loc].astype(BF16)


def attend(at, rec, group):
    blocks, loc, _ = rec.shape
    total = blocks * loc
    return pl.pallas_call(
        functools.partial(attend_kernel, group),
        out_shape=(
            jax.ShapeDtypeStruct((blocks, loc, group * HEAD_DIM), BF16),
            jax.ShapeDtypeStruct((blocks, group * loc, HEAD_DIM), F32),
            jax.ShapeDtypeStruct((blocks, group * loc, HEAD_DIM), F32),
        ),
        in_specs=[SMEM, VMEM],
        out_specs=(VMEM,) * 3,
        scratch_shapes=[pltpu.VMEM((total, HEAD_DIM), BF16)] * 2,
        compiler_params=params(60),
        cost_estimate=cost(),
    )(at, rec)


def attend_back_kernel(group, at_ref, rec_ref, grad_ref, full_ref, lse_ref, cos_ref, sin_ref, out_ref, keys, vals, d_keys, d_vals):
    blocks, loc, _ = rec_ref.shape
    base = group * HEAD_DIM
    scale = HEAD_DIM ** -0.5
    for p in range(blocks):
        i = at_ref[p]
        keys[p * loc:(p + 1) * loc, :] = rec_ref[i, :, base:base + HEAD_DIM]
        vals[p * loc:(p + 1) * loc, :] = rec_ref[i, :, base + HEAD_DIM:base + 2 * HEAD_DIM]
    rows = lax.broadcasted_iota(jnp.int32, (group * loc, loc), 0) % loc
    cols = lax.broadcasted_iota(jnp.int32, (group * loc, loc), 1)
    keep = cols <= rows

    def unrot(t, cosine, sine):
        return (t * cosine - pltpu.roll(t, HEAD_DIM // 2, 1) * sine).astype(BF16)

    for p in reversed(range(blocks)):
        i = at_ref[p]
        count = (p + 1) * loc
        span = slice(p * loc, count)
        query = jnp.concatenate([rec_ref[i, :, g * HEAD_DIM:(g + 1) * HEAD_DIM] for g in range(group)], axis=0)
        grad = jnp.concatenate([grad_ref[i, :, g * HEAD_DIM:(g + 1) * HEAD_DIM] for g in range(group)], axis=0)
        lse = lse_ref[p][:, :1]
        delta = jnp.sum(grad.astype(F32) * full_ref[p], axis=-1, keepdims=True)
        probs = jnp.exp(dot_rt(query, keys[:count, :]) * scale - lse)
        last = jnp.where(keep, probs[:, count - loc:], 0.0)
        probs = jnp.concatenate([probs[:, :count - loc], last], axis=1) if p else last
        d_probs = dot_rt(grad, vals[:count, :])
        g_scores = (probs * (d_probs - delta) * scale).astype(BF16)
        d_query = dot(g_scores, keys[:count, :])
        dk = dot_lt(g_scores, query)
        dv = dot_lt(probs.astype(BF16), grad)
        if p == blocks - 1:
            d_keys[...] = dk
            d_vals[...] = dv
        else:
            d_keys[:count, :] += dk
            d_vals[:count, :] += dv
        cosine, sine = cos_ref[span, :], sin_ref[span, :]
        for g in range(group):
            out_ref[i, :, g * HEAD_DIM:(g + 1) * HEAD_DIM] = unrot(d_query[g * loc:(g + 1) * loc], cosine, sine)
        out_ref[i, :, base:base + HEAD_DIM] = unrot(d_keys[span, :], cosine, sine)
        out_ref[i, :, base + HEAD_DIM:base + 2 * HEAD_DIM] = d_vals[span, :].astype(BF16)


def attend_back(at, rec, grad, full, lse, cosine, sine, group):
    blocks, loc, cols = rec.shape
    total = blocks * loc
    return pl.pallas_call(
        functools.partial(attend_back_kernel, group),
        out_shape=jax.ShapeDtypeStruct((blocks, loc, cols), BF16),
        in_specs=[SMEM] + [VMEM] * 6,
        out_specs=VMEM,
        scratch_shapes=[pltpu.VMEM((total, HEAD_DIM), BF16)] * 2 + [pltpu.VMEM((total, HEAD_DIM), F32)] * 2,
        compiler_params=params(60),
        cost_estimate=cost(),
    )(at, rec, grad, full, lse, cosine, sine)


def out_kernel(kv, mix_ref, w_ref, cat_ref, *outs):
    cols = mix_ref.shape[2]
    for s, out in enumerate(outs):
        cat_ref[s] = jnp.concatenate([mix_ref[s * kv + n] for n in range(kv)], axis=1)
        out[...] = dot(cat_ref[s], w_ref[...]).astype(BF16)


def out_project(mixed, w_out, seqs):
    units, loc, cols = mixed.shape
    kv = units // seqs
    width = w_out.shape[1]
    res = pl.pallas_call(
        functools.partial(out_kernel, kv),
        out_shape=(jax.ShapeDtypeStruct((seqs, loc, kv * cols), BF16),)
        + (jax.ShapeDtypeStruct((loc, width), BF16),) * seqs,
        in_specs=[VMEM] * 2,
        out_specs=(VMEM,) * (seqs + 1),
        compiler_params=params(24),
        cost_estimate=cost(),
    )(mixed, w_out)
    return res[0], res[1:]


def input_grads_kernel(seqs, kv, groups, back_ref, x_ref, wq_ref, wk_ref, wv_ref, *refs):
    gain_refs, outs, (rows_ref, inv_ref, attn_ref) = refs[:seqs], refs[seqs:seqs + groups], refs[seqs + groups:]
    per = seqs // groups
    loc, width = x_ref.shape[1], x_ref.shape[2]
    group = wq_ref.shape[1] // (kv * HEAD_DIM)
    gather(back_ref, rows_ref, seqs, kv, group)
    at_k = kv * group * HEAD_DIM
    at_v = at_k + kv * HEAD_DIM
    for s in range(seqs):
        x = x_ref[s].astype(F32)
        inv = lax.rsqrt(jnp.mean(x * x, axis=-1, keepdims=True) + EPS)
        inv_ref[s * loc:(s + 1) * loc, :] = jnp.broadcast_to(inv, (loc, HEAD_DIM))
    tile = 512
    for t in range(width // tile):
        span = slice(t * tile, (t + 1) * tile)
        grad = dot_rt(rows_ref[:, :at_k], wq_ref[span, :])
        grad += dot_rt(rows_ref[:, at_k:at_v], wk_ref[span, :])
        grad += dot_rt(rows_ref[:, at_v:], wv_ref[span, :])
        total = 0.0
        for s in range(seqs):
            part = grad[s * loc:(s + 1) * loc]
            at = (s % per) * loc
            outs[s // per][at:at + loc, span] = part.astype(BF16)
            unit = x_ref[s, :, span].astype(F32) * inv_ref[s * loc:(s + 1) * loc, :1]
            total = total + jnp.sum(part * unit, axis=0, keepdims=True)
        attn_ref[:, span] = total
    mlp = sum(ref[...] for ref in gain_refs)
    lines = []
    for gain in (attn_ref[...], mlp):
        high = gain.astype(BF16).astype(F32)
        lines += [high, gain - high]
    row = lax.broadcasted_iota(jnp.int32, (16, width), 0)
    extra = jnp.zeros((16, width), F32)
    for i, gain in enumerate(lines):
        extra = jnp.where(row == i, gain, extra)
    outs[0][per * loc:, :] = extra.astype(BF16)


def gather(back_ref, rows_ref, seqs, kv, group):
    loc = back_ref.shape[1]
    wide = group * HEAD_DIM
    for s in range(seqs):
        for n in range(kv):
            span = slice(s * loc, (s + 1) * loc)
            rows_ref[span, n * wide:(n + 1) * wide] = back_ref[s * kv + n, :, :wide]
            for i in range(2):
                at = kv * wide + (i * kv + n) * HEAD_DIM
                rows_ref[span, at:at + HEAD_DIM] = back_ref[s * kv + n, :, wide + i * HEAD_DIM:wide + (i + 1) * HEAD_DIM]


def input_grads(back, x, wq, wk, wv, gains, groups):
    seqs, loc, width = x.shape
    kv = wk.shape[1] // HEAD_DIM
    cols = wq.shape[1] + 2 * wk.shape[1]
    rows = seqs * loc // groups
    return pl.pallas_call(
        functools.partial(input_grads_kernel, seqs, kv, groups),
        out_shape=(jax.ShapeDtypeStruct((rows + 16, width), BF16),) + (jax.ShapeDtypeStruct((rows, width), BF16),) * (groups - 1),
        in_specs=[VMEM] * (5 + seqs),
        out_specs=(VMEM,) * groups,
        scratch_shapes=[
            pltpu.VMEM((seqs * loc, cols), BF16),
            pltpu.VMEM((seqs * loc, HEAD_DIM), F32),
            pltpu.VMEM((1, width), F32),
        ],
        compiler_params=params(60),
        cost_estimate=cost(),
    )(back, x, wq, wk, wv, *gains)


def shares_call(body, fixed, tall, cols, scratch, core, shares):
    width = tall[0].shape[-1]
    tile = width // shares

    def mine(step, keep, core_ref):
        return 2 * step + jnp.where(keep == 0, 1 - core_ref[0], core_ref[0])

    def tall_spec(a):
        lead = (0,) * (a.ndim - 1)
        return pl.BlockSpec(a.shape[:-1] + (tile,), lambda i, k, c: lead + (mine(i, k, c),))

    out = pl.BlockSpec((1, tile, cols), lambda i, k, c: (i, 0, 0))
    return pl.pallas_call(
        body,
        grid_spec=pltpu.PrefetchScalarGridSpec(
            num_scalar_prefetch=1,
            grid=(shares // 2, 2),
            in_specs=[pl.BlockSpec(a.shape, lambda i, k, c, n=a.ndim: (0,) * n) for a in fixed] + [tall_spec(a) for a in tall],
            out_specs=(out, out),
            scratch_shapes=scratch,
        ),
        out_shape=(jax.ShapeDtypeStruct((shares // 2, tile, cols), BF16),) * 2,
        compiler_params=params(60),
        cost_estimate=cost(),
    )(core, *fixed, *tall)


def put_share(send_ref, keep_ref, pieces):
    def store(ref):
        at = 0
        for piece in pieces:
            ref[0, :, at:at + piece.shape[1]] = piece.astype(BF16)
            at += piece.shape[1]

    @pl.when(pl.program_id(1) == 0)
    def _():
        store(send_ref)

    @pl.when(pl.program_id(1) == 1)
    def _():
        store(keep_ref)


def attn_grads_kernel(seqs, kv, group, core_ref, back_ref, mix_ref, norm_ref, *refs):
    grad_refs, (send_ref, keep_ref, rows_ref) = refs[:seqs], refs[seqs:]

    @pl.when((pl.program_id(0) == 0) & (pl.program_id(1) == 0))
    def _():
        gather(back_ref, rows_ref, seqs, kv, group)

    rows = rows_ref.shape[0]
    left = norm_ref[...].reshape(rows, norm_ref.shape[2])
    grad = jnp.concatenate([ref[...] for ref in grad_refs], axis=0)
    mixed = mix_ref[...].reshape(rows, mix_ref.shape[2])
    put_share(send_ref, keep_ref, [dot_lt(left, rows_ref[...]), dot_lt(grad, mixed)])


def attn_grads(core, back, mixed, normed, g_attns, kv, shares):
    seqs, loc, width = normed.shape
    group = back.shape[2] // HEAD_DIM - 2
    cols = kv * back.shape[2]
    scratch = [pltpu.VMEM((seqs * loc, cols), BF16)]
    body = functools.partial(attn_grads_kernel, seqs, kv, group)
    return shares_call(body, (back, mixed), (normed,) + tuple(g_attns), cols + mixed.shape[2], scratch, core, shares)


def ffn_grads_kernel(seqs, count, core_ref, *refs):
    rights, lefts = refs[:count * seqs], refs[count * seqs:-3]
    send_ref, keep_ref, right_ref = refs[-3:]
    lefts = [ref for ref in lefts if len(ref.shape) == 2 and ref.shape[1] < right_ref.shape[2]]

    @pl.when((pl.program_id(0) == 0) & (pl.program_id(1) == 0))
    def _():
        loc = rights[0].shape[0]
        for i in range(count):
            for s in range(seqs):
                right_ref[i, s * loc:(s + 1) * loc, :] = rights[i * seqs + s][...]

    left = jnp.concatenate([ref[...] for ref in lefts], axis=0)
    put_share(send_ref, keep_ref, [dot_lt(left, right_ref[i]) for i in range(count)])


def ffn_grads(core, rights, lefts, before, total, shares):
    seqs, count = len(rights[0]), len(rights)
    loc, units = rights[0][0].shape
    width = lefts[0].shape[1]
    tile = width // shares
    start = total - count if before else 0
    fixed = sum((tuple(r) for r in rights), ())
    left = [pl.BlockSpec((a.shape[0], tile), lambda i, k, c: (0, 2 * i + jnp.where(k == 0, 1 - c[0], c[0]))) for a in lefts]
    out = pl.BlockSpec((1, tile, count * units), lambda i, k, c: (i, 0, start // count))
    args = fixed + tuple(lefts) + tuple(before)
    return pl.pallas_call(
        functools.partial(ffn_grads_kernel, seqs, count),
        grid_spec=pltpu.PrefetchScalarGridSpec(
            num_scalar_prefetch=1,
            grid=(shares // 2, 2),
            in_specs=[pl.BlockSpec((loc, units), lambda i, k, c: (0, 0))] * len(fixed)
            + left
            + [pl.BlockSpec(memory_space=pl.ANY)] * len(before),
            out_specs=(out, out),
            scratch_shapes=[pltpu.VMEM((count, seqs * loc, units), BF16)],
        ),
        out_shape=(jax.ShapeDtypeStruct((shares // 2, tile, total * units), BF16),) * 2,
        input_output_aliases={len(args) - 1: 0, len(args): 1} if before else {},
        compiler_params=params(60),
        cost_estimate=cost(),
    )(core, *args)


def fold_two_kernel(place_ref, *refs):
    keeps, gots, outs = refs[:4], refs[4:8], refs[8:]
    for keep, got, out in zip(keeps, gots, outs):
        out[0] = (keep[0, 0].astype(F32) + got[0, 0].astype(F32)).astype(BF16)


def fold_two(place, keep, got):
    _, rows, cols = keep.shape
    half = rows // 2
    keep, got = keep.reshape(2, 2, rows, cols), got.reshape(2, 2, rows, cols)
    tile = half // 2
    ins = []
    for own in (0, 1):
        ins.append(pl.BlockSpec((1, 1, tile, cols), lambda i, j, p, own=own: (i, jnp.where(own == 1, p[0], 1 - p[0]), j, 0)))
    for own in (0, 1):
        ins.append(pl.BlockSpec((1, 1, tile, cols), lambda i, j, p, own=own: (jnp.where(own == 1, p[1], 1 - p[1]), i, j + 2, 0)))
    return pl.pallas_call(
        fold_two_kernel,
        grid_spec=pltpu.PrefetchScalarGridSpec(
            num_scalar_prefetch=1,
            grid=(2, 2),
            in_specs=ins + ins,
            out_specs=(pl.BlockSpec((1, tile, cols), lambda i, j, p: (i, j, 0)),) * 4,
        ),
        out_shape=(jax.ShapeDtypeStruct((2, half, cols), BF16),) * 4,
        compiler_params=params(60),
        cost_estimate=cost(),
    )(place, keep, keep, keep, keep, got, got, got, got)


def fold_three(place, upper, upper_got, lower, lower_got):
    _, half, cols = upper.shape
    tile = half // 2
    ins = []
    for axis in (1, 0):
        for own in (0, 1):
            ins.append(pl.BlockSpec((1, 1, tile, cols), lambda j, p, own=own, axis=axis: (0, jnp.where(own == 1, p[axis], 1 - p[axis]), j, 0)))
    flat = pl.BlockSpec((1, tile, cols), lambda j, p: (0, j, 0))
    u, ug, l, lg = (a[None] for a in (upper, upper_got, lower, lower_got))
    res = pl.pallas_call(
        fold_two_kernel,
        grid_spec=pltpu.PrefetchScalarGridSpec(
            num_scalar_prefetch=1, grid=(2,), in_specs=ins + ins, out_specs=(flat,) * 4
        ),
        out_shape=(jax.ShapeDtypeStruct((1, half, cols), BF16),) * 4,
        compiler_params=params(60),
        cost_estimate=cost(),
    )(place, u, u, l, l, ug, ug, lg, lg)
    return [a[0] for a in res]


def fold_four_kernel(widths, upper, upper_got, lower, lower_got, *outs):
    half = upper.shape[0]
    for at, (one, two) in enumerate(((upper, upper_got), (lower, lower_got))):
        start = 0
        for out, width in zip(outs, widths):
            part = one[:, start:start + width].astype(F32) + two[:, start:start + width].astype(F32)
            if out is outs[-1]:
                out[:, at * half:(at + 1) * half] = part.T
            else:
                out[at * half:(at + 1) * half, :] = part
            start += width


def fold_four(widths, upper, upper_got, lower, lower_got):
    rows = 2 * upper.shape[0]
    shapes = [(rows, w) for w in widths[:-1]] + [(widths[-1], rows)]
    return pl.pallas_call(
        functools.partial(fold_four_kernel, widths),
        out_shape=tuple(jax.ShapeDtypeStruct(shape, F32) for shape in shapes),
        in_specs=[VMEM] * 4,
        out_specs=(VMEM,) * len(widths),
        compiler_params=params(40),
        cost_estimate=cost(),
    )(upper, upper_got, lower, lower_got)


def finish_kernel(seqs, mid_ref, x_ref, gain_ref, *refs):
    inner, ends, resids, out_ref = refs[:seqs], refs[seqs:2 * seqs], refs[2 * seqs:3 * seqs], refs[3 * seqs]
    gain = gain_ref[...].astype(F32)
    for s in range(seqs):
        grad = jnp.where(mid_ref[0] == 1, inner[s][...].astype(F32), ends[s][...].astype(F32))
        x = x_ref[s].astype(F32)
        inv = lax.rsqrt(jnp.mean(x * x, axis=-1, keepdims=True) + EPS)
        unit = x * inv
        scaled = grad * gain
        back = inv * (scaled - unit * jnp.mean(scaled * unit, axis=-1, keepdims=True))
        out_ref[:, s, :] = resids[s][...] + back


def by_seq(group, seqs, loc, tile):
    per = seqs // len(group)
    return [
        (group[s // per], pl.BlockSpec((tile, group[0].shape[1]), lambda i, at=(s % per) * (loc // tile): (i + at, 0)))
        for s in range(seqs)
    ]


def finish(mid, x, gain, inner, ends, resids):
    seqs, loc, width = x.shape
    tile = 32
    parts = by_seq(inner, seqs, loc, tile) + by_seq(ends, seqs, loc, tile) + by_seq(resids, seqs, loc, tile)
    return pl.pallas_call(
        functools.partial(finish_kernel, seqs),
        grid=(loc // tile,),
        out_shape=jax.ShapeDtypeStruct((loc, seqs, width), F32),
        in_specs=[SMEM, pl.BlockSpec((seqs, tile, width), lambda i: (0, i, 0)), pl.BlockSpec((1, width), lambda i: (0, 0))]
        + [spec for _, spec in parts],
        out_specs=pl.BlockSpec((tile, seqs, width), lambda i: (i, 0, 0)),
        compiler_params=params(60),
        cost_estimate=cost(),
    )(mid, x, gain, *(a for a, _ in parts))


def output_kernel(seqs, mid_ref, x_ref, *refs):
    attn, inner, ends, out_ref, wide = refs[:seqs], refs[seqs:2 * seqs], refs[2 * seqs:3 * seqs], refs[3 * seqs], refs[3 * seqs + 1]
    for s in range(seqs):
        down = jnp.where(mid_ref[0] == 1, inner[s][...].astype(F32), ends[s][...].astype(F32))
        wide[:, s, :] = x_ref[s].astype(F32) + attn[s][...].astype(F32) + down
    out_ref[...] = wide[...].astype(BF16)


def block_output(mid, x, attn, inner, ends):
    seqs, loc, width = x.shape
    tile = 32
    parts = by_seq(attn, seqs, loc, tile) + by_seq(inner, seqs, loc, tile) + by_seq(ends, seqs, loc, tile)
    return pl.pallas_call(
        functools.partial(output_kernel, seqs),
        grid=(loc // tile,),
        out_shape=jax.ShapeDtypeStruct((loc, seqs, width), BF16),
        in_specs=[SMEM, pl.BlockSpec((seqs, tile, width), lambda i: (0, i, 0))] + [spec for _, spec in parts],
        out_specs=pl.BlockSpec((tile, seqs, width), lambda i: (i, 0, 0)),
        scratch_shapes=[pltpu.VMEM((tile, seqs, width), F32)],
        compiler_params=params(60),
        cost_estimate=cost(),
    )(mid, x, *(a for a, _ in parts))


def add_kernel(left, right, out):
    out[...] = (left[...].astype(F32) + right[...].astype(F32)).astype(BF16)


def add(left, right):
    return pl.pallas_call(
        add_kernel,
        out_shape=jax.ShapeDtypeStruct(left.shape, BF16),
        in_specs=[VMEM, VMEM],
        out_specs=VMEM,
        compiler_params=params(16),
        cost_estimate=cost(),
    )(left, right)


def rope_tables(positions, head_dim):
    half = head_dim // 2
    freq = jnp.exp(jnp.arange(half, dtype=jnp.float32) * (-2.0 * math.log(THETA) / head_dim))
    angles = positions.astype(jnp.float32)[:, None] * freq[None, :]
    return (jnp.cos(angles), jnp.sin(angles))


def rotate(values, cosine, sine):
    half = values.shape[-1] // 2
    first = values[..., :half]
    second = values[..., half:]
    cosine = cosine[:, None, None, :]
    sine = sine[:, None, None, :]
    return jnp.concatenate(
        [first * cosine - second * sine, second * cosine + first * sine], axis=-1
    )


def inverse_rms(values):
    return lax.rsqrt(jnp.mean(values * values, axis=-1, keepdims=True) + EPS)


def norm_back(values, inverse, gain, grad):
    unit = values * inverse
    scaled = grad * gain
    back = inverse * (scaled - unit * jnp.mean(scaled * unit, axis=-1, keepdims=True))
    return (back, jnp.sum(grad * unit, axis=(0, 1)))


def matmul(values, weight):
    return jnp.einsum("lsd,de->lse", values, weight, preferred_element_type=jnp.float32)


def matmul_back(values, weight):
    return jnp.einsum("lse,de->lsd", values, weight, preferred_element_type=jnp.float32)


def weight_grad(left, right):
    return jnp.einsum("lsd,lse->de", left, right, preferred_element_type=jnp.float32)


def general(
    hidden_in,
    block_order,
    seq_labels,
    exit_scales,
    attn_gain,
    w_query,
    w_key,
    w_value,
    w_out,
    mlp_gain,
    w_gate,
    w_up,
    w_down,
    d_out,
):
    f32 = jnp.float32
    bf16 = jnp.bfloat16
    loc, seqs, width = hidden_in.shape
    head_dim = HEAD_DIM
    q_heads = w_query.shape[1] // head_dim
    kv_heads = w_key.shape[1] // head_dim
    group = q_heads // kv_heads
    scale = head_dim ** (-0.5)
    blocks_all = block_order.shape[0]
    total_rows = loc * lax.axis_size("blk")
    key_rows = math.gcd(512, total_rows)
    block_count = total_rows // key_rows
    kv_width = 2 * kv_heads * head_dim
    positions = block_order[lax.axis_index("blk")] * loc + jnp.arange(loc, dtype=jnp.int32)
    cosine, sine = rope_tables(positions, head_dim)

    def key_positions(start, count):
        index = start + jnp.arange(count, dtype=jnp.int32)
        owner = index // loc
        table = jnp.sum(
            jnp.where(
                owner[:, None] == jnp.arange(blocks_all, dtype=jnp.int32)[None, :],
                block_order[None, :],
                0,
            ),
            axis=1,
        )
        return table * loc + index % loc

    xin = hidden_in.astype(f32)
    inv_a = inverse_rms(xin)
    gain_a = attn_gain.astype(f32)
    normed = (xin * inv_a * gain_a).astype(bf16)
    query_bf = rotate(
        matmul(normed, w_query).reshape(loc, seqs, q_heads, head_dim), cosine, sine
    ).astype(bf16)
    keys_bf = (
        rotate(matmul(normed, w_key).reshape(loc, seqs, kv_heads, head_dim), cosine, sine)
        .astype(bf16)
        .reshape(loc, seqs, kv_heads * head_dim)
    )
    vals_bf = matmul(normed, w_value).astype(bf16)
    query_g = query_bf.reshape(loc, seqs, kv_heads, group, head_dim)
    starts = jnp.arange(block_count, dtype=jnp.int32) * key_rows
    top = jnp.full((seqs, kv_heads, group, loc), NEG, f32)
    key_part = lax.all_gather(keys_bf, "blk", axis=0, tiled=True)
    val_part = lax.all_gather(vals_bf, "blk", axis=0, tiled=True)
    count = key_part.shape[0]
    kk = key_part.reshape(count, seqs, kv_heads, head_dim)
    vv = val_part.reshape(count, seqs, kv_heads, head_dim)
    mask = key_positions(jnp.int32(0), count)[None, :] <= positions[:, None]
    raw = jnp.einsum("lsngd,msnd->snglm", query_g, kk, preferred_element_type=f32)
    scores = jnp.where(mask, raw * scale, NEG)
    new_top = jnp.maximum(top, jnp.max(scores, axis=-1))
    weights = jnp.where(mask, jnp.exp(scores - new_top[..., None]), 0.0)
    total = jnp.sum(weights, axis=-1)
    acc = jnp.einsum("snglm,msnd->sngld", weights.astype(bf16), vv, preferred_element_type=f32)
    top, total, acc = (new_top, total, acc)
    lse = top + jnp.log(total)
    mixed_raw = acc / total[..., None]
    mixed_bf = (
        mixed_raw.transpose(3, 0, 1, 2, 4).reshape(loc, seqs, q_heads * head_dim).astype(bf16)
    )
    resid = xin + lax.psum(matmul(mixed_bf, w_out).astype(jnp.bfloat16), "tp").astype(jnp.float32)
    inv_m = inverse_rms(resid)
    gain_m = mlp_gain.astype(f32)
    normed_m = (resid * inv_m * gain_m).astype(bf16)
    gate = matmul(normed_m, w_gate)
    up = matmul(normed_m, w_up)
    sig = jax.nn.sigmoid(gate)
    silu = gate * sig
    hidden = (silu * up).astype(bf16)
    output = resid + lax.psum(matmul(hidden, w_down).astype(jnp.bfloat16), "tp").astype(jnp.float32)
    block_out = output.astype(bf16)
    scale_rows = jnp.where(seq_labels == 1, exit_scales[1], exit_scales[0])
    cot = d_out.astype(f32) * scale_rows[None, :, None]
    g_down = cot.astype(bf16)
    d_w_down = weight_grad(hidden, g_down)
    d_hidden = matmul_back(g_down, w_down)
    g_up = (d_hidden * silu).astype(bf16)
    g_gate = (d_hidden * up * (sig * (1.0 + gate * (1.0 - sig)))).astype(bf16)
    d_w_gate = weight_grad(normed_m, g_gate)
    d_w_up = weight_grad(normed_m, g_up)
    d_nm = lax.psum(
        (matmul_back(g_gate, w_gate) + matmul_back(g_up, w_up)).astype(jnp.bfloat16), "tp"
    ).astype(jnp.float32)
    d_resid_norm, d_mlp_gain = norm_back(resid, inv_m, gain_m, d_nm)
    d_resid = cot + d_resid_norm
    g_attn = d_resid.astype(bf16)
    d_w_out = weight_grad(mixed_bf, g_attn)
    g_mixed = matmul_back(g_attn, w_out).astype(bf16)
    g_mixed_g = g_mixed.reshape(loc, seqs, kv_heads, group, head_dim)
    delta = jnp.sum(g_mixed_g.astype(f32).transpose(1, 2, 3, 0, 4) * mixed_raw, axis=-1)
    whole_keys, whole_vals = (
        lax.all_gather(keys_bf, "blk", axis=0, tiled=True),
        lax.all_gather(vals_bf, "blk", axis=0, tiled=True),
    )

    def probe(kk, vv, start, count):
        mask = key_positions(start, count)[None, :] <= positions[:, None]
        raw = jnp.einsum("lsngd,msnd->snglm", query_g, kk, preferred_element_type=f32)
        probs = jnp.where(mask, jnp.exp(raw * scale - lse[..., None]), 0.0)
        d_probs = jnp.einsum("lsngd,msnd->snglm", g_mixed_g, vv, preferred_element_type=f32)
        g_scores = (probs * (d_probs - delta[..., None]) * scale).astype(bf16)
        return (g_scores, probs)

    def kv_pair(g_scores, probs, count):
        d_keys = jnp.einsum("snglm,lsngd->msnd", g_scores, query_g, preferred_element_type=f32)
        d_vals = jnp.einsum(
            "snglm,lsngd->msnd", probs.astype(bf16), g_mixed_g, preferred_element_type=f32
        )
        return jnp.concatenate([d_keys, d_vals], axis=2).reshape(count, seqs, kv_width)

    scan_items = (
        whole_keys.reshape(block_count, key_rows, seqs, -1),
        whole_vals.reshape(block_count, key_rows, seqs, -1),
        starts,
    )
    zero_query = jnp.zeros((loc, seqs, kv_heads, group, head_dim), f32)

    def back_step(d_query, item):
        key_part, val_part, start = item
        kk = key_part.reshape(key_rows, seqs, kv_heads, head_dim)
        vv = val_part.reshape(key_rows, seqs, kv_heads, head_dim)
        g_scores, probs = probe(kk, vv, start, key_rows)
        d_query = d_query + jnp.einsum(
            "snglm,msnd->lsngd", g_scores, kk, preferred_element_type=f32
        )
        return (d_query, kv_pair(g_scores, probs, key_rows))

    d_query, kv_terms = lax.scan(back_step, zero_query, scan_items)
    kv_local = lax.psum_scatter(
        kv_terms.reshape(total_rows, seqs, kv_width).astype(jnp.bfloat16),
        "blk",
        scatter_dimension=0,
        tiled=True,
    ).astype(jnp.float32)
    kv_local = kv_local.reshape(loc, seqs, 2, kv_heads, head_dim)
    g_q = (
        rotate(d_query.reshape(loc, seqs, q_heads, head_dim), cosine, -sine)
        .astype(bf16)
        .reshape(loc, seqs, q_heads * head_dim)
    )
    g_k = (
        rotate(kv_local[:, :, 0], cosine, -sine)
        .astype(bf16)
        .reshape(loc, seqs, kv_heads * head_dim)
    )
    g_v = kv_local[:, :, 1].astype(bf16).reshape(loc, seqs, kv_heads * head_dim)
    d_w_query = weight_grad(normed, g_q)
    d_w_key = weight_grad(normed, g_k)
    d_w_value = weight_grad(normed, g_v)
    d_n = lax.psum(
        (matmul_back(g_q, w_query) + matmul_back(g_k, w_key) + matmul_back(g_v, w_value)).astype(
            jnp.bfloat16
        ),
        "tp",
    ).astype(jnp.float32)
    d_in_norm, d_attn_gain = norm_back(xin, inv_a, gain_a, d_n)
    d_hidden_in = d_resid + d_in_norm
    d_attn_gain, d_w_query, d_w_key, d_w_value, d_w_out, d_mlp_gain, d_w_gate, d_w_up, d_w_down = (
        lax.psum_scatter(
            d_attn_gain.astype(jnp.bfloat16), "blk", scatter_dimension=0, tiled=True
        ).astype(jnp.float32),
        lax.psum_scatter(
            d_w_query.astype(jnp.bfloat16), "blk", scatter_dimension=0, tiled=True
        ).astype(jnp.float32),
        lax.psum_scatter(
            d_w_key.astype(jnp.bfloat16), "blk", scatter_dimension=0, tiled=True
        ).astype(jnp.float32),
        lax.psum_scatter(
            d_w_value.astype(jnp.bfloat16), "blk", scatter_dimension=0, tiled=True
        ).astype(jnp.float32),
        lax.psum_scatter(
            d_w_out.astype(jnp.bfloat16), "blk", scatter_dimension=1, tiled=True
        ).astype(jnp.float32),
        lax.psum_scatter(
            d_mlp_gain.astype(jnp.bfloat16), "blk", scatter_dimension=0, tiled=True
        ).astype(jnp.float32),
        lax.psum_scatter(
            d_w_gate.astype(jnp.bfloat16), "blk", scatter_dimension=0, tiled=True
        ).astype(jnp.float32),
        lax.psum_scatter(
            d_w_up.astype(jnp.bfloat16), "blk", scatter_dimension=0, tiled=True
        ).astype(jnp.float32),
        lax.psum_scatter(
            d_w_down.astype(jnp.bfloat16), "blk", scatter_dimension=1, tiled=True
        ).astype(jnp.float32),
    )
    return (
        block_out,
        d_hidden_in,
        d_attn_gain,
        d_w_query,
        d_w_key,
        d_w_value,
        d_w_out,
        d_mlp_gain,
        d_w_gate,
        d_w_up,
        d_w_down,
    )


class Steps:
    def __init__(self):
        self.last = None

    def enter(self, *values):
        if self.last is not None:
            values, _ = lax.optimization_barrier((values, self.last))
        return values if len(values) > 1 else values[0]

    def leave(self, value):
        self.last = value
        return value


class Line:
    def __init__(self, steps, middle, parts):
        self.steps, self.middle, self.parts = steps, middle, list(parts)
        count = len(self.parts)
        self.first, self.half, self.second, self.total, self.third, self.done = ([None] * count for _ in range(6))

    def one(self, c):
        self.first[c] = lax.ppermute(self.parts[c], "tp", [(0, 1), (3, 2)])

    def two(self, c):
        part, got = self.steps.enter(self.parts[c], self.first[c])
        self.half[c] = self.steps.leave(add(part, got))
        self.second[c] = lax.ppermute(self.half[c], "tp", [(1, 2), (2, 1)])

    def three(self, c):
        half, got = self.steps.enter(self.half[c], self.second[c])
        self.total[c] = self.steps.leave(add(half, got))
        self.third[c] = lax.ppermute(self.total[c], "tp", [(1, 0), (2, 3)])

    def four(self, c):
        total, got = self.steps.enter(self.total[c], self.third[c])
        self.done[c] = self.steps.leave(jnp.where(self.middle, total, got))

    def five(self, c):
        self.third[c] = self.steps.leave(self.steps.enter(self.third[c]))


def partner(bit):
    return [(i, i ^ bit) for i in range(8)]


class Scatter:
    def __init__(self, steps, place, send, keep):
        self.steps, self.place, self.send, self.keep = steps, place, send, keep

    def one_go(self):
        self.got = lax.ppermute(self.steps.enter(self.send), "blk", partner(1))

    def two(self):
        keep, got = self.steps.enter(self.keep, self.got)
        self.away, self.upper, self.off, self.lower = fold_two(self.place, keep, got)
        self.steps.leave(self.upper)

    def two_go(self, first=2, second=4):
        away, off = self.steps.enter(self.away, self.off)
        self.upper_got = lax.ppermute(away, "blk", partner(first))
        self.lower_got = lax.ppermute(off, "blk", partner(second))

    def three(self):
        values = self.steps.enter(self.upper, self.upper_got, self.lower, self.lower_got)
        self.away, self.upper, self.off, self.lower = fold_three(self.place, *values)
        self.steps.leave(self.upper)

    def three_go(self):
        self.two_go(4, 2)

    def four(self, widths):
        values = self.steps.enter(self.upper, self.upper_got, self.lower, self.lower_got)
        res = fold_four(widths, *values)
        self.steps.leave(res[0])
        return res


def inverse(values):
    return lax.rsqrt(jnp.mean(values * values, axis=-1, keepdims=True) + EPS)


def tables(positions):
    cosine, sine = rope_tables(positions, HEAD_DIM)
    return jnp.concatenate([cosine, cosine], axis=1), jnp.concatenate([-sine, sine], axis=1)


def fast(
    hidden_in,
    block_order,
    seq_labels,
    exit_scales,
    attn_gain,
    w_query,
    w_key,
    w_value,
    w_out,
    mlp_gain,
    w_gate,
    w_up,
    w_down,
    d_out,
):
    loc, seqs, width = hidden_in.shape
    blocks = block_order.shape[0]
    rows = seqs * loc
    units = w_gate.shape[1]
    kv = w_key.shape[1] // HEAD_DIM
    group = w_query.shape[1] // w_key.shape[1]
    wide = group * HEAD_DIM
    me = lax.axis_index("blk")
    line = lax.axis_index("tp")
    middle = (line == 1) | (line == 2)
    index = jnp.arange(blocks, dtype=jnp.int32)
    at = jnp.sum(jnp.where(block_order[None, :] == index[:, None], index[None, :], 0), axis=1)
    mine = jnp.sum(jnp.where(index == me, block_order, 0)) * loc + jnp.arange(loc, dtype=jnp.int32)
    steps = Steps()
    enter, leave = steps.enter, steps.leave

    x = hidden_in.transpose(1, 0, 2)
    cosine, sine = tables(mine)
    messages, normed = project(x, attn_gain[None, :], cosine, sine, w_query, w_key, w_value)
    leave(messages)
    rec = lax.all_to_all(messages, "blk", 0, 0, tiled=True)
    scales = jnp.where(seq_labels == 1, exit_scales[1], exit_scales[0])
    cot = enter(d_out).transpose(1, 0, 2).astype(F32) * scales[:, None, None]
    g_down = leave(cot.astype(BF16).reshape(rows, width))
    d_hidden = leave(dot_rt(g_down, w_down).astype(BF16))
    mixed, full, lse = attend(at, enter(rec), group)
    leave(mixed)
    mixed = lax.all_to_all(mixed, "blk", 0, 0, tiled=True)
    all_cosine, all_sine = tables(enter(jnp.arange(blocks * loc, dtype=jnp.int32)))
    leave(all_cosine)
    mixed, parts = out_project(enter(mixed), w_out, seqs)
    leave(mixed)

    gain_m = mlp_gain.astype(F32)
    attn = Line(steps, middle, parts)
    back = Line(steps, middle, [None] * seqs)
    norms, hiddens, gates, ups, gains = ([None] * seqs for _ in range(5))

    def feed(s):
        total = attn.done[s]
        resid = x[s].astype(F32) + total.astype(F32)
        unit = resid * inverse(resid)
        norm = (unit * gain_m).astype(BF16)
        gate = dot(norm, w_gate)
        up = dot(norm, w_up)
        sig = jax.nn.sigmoid(gate)
        silu = gate * sig
        grad_h = d_hidden[s * loc:(s + 1) * loc].astype(F32)
        g_up = (grad_h * silu).astype(BF16)
        g_gate = (grad_h * up * (sig * (1.0 + gate * (1.0 - sig)))).astype(BF16)
        grad = dot_rt(g_gate, w_gate) + dot_rt(g_up, w_up)
        gains[s] = jnp.sum(grad * unit, axis=0)
        back.parts[s] = leave(grad.astype(BF16))
        norms[s], gates[s], ups[s] = norm, g_gate, g_up
        hiddens[s] = (silu * up).astype(BF16)

    d_resids, g_attns, sends = ([None] * seqs for _ in range(3))

    def norm_back(s):
        resid = x[s].astype(F32) + attn.done[s].astype(F32)
        inv = inverse(resid)
        unit = resid * inv
        scaled = back.done[s].astype(F32) * gain_m
        d_resids[s] = cot[s] + inv * (scaled - unit * jnp.mean(scaled * unit, axis=-1, keepdims=True))
        g_attns[s] = d_resids[s].astype(BF16)
        sends[s] = leave(dot_rt(g_attns[s], w_out).astype(BF16))

    def run(lines, *texts):
        for word in " ".join(texts).split():
            name, c = word[:-1], int(word[-1])
            if name == "F":
                feed(c)
            elif name == "N":
                norm_back(c)
            elif name == "O":
                hidden = jnp.concatenate(enter(hiddens[2 * c:2 * c + 2]), axis=0)
                outs.parts[c] = leave(dot(hidden, w_down).astype(BF16))
            else:
                obj = lines[name[0]]
                (obj.one, obj.two, obj.three, obj.four, obj.five)[int(name[1]) - 1](c)

    outs = Line(steps, middle, [None] * 2)
    lines = {"a": attn, "b": back, "c": outs}
    core = (me % 2).astype(jnp.int32)[None]
    place = jnp.stack([(me // 2) % 2, me // 4]).astype(jnp.int32)
    run(
        lines,
        "a10 a11 a12 a13",
        "a20 a21 a30 a22",
        "a31 a40 F0 b10",
        "a23 a32 a41 F1",
        "b11",
    )
    run(
        lines,
        "a33 a42 F2 b12",
        "b20 a43 F3 b13",
        "b21 b30",
    )
    run(
        lines,
        "O0 O1 b22 b31",
        "b40 N0 b23 b32",
        "b41 N1 b33 b42",
        "N2 b43 N3",
    )
    send = jnp.stack(enter(sends)).reshape(seqs, loc, kv, wide).transpose(0, 2, 1, 3).reshape(seqs * kv, loc, wide)
    grad = lax.all_to_all(send, "blk", 0, 0, tiled=True)
    made = leave(ffn_grads(core, *enter([gates, ups], norms), (), 3, blocks))
    run(lines, "c10 c11 c20")
    grads = leave(attend_back(at, rec, enter(grad), full, lse, all_cosine, all_sine, group))
    grads = lax.all_to_all(grads, "blk", 0, 0, tiled=True)
    send, keep = ffn_grads(core, *enter([hiddens], [g_down], made), 3, blocks)
    leave(keep)
    ffn_sum = Scatter(steps, place, send, keep)
    run(lines, "c21 c30")

    grads = enter(grads)
    parts = input_grads(grads, x, w_query, w_key, w_value, [g[None, :] for g in gains], 2)
    ins = Line(steps, middle, parts)
    leave(ins.parts[0])
    lines["d"] = ins
    run(lines, "d10 d11")
    ffn_sum.one_go()
    send, keep = attn_grads(*enter(core, grads, mixed, normed, g_attns), kv, blocks)
    leave(keep)
    attn_sum = Scatter(steps, place, send, keep)
    ffn_sum.two()
    ffn_sum.two_go()
    run(lines, "c31 c50 d20")
    attn_sum.one_go()
    run(lines, "d21 d30")
    attn_sum.two()
    attn_sum.two_go()
    ffn_sum.three()
    ffn_sum.three_go()
    run(lines, "c51")
    mid = middle.astype(jnp.int32)[None]
    block_out = leave(block_output(mid, x, attn.done, enter(outs.total), outs.third))
    attn_sum.three()
    run(lines, "d31")
    attn_sum.three_go()
    run(lines, "d40")
    extra = ins.done[0][2 * loc:2 * loc + 4].astype(F32)
    both = (extra[0::2] + extra[1::2]).reshape(2, 8, width // 8)
    both = leave(both + lax.ppermute(both, "blk", partner(1)))
    others = [lax.ppermute(enter(both), "blk", partner(bit)) for bit in (2, 4, 6)]
    d_w_gate, d_w_up, d_w_down = ffn_sum.four((units, units, units))
    run(lines, "d51")
    d_hidden_in = finish(
        mid,
        x,
        attn_gain[None, :],
        ins.total,
        ins.third,
        d_resids,
    )
    leave(d_hidden_in)
    d_w_query, d_w_key, d_w_value, d_w_out = attn_sum.four((kv * wide, kv * HEAD_DIM, kv * HEAD_DIM, kv * wide))
    others = enter(others)
    both = both + others[0] + others[1] + others[2]
    both = lax.dynamic_index_in_dim(both, me, 1, keepdims=False)
    return (
        block_out,
        d_hidden_in,
        both[0],
        d_w_query,
        d_w_key,
        d_w_value,
        d_w_out,
        both[1],
        d_w_gate,
        d_w_up,
        d_w_down,
    )


def per_device(*args):
    seqs = args[0].shape[1]
    kv_heads = args[6].shape[1] // HEAD_DIM
    fits = lax.axis_size("blk") == 8 and lax.axis_size("tp") == 4 and seqs * kv_heads == 8
    return (fast if fits else general)(*args)


def solution(mesh):
    return jax.shard_map(
        per_device,
        mesh=mesh,
        in_specs=(
            P("blk", None, None),
            P(),
            P(),
            P(),
            P(),
            P(None, "tp"),
            P(None, "tp"),
            P(None, "tp"),
            P("tp", None),
            P(),
            P(None, "tp"),
            P(None, "tp"),
            P("tp", None),
            P("blk", None, None),
        ),
        out_specs=(
            P("blk", None, None),
            P("blk", None, None),
            P("blk"),
            P("blk", "tp"),
            P("blk", "tp"),
            P("blk", "tp"),
            P("tp", "blk"),
            P("blk"),
            P("blk", "tp"),
            P("blk", "tp"),
            P("tp", "blk"),
        ),
        check_vma=False,
    )
```

```python
import functools
import math

import jax
import jax.numpy as jnp
from jax import lax
from jax.experimental import pallas as pl
from jax.experimental.pallas import tpu as pltpu
from jax.sharding import PartitionSpec as P

HEAD_DIM = 128
EPS = 1e-05
THETA = 10000.0
NEG = -1e30
F32 = jnp.float32
BF16 = jnp.bfloat16
MIB = 1024 * 1024


def dot(left, right):
    return lax.dot_general(left, right, (((1,), (0,)), ((), ())), preferred_element_type=F32)


def dot_rt(left, right):
    return lax.dot_general(left, right, (((1,), (1,)), ((), ())), preferred_element_type=F32)


def dot_lt(left, right):
    return lax.dot_general(left, right, (((0,), (0,)), ((), ())), preferred_element_type=F32)


def params(limit):
    return pltpu.CompilerParams(vmem_limit_bytes=limit * MIB)


def cost():
    return pl.CostEstimate(flops=10**9, bytes_accessed=10**6, transcendentals=0)


SMEM = pl.BlockSpec(memory_space=pltpu.SMEM)
VMEM = pl.BlockSpec(memory_space=pltpu.VMEM)


def project_kernel(heads, kv, x_ref, gain_ref, cos_ref, sin_ref, wq_ref, wk_ref, wv_ref, msg_ref, norm_ref):
    group = heads // kv
    seqs, loc, width = x_ref.shape
    gain = gain_ref[...].astype(F32)
    for s in range(seqs):
        x = x_ref[s].astype(F32)
        inv = lax.rsqrt(jnp.mean(x * x, axis=-1, keepdims=True) + EPS)
        norm_ref[s] = (x * inv * gain).astype(BF16)
    normed = norm_ref[...].reshape(seqs * loc, width)
    cosine, sine = cos_ref[...], sin_ref[...]

    def rot(t):
        return (t * cosine + pltpu.roll(t, HEAD_DIM // 2, 1) * sine).astype(BF16)

    def put(res, h, s, n, slot, turn):
        part = res[s * loc:(s + 1) * loc, h * HEAD_DIM:(h + 1) * HEAD_DIM]
        msg_ref[s * kv + n, :, slot * HEAD_DIM:(slot + 1) * HEAD_DIM] = rot(part) if turn else part.astype(BF16)

    query = dot(normed, wq_ref[...])
    for s in range(seqs):
        for h in range(heads):
            put(query, h, s, h // group, h % group, True)
    keys = dot(normed, wk_ref[...])
    for s in range(seqs):
        for n in range(kv):
            put(keys, n, s, n, group, True)
    vals = dot(normed, wv_ref[...])
    for s in range(seqs):
        for n in range(kv):
            put(vals, n, s, n, group + 1, False)


def project(x, gain, cosine, sine, wq, wk, wv):
    seqs, loc, width = x.shape
    heads, kv = wq.shape[1] // HEAD_DIM, wk.shape[1] // HEAD_DIM
    cols = (heads // kv + 2) * HEAD_DIM
    return pl.pallas_call(
        functools.partial(project_kernel, heads, kv),
        out_shape=(jax.ShapeDtypeStruct((seqs * kv, loc, cols), BF16), jax.ShapeDtypeStruct(x.shape, BF16)),
        in_specs=[VMEM] * 7,
        out_specs=(VMEM, VMEM),
        compiler_params=params(32),
        cost_estimate=cost(),
    )(x, gain, cosine, sine, wq, wk, wv)


def attend_kernel(group, at_ref, rec_ref, out_ref, full_ref, lse_ref, keys, vals):
    blocks, loc, _ = rec_ref.shape
    base = group * HEAD_DIM
    for p in range(blocks):
        i = at_ref[p]
        keys[p * loc:(p + 1) * loc, :] = rec_ref[i, :, base:base + HEAD_DIM]
        vals[p * loc:(p + 1) * loc, :] = rec_ref[i, :, base + HEAD_DIM:base + 2 * HEAD_DIM]
    rows = lax.broadcasted_iota(jnp.int32, (group * loc, loc), 0) % loc
    cols = lax.broadcasted_iota(jnp.int32, (group * loc, loc), 1)
    keep = cols <= rows
    for p in range(blocks):
        i = at_ref[p]
        count = (p + 1) * loc
        query = jnp.concatenate([rec_ref[i, :, g * HEAD_DIM:(g + 1) * HEAD_DIM] for g in range(group)], axis=0)
        scores = dot_rt(query, keys[:count, :]) * (HEAD_DIM ** -0.5)
        last = jnp.where(keep, scores[:, count - loc:], NEG)
        scores = jnp.concatenate([scores[:, :count - loc], last], axis=1) if p else last
        top = jnp.max(scores, axis=-1, keepdims=True)
        weights = jnp.exp(scores - top)
        total = jnp.sum(weights, axis=-1, keepdims=True)
        mixed = dot(weights.astype(BF16), vals[:count, :]) / total
        lse_ref[p] = jnp.broadcast_to(top + jnp.log(total), (group * loc, HEAD_DIM))
        full_ref[p] = mixed
        for g in range(group):
            out_ref[i, :, g * HEAD_DIM:(g + 1) * HEAD_DIM] = mixed[g * loc:(g + 1) * loc].astype(BF16)


def attend(at, rec, group):
    blocks, loc, _ = rec.shape
    total = blocks * loc
    return pl.pallas_call(
        functools.partial(attend_kernel, group),
        out_shape=(
            jax.ShapeDtypeStruct((blocks, loc, group * HEAD_DIM), BF16),
            jax.ShapeDtypeStruct((blocks, group * loc, HEAD_DIM), F32),
            jax.ShapeDtypeStruct((blocks, group * loc, HEAD_DIM), F32),
        ),
        in_specs=[SMEM, VMEM],
        out_specs=(VMEM,) * 3,
        scratch_shapes=[pltpu.VMEM((total, HEAD_DIM), BF16)] * 2,
        compiler_params=params(60),
        cost_estimate=cost(),
    )(at, rec)


def attend_back_kernel(group, at_ref, rec_ref, grad_ref, full_ref, lse_ref, cos_ref, sin_ref, out_ref, keys, vals, d_keys, d_vals):
    blocks, loc, _ = rec_ref.shape
    base = group * HEAD_DIM
    scale = HEAD_DIM ** -0.5
    for p in range(blocks):
        i = at_ref[p]
        keys[p * loc:(p + 1) * loc, :] = rec_ref[i, :, base:base + HEAD_DIM]
        vals[p * loc:(p + 1) * loc, :] = rec_ref[i, :, base + HEAD_DIM:base + 2 * HEAD_DIM]
    rows = lax.broadcasted_iota(jnp.int32, (group * loc, loc), 0) % loc
    cols = lax.broadcasted_iota(jnp.int32, (group * loc, loc), 1)
    keep = cols <= rows

    def unrot(t, cosine, sine):
        return (t * cosine - pltpu.roll(t, HEAD_DIM // 2, 1) * sine).astype(BF16)

    for p in reversed(range(blocks)):
        i = at_ref[p]
        count = (p + 1) * loc
        span = slice(p * loc, count)
        query = jnp.concatenate([rec_ref[i, :, g * HEAD_DIM:(g + 1) * HEAD_DIM] for g in range(group)], axis=0)
        grad = jnp.concatenate([grad_ref[i, :, g * HEAD_DIM:(g + 1) * HEAD_DIM] for g in range(group)], axis=0)
        lse = lse_ref[p][:, :1]
        delta = jnp.sum(grad.astype(F32) * full_ref[p], axis=-1, keepdims=True)
        probs = jnp.exp(dot_rt(query, keys[:count, :]) * scale - lse)
        last = jnp.where(keep, probs[:, count - loc:], 0.0)
        probs = jnp.concatenate([probs[:, :count - loc], last], axis=1) if p else last
        d_probs = dot_rt(grad, vals[:count, :])
        g_scores = (probs * (d_probs - delta) * scale).astype(BF16)
        d_query = dot(g_scores, keys[:count, :])
        dk = dot_lt(g_scores, query)
        dv = dot_lt(probs.astype(BF16), grad)
        if p == blocks - 1:
            d_keys[...] = dk
            d_vals[...] = dv
        else:
            d_keys[:count, :] += dk
            d_vals[:count, :] += dv
        cosine, sine = cos_ref[span, :], sin_ref[span, :]
        for g in range(group):
            out_ref[i, :, g * HEAD_DIM:(g + 1) * HEAD_DIM] = unrot(d_query[g * loc:(g + 1) * loc], cosine, sine)
        out_ref[i, :, base:base + HEAD_DIM] = unrot(d_keys[span, :], cosine, sine)
        out_ref[i, :, base + HEAD_DIM:base + 2 * HEAD_DIM] = d_vals[span, :].astype(BF16)


def attend_back(at, rec, grad, full, lse, cosine, sine, group):
    blocks, loc, cols = rec.shape
    total = blocks * loc
    return pl.pallas_call(
        functools.partial(attend_back_kernel, group),
        out_shape=jax.ShapeDtypeStruct((blocks, loc, cols), BF16),
        in_specs=[SMEM] + [VMEM] * 6,
        out_specs=VMEM,
        scratch_shapes=[pltpu.VMEM((total, HEAD_DIM), BF16)] * 2 + [pltpu.VMEM((total, HEAD_DIM), F32)] * 2,
        compiler_params=params(60),
        cost_estimate=cost(),
    )(at, rec, grad, full, lse, cosine, sine)


def out_kernel(kv, mix_ref, w_ref, cat_ref, *outs):
    cols = mix_ref.shape[2]
    for s, out in enumerate(outs):
        cat_ref[s] = jnp.concatenate([mix_ref[s * kv + n] for n in range(kv)], axis=1)
        out[...] = dot(cat_ref[s], w_ref[...]).astype(BF16)


def out_project(mixed, w_out, seqs):
    units, loc, cols = mixed.shape
    kv = units // seqs
    width = w_out.shape[1]
    res = pl.pallas_call(
        functools.partial(out_kernel, kv),
        out_shape=(jax.ShapeDtypeStruct((seqs, loc, kv * cols), BF16),)
        + (jax.ShapeDtypeStruct((loc, width), BF16),) * seqs,
        in_specs=[VMEM] * 2,
        out_specs=(VMEM,) * (seqs + 1),
        compiler_params=params(24),
        cost_estimate=cost(),
    )(mixed, w_out)
    return res[0], res[1:]


def input_grads_kernel(seqs, kv, groups, back_ref, x_ref, wq_ref, wk_ref, wv_ref, *refs):
    gain_refs, outs, (rows_ref, inv_ref, attn_ref) = refs[:seqs], refs[seqs:seqs + groups], refs[seqs + groups:]
    per = seqs // groups
    loc, width = x_ref.shape[1], x_ref.shape[2]
    group = wq_ref.shape[1] // (kv * HEAD_DIM)
    gather(back_ref, rows_ref, seqs, kv, group)
    at_k = kv * group * HEAD_DIM
    at_v = at_k + kv * HEAD_DIM
    for s in range(seqs):
        x = x_ref[s].astype(F32)
        inv = lax.rsqrt(jnp.mean(x * x, axis=-1, keepdims=True) + EPS)
        inv_ref[s * loc:(s + 1) * loc, :] = jnp.broadcast_to(inv, (loc, HEAD_DIM))
    tile = 512
    for t in range(width // tile):
        span = slice(t * tile, (t + 1) * tile)
        grad = dot_rt(rows_ref[:, :at_k], wq_ref[span, :])
        grad += dot_rt(rows_ref[:, at_k:at_v], wk_ref[span, :])
        grad += dot_rt(rows_ref[:, at_v:], wv_ref[span, :])
        total = 0.0
        for s in range(seqs):
            part = grad[s * loc:(s + 1) * loc]
            at = (s % per) * loc
            outs[s // per][at:at + loc, span] = part.astype(BF16)
            unit = x_ref[s, :, span].astype(F32) * inv_ref[s * loc:(s + 1) * loc, :1]
            total = total + jnp.sum(part * unit, axis=0, keepdims=True)
        attn_ref[:, span] = total
    mlp = sum(ref[...] for ref in gain_refs)
    lines = []
    for gain in (attn_ref[...], mlp):
        high = gain.astype(BF16).astype(F32)
        lines += [high, gain - high]
    row = lax.broadcasted_iota(jnp.int32, (16, width), 0)
    extra = jnp.zeros((16, width), F32)
    for i, gain in enumerate(lines):
        extra = jnp.where(row == i, gain, extra)
    outs[0][per * loc:, :] = extra.astype(BF16)


def gather(back_ref, rows_ref, seqs, kv, group):
    loc = back_ref.shape[1]
    wide = group * HEAD_DIM
    for s in range(seqs):
        for n in range(kv):
            span = slice(s * loc, (s + 1) * loc)
            rows_ref[span, n * wide:(n + 1) * wide] = back_ref[s * kv + n, :, :wide]
            for i in range(2):
                at = kv * wide + (i * kv + n) * HEAD_DIM
                rows_ref[span, at:at + HEAD_DIM] = back_ref[s * kv + n, :, wide + i * HEAD_DIM:wide + (i + 1) * HEAD_DIM]


def input_grads(back, x, wq, wk, wv, gains, groups):
    seqs, loc, width = x.shape
    kv = wk.shape[1] // HEAD_DIM
    cols = wq.shape[1] + 2 * wk.shape[1]
    rows = seqs * loc // groups
    return pl.pallas_call(
        functools.partial(input_grads_kernel, seqs, kv, groups),
        out_shape=(jax.ShapeDtypeStruct((rows + 16, width), BF16),) + (jax.ShapeDtypeStruct((rows, width), BF16),) * (groups - 1),
        in_specs=[VMEM] * (5 + seqs),
        out_specs=(VMEM,) * groups,
        scratch_shapes=[
            pltpu.VMEM((seqs * loc, cols), BF16),
            pltpu.VMEM((seqs * loc, HEAD_DIM), F32),
            pltpu.VMEM((1, width), F32),
        ],
        compiler_params=params(60),
        cost_estimate=cost(),
    )(back, x, wq, wk, wv, *gains)


def shares_call(body, fixed, tall, cols, scratch, core, shares):
    width = tall[0].shape[-1]
    tile = width // shares

    def mine(step, keep, core_ref):
        return 2 * step + jnp.where(keep == 0, 1 - core_ref[0], core_ref[0])

    def tall_spec(a):
        lead = (0,) * (a.ndim - 1)
        return pl.BlockSpec(a.shape[:-1] + (tile,), lambda i, k, c: lead + (mine(i, k, c),))

    out = pl.BlockSpec((1, tile, cols), lambda i, k, c: (i, 0, 0))
    return pl.pallas_call(
        body,
        grid_spec=pltpu.PrefetchScalarGridSpec(
            num_scalar_prefetch=1,
            grid=(shares // 2, 2),
            in_specs=[pl.BlockSpec(a.shape, lambda i, k, c, n=a.ndim: (0,) * n) for a in fixed] + [tall_spec(a) for a in tall],
            out_specs=(out, out),
            scratch_shapes=scratch,
        ),
        out_shape=(jax.ShapeDtypeStruct((shares // 2, tile, cols), BF16),) * 2,
        compiler_params=params(60),
        cost_estimate=cost(),
    )(core, *fixed, *tall)


def put_share(send_ref, keep_ref, pieces):
    def store(ref):
        at = 0
        for piece in pieces:
            ref[0, :, at:at + piece.shape[1]] = piece.astype(BF16)
            at += piece.shape[1]

    @pl.when(pl.program_id(1) == 0)
    def _():
        store(send_ref)

    @pl.when(pl.program_id(1) == 1)
    def _():
        store(keep_ref)


def attn_grads_kernel(seqs, kv, group, core_ref, back_ref, mix_ref, norm_ref, *refs):
    grad_refs, (send_ref, keep_ref, rows_ref) = refs[:seqs], refs[seqs:]

    @pl.when((pl.program_id(0) == 0) & (pl.program_id(1) == 0))
    def _():
        gather(back_ref, rows_ref, seqs, kv, group)

    rows = rows_ref.shape[0]
    left = norm_ref[...].reshape(rows, norm_ref.shape[2])
    grad = jnp.concatenate([ref[...] for ref in grad_refs], axis=0)
    mixed = mix_ref[...].reshape(rows, mix_ref.shape[2])
    put_share(send_ref, keep_ref, [dot_lt(left, rows_ref[...]), dot_lt(grad, mixed)])


def attn_grads(core, back, mixed, normed, g_attns, kv, shares):
    seqs, loc, width = normed.shape
    group = back.shape[2] // HEAD_DIM - 2
    cols = kv * back.shape[2]
    scratch = [pltpu.VMEM((seqs * loc, cols), BF16)]
    body = functools.partial(attn_grads_kernel, seqs, kv, group)
    return shares_call(body, (back, mixed), (normed,) + tuple(g_attns), cols + mixed.shape[2], scratch, core, shares)


def ffn_grads_kernel(seqs, count, core_ref, *refs):
    rights, lefts = refs[:count * seqs], refs[count * seqs:-3]
    send_ref, keep_ref, right_ref = refs[-3:]
    lefts = [ref for ref in lefts if len(ref.shape) == 2 and ref.shape[1] < right_ref.shape[2]]

    @pl.when((pl.program_id(0) == 0) & (pl.program_id(1) == 0))
    def _():
        loc = rights[0].shape[0]
        for i in range(count):
            for s in range(seqs):
                right_ref[i, s * loc:(s + 1) * loc, :] = rights[i * seqs + s][...]

    left = jnp.concatenate([ref[...] for ref in lefts], axis=0)
    put_share(send_ref, keep_ref, [dot_lt(left, right_ref[i]) for i in range(count)])


def ffn_grads(core, rights, lefts, before, total, shares):
    seqs, count = len(rights[0]), len(rights)
    loc, units = rights[0][0].shape
    width = lefts[0].shape[1]
    tile = width // shares
    start = total - count if before else 0
    fixed = sum((tuple(r) for r in rights), ())
    left = [pl.BlockSpec((a.shape[0], tile), lambda i, k, c: (0, 2 * i + jnp.where(k == 0, 1 - c[0], c[0]))) for a in lefts]
    out = pl.BlockSpec((1, tile, count * units), lambda i, k, c: (i, 0, start // count))
    args = fixed + tuple(lefts) + tuple(before)
    return pl.pallas_call(
        functools.partial(ffn_grads_kernel, seqs, count),
        grid_spec=pltpu.PrefetchScalarGridSpec(
            num_scalar_prefetch=1,
            grid=(shares // 2, 2),
            in_specs=[pl.BlockSpec((loc, units), lambda i, k, c: (0, 0))] * len(fixed)
            + left
            + [pl.BlockSpec(memory_space=pl.ANY)] * len(before),
            out_specs=(out, out),
            scratch_shapes=[pltpu.VMEM((count, seqs * loc, units), BF16)],
        ),
        out_shape=(jax.ShapeDtypeStruct((shares // 2, tile, total * units), BF16),) * 2,
        input_output_aliases={len(args) - 1: 0, len(args): 1} if before else {},
        compiler_params=params(60),
        cost_estimate=cost(),
    )(core, *args)


def fold_two_kernel(place_ref, *refs):
    keeps, gots, outs = refs[:4], refs[4:8], refs[8:]
    for keep, got, out in zip(keeps, gots, outs):
        out[0] = (keep[0, 0].astype(F32) + got[0, 0].astype(F32)).astype(BF16)


def fold_two(place, keep, got):
    _, rows, cols = keep.shape
    half = rows // 2
    keep, got = keep.reshape(2, 2, rows, cols), got.reshape(2, 2, rows, cols)
    tile = half // 2
    ins = []
    for own in (0, 1):
        ins.append(pl.BlockSpec((1, 1, tile, cols), lambda i, j, p, own=own: (i, jnp.where(own == 1, p[0], 1 - p[0]), j, 0)))
    for own in (0, 1):
        ins.append(pl.BlockSpec((1, 1, tile, cols), lambda i, j, p, own=own: (jnp.where(own == 1, p[1], 1 - p[1]), i, j + 2, 0)))
    return pl.pallas_call(
        fold_two_kernel,
        grid_spec=pltpu.PrefetchScalarGridSpec(
            num_scalar_prefetch=1,
            grid=(2, 2),
            in_specs=ins + ins,
            out_specs=(pl.BlockSpec((1, tile, cols), lambda i, j, p: (i, j, 0)),) * 4,
        ),
        out_shape=(jax.ShapeDtypeStruct((2, half, cols), BF16),) * 4,
        compiler_params=params(60),
        cost_estimate=cost(),
    )(place, keep, keep, keep, keep, got, got, got, got)


def fold_three(place, upper, upper_got, lower, lower_got):
    _, half, cols = upper.shape
    tile = half // 2
    ins = []
    for axis in (1, 0):
        for own in (0, 1):
            ins.append(pl.BlockSpec((1, 1, tile, cols), lambda j, p, own=own, axis=axis: (0, jnp.where(own == 1, p[axis], 1 - p[axis]), j, 0)))
    flat = pl.BlockSpec((1, tile, cols), lambda j, p: (0, j, 0))
    u, ug, l, lg = (a[None] for a in (upper, upper_got, lower, lower_got))
    res = pl.pallas_call(
        fold_two_kernel,
        grid_spec=pltpu.PrefetchScalarGridSpec(
            num_scalar_prefetch=1, grid=(2,), in_specs=ins + ins, out_specs=(flat,) * 4
        ),
        out_shape=(jax.ShapeDtypeStruct((1, half, cols), BF16),) * 4,
        compiler_params=params(60),
        cost_estimate=cost(),
    )(place, u, u, l, l, ug, ug, lg, lg)
    return [a[0] for a in res]


def fold_four_kernel(widths, upper, upper_got, lower, lower_got, *outs):
    half = upper.shape[0]
    for at, (one, two) in enumerate(((upper, upper_got), (lower, lower_got))):
        start = 0
        for out, width in zip(outs, widths):
            part = one[:, start:start + width].astype(F32) + two[:, start:start + width].astype(F32)
            if out is outs[-1]:
                out[:, at * half:(at + 1) * half] = part.T
            else:
                out[at * half:(at + 1) * half, :] = part
            start += width


def fold_four(widths, upper, upper_got, lower, lower_got):
    rows = 2 * upper.shape[0]
    shapes = [(rows, w) for w in widths[:-1]] + [(widths[-1], rows)]
    return pl.pallas_call(
        functools.partial(fold_four_kernel, widths),
        out_shape=tuple(jax.ShapeDtypeStruct(shape, F32) for shape in shapes),
        in_specs=[VMEM] * 4,
        out_specs=(VMEM,) * len(widths),
        compiler_params=params(60),
        cost_estimate=cost(),
    )(upper, upper_got, lower, lower_got)


def finish_kernel(seqs, mid_ref, x_ref, gain_ref, *refs):
    inner, ends, resids, out_ref = refs[:seqs], refs[seqs:2 * seqs], refs[2 * seqs:3 * seqs], refs[3 * seqs]
    gain = gain_ref[...].astype(F32)
    for s in range(seqs):
        grad = jnp.where(mid_ref[0] == 1, inner[s][...].astype(F32), ends[s][...].astype(F32))
        x = x_ref[s].astype(F32)
        inv = lax.rsqrt(jnp.mean(x * x, axis=-1, keepdims=True) + EPS)
        unit = x * inv
        scaled = grad * gain
        back = inv * (scaled - unit * jnp.mean(scaled * unit, axis=-1, keepdims=True))
        out_ref[:, s, :] = resids[s][...] + back


def by_seq(group, seqs, loc, tile):
    per = seqs // len(group)
    return [
        (group[s // per], pl.BlockSpec((tile, group[0].shape[1]), lambda i, at=(s % per) * (loc // tile): (i + at, 0)))
        for s in range(seqs)
    ]


def finish(mid, x, gain, inner, ends, resids):
    seqs, loc, width = x.shape
    tile = 32
    parts = by_seq(inner, seqs, loc, tile) + by_seq(ends, seqs, loc, tile) + by_seq(resids, seqs, loc, tile)
    return pl.pallas_call(
        functools.partial(finish_kernel, seqs),
        grid=(loc // tile,),
        out_shape=jax.ShapeDtypeStruct((loc, seqs, width), F32),
        in_specs=[SMEM, pl.BlockSpec((seqs, tile, width), lambda i: (0, i, 0)), pl.BlockSpec((1, width), lambda i: (0, 0))]
        + [spec for _, spec in parts],
        out_specs=pl.BlockSpec((tile, seqs, width), lambda i: (i, 0, 0)),
        compiler_params=params(60),
        cost_estimate=cost(),
    )(mid, x, gain, *(a for a, _ in parts))


def output_kernel(seqs, mid_ref, x_ref, *refs):
    attn, inner, ends, out_ref, wide = refs[:seqs], refs[seqs:2 * seqs], refs[2 * seqs:3 * seqs], refs[3 * seqs], refs[3 * seqs + 1]
    for s in range(seqs):
        down = jnp.where(mid_ref[0] == 1, inner[s][...].astype(F32), ends[s][...].astype(F32))
        wide[:, s, :] = x_ref[s].astype(F32) + attn[s][...].astype(F32) + down
    out_ref[...] = wide[...].astype(BF16)


def block_output(mid, x, attn, inner, ends):
    seqs, loc, width = x.shape
    tile = 32
    parts = by_seq(attn, seqs, loc, tile) + by_seq(inner, seqs, loc, tile) + by_seq(ends, seqs, loc, tile)
    return pl.pallas_call(
        functools.partial(output_kernel, seqs),
        grid=(loc // tile,),
        out_shape=jax.ShapeDtypeStruct((loc, seqs, width), BF16),
        in_specs=[SMEM, pl.BlockSpec((seqs, tile, width), lambda i: (0, i, 0))] + [spec for _, spec in parts],
        out_specs=pl.BlockSpec((tile, seqs, width), lambda i: (i, 0, 0)),
        scratch_shapes=[pltpu.VMEM((tile, seqs, width), F32)],
        compiler_params=params(60),
        cost_estimate=cost(),
    )(mid, x, *(a for a, _ in parts))


def add_kernel(left, right, out):
    out[...] = (left[...].astype(F32) + right[...].astype(F32)).astype(BF16)


def add(left, right):
    return pl.pallas_call(
        add_kernel,
        out_shape=jax.ShapeDtypeStruct(left.shape, BF16),
        in_specs=[VMEM, VMEM],
        out_specs=VMEM,
        compiler_params=params(16),
        cost_estimate=cost(),
    )(left, right)


def rope_tables(positions, head_dim):
    half = head_dim // 2
    freq = jnp.exp(jnp.arange(half, dtype=jnp.float32) * (-2.0 * math.log(THETA) / head_dim))
    angles = positions.astype(jnp.float32)[:, None] * freq[None, :]
    return (jnp.cos(angles), jnp.sin(angles))


def rotate(values, cosine, sine):
    half = values.shape[-1] // 2
    first = values[..., :half]
    second = values[..., half:]
    cosine = cosine[:, None, None, :]
    sine = sine[:, None, None, :]
    return jnp.concatenate(
        [first * cosine - second * sine, second * cosine + first * sine], axis=-1
    )


def inverse_rms(values):
    return lax.rsqrt(jnp.mean(values * values, axis=-1, keepdims=True) + EPS)


def norm_back(values, inverse, gain, grad):
    unit = values * inverse
    scaled = grad * gain
    back = inverse * (scaled - unit * jnp.mean(scaled * unit, axis=-1, keepdims=True))
    return (back, jnp.sum(grad * unit, axis=(0, 1)))


def matmul(values, weight):
    return jnp.einsum("lsd,de->lse", values, weight, preferred_element_type=jnp.float32)


def matmul_back(values, weight):
    return jnp.einsum("lse,de->lsd", values, weight, preferred_element_type=jnp.float32)


def weight_grad(left, right):
    return jnp.einsum("lsd,lse->de", left, right, preferred_element_type=jnp.float32)


def general(
    hidden_in,
    block_order,
    seq_labels,
    exit_scales,
    attn_gain,
    w_query,
    w_key,
    w_value,
    w_out,
    mlp_gain,
    w_gate,
    w_up,
    w_down,
    d_out,
):
    f32 = jnp.float32
    bf16 = jnp.bfloat16
    loc, seqs, width = hidden_in.shape
    head_dim = HEAD_DIM
    q_heads = w_query.shape[1] // head_dim
    kv_heads = w_key.shape[1] // head_dim
    group = q_heads // kv_heads
    scale = head_dim ** (-0.5)
    blocks_all = block_order.shape[0]
    total_rows = loc * lax.axis_size("blk")
    key_rows = math.gcd(512, total_rows)
    block_count = total_rows // key_rows
    kv_width = 2 * kv_heads * head_dim
    positions = block_order[lax.axis_index("blk")] * loc + jnp.arange(loc, dtype=jnp.int32)
    cosine, sine = rope_tables(positions, head_dim)

    def key_positions(start, count):
        index = start + jnp.arange(count, dtype=jnp.int32)
        owner = index // loc
        table = jnp.sum(
            jnp.where(
                owner[:, None] == jnp.arange(blocks_all, dtype=jnp.int32)[None, :],
                block_order[None, :],
                0,
            ),
            axis=1,
        )
        return table * loc + index % loc

    xin = hidden_in.astype(f32)
    inv_a = inverse_rms(xin)
    gain_a = attn_gain.astype(f32)
    normed = (xin * inv_a * gain_a).astype(bf16)
    query_bf = rotate(
        matmul(normed, w_query).reshape(loc, seqs, q_heads, head_dim), cosine, sine
    ).astype(bf16)
    keys_bf = (
        rotate(matmul(normed, w_key).reshape(loc, seqs, kv_heads, head_dim), cosine, sine)
        .astype(bf16)
        .reshape(loc, seqs, kv_heads * head_dim)
    )
    vals_bf = matmul(normed, w_value).astype(bf16)
    query_g = query_bf.reshape(loc, seqs, kv_heads, group, head_dim)
    starts = jnp.arange(block_count, dtype=jnp.int32) * key_rows
    top = jnp.full((seqs, kv_heads, group, loc), NEG, f32)
    key_part = lax.all_gather(keys_bf, "blk", axis=0, tiled=True)
    val_part = lax.all_gather(vals_bf, "blk", axis=0, tiled=True)
    count = key_part.shape[0]
    kk = key_part.reshape(count, seqs, kv_heads, head_dim)
    vv = val_part.reshape(count, seqs, kv_heads, head_dim)
    mask = key_positions(jnp.int32(0), count)[None, :] <= positions[:, None]
    raw = jnp.einsum("lsngd,msnd->snglm", query_g, kk, preferred_element_type=f32)
    scores = jnp.where(mask, raw * scale, NEG)
    new_top = jnp.maximum(top, jnp.max(scores, axis=-1))
    weights = jnp.where(mask, jnp.exp(scores - new_top[..., None]), 0.0)
    total = jnp.sum(weights, axis=-1)
    acc = jnp.einsum("snglm,msnd->sngld", weights.astype(bf16), vv, preferred_element_type=f32)
    top, total, acc = (new_top, total, acc)
    lse = top + jnp.log(total)
    mixed_raw = acc / total[..., None]
    mixed_bf = (
        mixed_raw.transpose(3, 0, 1, 2, 4).reshape(loc, seqs, q_heads * head_dim).astype(bf16)
    )
    resid = xin + lax.psum(matmul(mixed_bf, w_out).astype(jnp.bfloat16), "tp").astype(jnp.float32)
    inv_m = inverse_rms(resid)
    gain_m = mlp_gain.astype(f32)
    normed_m = (resid * inv_m * gain_m).astype(bf16)
    gate = matmul(normed_m, w_gate)
    up = matmul(normed_m, w_up)
    sig = jax.nn.sigmoid(gate)
    silu = gate * sig
    hidden = (silu * up).astype(bf16)
    output = resid + lax.psum(matmul(hidden, w_down).astype(jnp.bfloat16), "tp").astype(jnp.float32)
    block_out = output.astype(bf16)
    scale_rows = jnp.where(seq_labels == 1, exit_scales[1], exit_scales[0])
    cot = d_out.astype(f32) * scale_rows[None, :, None]
    g_down = cot.astype(bf16)
    d_w_down = weight_grad(hidden, g_down)
    d_hidden = matmul_back(g_down, w_down)
    g_up = (d_hidden * silu).astype(bf16)
    g_gate = (d_hidden * up * (sig * (1.0 + gate * (1.0 - sig)))).astype(bf16)
    d_w_gate = weight_grad(normed_m, g_gate)
    d_w_up = weight_grad(normed_m, g_up)
    d_nm = lax.psum(
        (matmul_back(g_gate, w_gate) + matmul_back(g_up, w_up)).astype(jnp.bfloat16), "tp"
    ).astype(jnp.float32)
    d_resid_norm, d_mlp_gain = norm_back(resid, inv_m, gain_m, d_nm)
    d_resid = cot + d_resid_norm
    g_attn = d_resid.astype(bf16)
    d_w_out = weight_grad(mixed_bf, g_attn)
    g_mixed = matmul_back(g_attn, w_out).astype(bf16)
    g_mixed_g = g_mixed.reshape(loc, seqs, kv_heads, group, head_dim)
    delta = jnp.sum(g_mixed_g.astype(f32).transpose(1, 2, 3, 0, 4) * mixed_raw, axis=-1)
    whole_keys, whole_vals = (
        lax.all_gather(keys_bf, "blk", axis=0, tiled=True),
        lax.all_gather(vals_bf, "blk", axis=0, tiled=True),
    )

    def probe(kk, vv, start, count):
        mask = key_positions(start, count)[None, :] <= positions[:, None]
        raw = jnp.einsum("lsngd,msnd->snglm", query_g, kk, preferred_element_type=f32)
        probs = jnp.where(mask, jnp.exp(raw * scale - lse[..., None]), 0.0)
        d_probs = jnp.einsum("lsngd,msnd->snglm", g_mixed_g, vv, preferred_element_type=f32)
        g_scores = (probs * (d_probs - delta[..., None]) * scale).astype(bf16)
        return (g_scores, probs)

    def kv_pair(g_scores, probs, count):
        d_keys = jnp.einsum("snglm,lsngd->msnd", g_scores, query_g, preferred_element_type=f32)
        d_vals = jnp.einsum(
            "snglm,lsngd->msnd", probs.astype(bf16), g_mixed_g, preferred_element_type=f32
        )
        return jnp.concatenate([d_keys, d_vals], axis=2).reshape(count, seqs, kv_width)

    scan_items = (
        whole_keys.reshape(block_count, key_rows, seqs, -1),
        whole_vals.reshape(block_count, key_rows, seqs, -1),
        starts,
    )
    zero_query = jnp.zeros((loc, seqs, kv_heads, group, head_dim), f32)

    def back_step(d_query, item):
        key_part, val_part, start = item
        kk = key_part.reshape(key_rows, seqs, kv_heads, head_dim)
        vv = val_part.reshape(key_rows, seqs, kv_heads, head_dim)
        g_scores, probs = probe(kk, vv, start, key_rows)
        d_query = d_query + jnp.einsum(
            "snglm,msnd->lsngd", g_scores, kk, preferred_element_type=f32
        )
        return (d_query, kv_pair(g_scores, probs, key_rows))

    d_query, kv_terms = lax.scan(back_step, zero_query, scan_items)
    kv_local = lax.psum_scatter(
        kv_terms.reshape(total_rows, seqs, kv_width).astype(jnp.bfloat16),
        "blk",
        scatter_dimension=0,
        tiled=True,
    ).astype(jnp.float32)
    kv_local = kv_local.reshape(loc, seqs, 2, kv_heads, head_dim)
    g_q = (
        rotate(d_query.reshape(loc, seqs, q_heads, head_dim), cosine, -sine)
        .astype(bf16)
        .reshape(loc, seqs, q_heads * head_dim)
    )
    g_k = (
        rotate(kv_local[:, :, 0], cosine, -sine)
        .astype(bf16)
        .reshape(loc, seqs, kv_heads * head_dim)
    )
    g_v = kv_local[:, :, 1].astype(bf16).reshape(loc, seqs, kv_heads * head_dim)
    d_w_query = weight_grad(normed, g_q)
    d_w_key = weight_grad(normed, g_k)
    d_w_value = weight_grad(normed, g_v)
    d_n = lax.psum(
        (matmul_back(g_q, w_query) + matmul_back(g_k, w_key) + matmul_back(g_v, w_value)).astype(
            jnp.bfloat16
        ),
        "tp",
    ).astype(jnp.float32)
    d_in_norm, d_attn_gain = norm_back(xin, inv_a, gain_a, d_n)
    d_hidden_in = d_resid + d_in_norm
    d_attn_gain, d_w_query, d_w_key, d_w_value, d_w_out, d_mlp_gain, d_w_gate, d_w_up, d_w_down = (
        lax.psum_scatter(
            d_attn_gain.astype(jnp.bfloat16), "blk", scatter_dimension=0, tiled=True
        ).astype(jnp.float32),
        lax.psum_scatter(
            d_w_query.astype(jnp.bfloat16), "blk", scatter_dimension=0, tiled=True
        ).astype(jnp.float32),
        lax.psum_scatter(
            d_w_key.astype(jnp.bfloat16), "blk", scatter_dimension=0, tiled=True
        ).astype(jnp.float32),
        lax.psum_scatter(
            d_w_value.astype(jnp.bfloat16), "blk", scatter_dimension=0, tiled=True
        ).astype(jnp.float32),
        lax.psum_scatter(
            d_w_out.astype(jnp.bfloat16), "blk", scatter_dimension=1, tiled=True
        ).astype(jnp.float32),
        lax.psum_scatter(
            d_mlp_gain.astype(jnp.bfloat16), "blk", scatter_dimension=0, tiled=True
        ).astype(jnp.float32),
        lax.psum_scatter(
            d_w_gate.astype(jnp.bfloat16), "blk", scatter_dimension=0, tiled=True
        ).astype(jnp.float32),
        lax.psum_scatter(
            d_w_up.astype(jnp.bfloat16), "blk", scatter_dimension=0, tiled=True
        ).astype(jnp.float32),
        lax.psum_scatter(
            d_w_down.astype(jnp.bfloat16), "blk", scatter_dimension=1, tiled=True
        ).astype(jnp.float32),
    )
    return (
        block_out,
        d_hidden_in,
        d_attn_gain,
        d_w_query,
        d_w_key,
        d_w_value,
        d_w_out,
        d_mlp_gain,
        d_w_gate,
        d_w_up,
        d_w_down,
    )


class Steps:
    def __init__(self):
        self.last = None

    def enter(self, *values):
        if self.last is not None:
            values, _ = lax.optimization_barrier((values, self.last))
        return values if len(values) > 1 else values[0]

    def leave(self, value):
        self.last = value
        return value


class Line:
    def __init__(self, steps, middle, parts):
        self.steps, self.middle, self.parts = steps, middle, list(parts)
        count = len(self.parts)
        self.first, self.half, self.second, self.total, self.third, self.done = ([None] * count for _ in range(6))

    def one(self, c):
        self.first[c] = lax.ppermute(self.parts[c], "tp", [(0, 1), (3, 2)])

    def two(self, c):
        part, got = self.steps.enter(self.parts[c], self.first[c])
        self.half[c] = self.steps.leave(add(part, got))
        self.second[c] = lax.ppermute(self.half[c], "tp", [(1, 2), (2, 1)])

    def three(self, c):
        half, got = self.steps.enter(self.half[c], self.second[c])
        self.total[c] = self.steps.leave(add(half, got))
        self.third[c] = lax.ppermute(self.total[c], "tp", [(1, 0), (2, 3)])

    def four(self, c):
        total, got = self.steps.enter(self.total[c], self.third[c])
        self.done[c] = self.steps.leave(jnp.where(self.middle, total, got))

    def five(self, c):
        self.third[c] = self.steps.leave(self.steps.enter(self.third[c]))


def partner(bit):
    return [(i, i ^ bit) for i in range(8)]


class Scatter:
    def __init__(self, steps, place, send, keep):
        self.steps, self.place, self.send, self.keep = steps, place, send, keep

    def one_go(self):
        self.got = lax.ppermute(self.steps.enter(self.send), "blk", partner(1))

    def two(self):
        keep, got = self.steps.enter(self.keep, self.got)
        self.away, self.upper, self.off, self.lower = fold_two(self.place, keep, got)
        self.steps.leave(self.upper)

    def two_go(self, first=2, second=4):
        away, off = self.steps.enter(self.away, self.off)
        self.upper_got = lax.ppermute(away, "blk", partner(first))
        self.lower_got = lax.ppermute(off, "blk", partner(second))

    def three(self):
        values = self.steps.enter(self.upper, self.upper_got, self.lower, self.lower_got)
        self.away, self.upper, self.off, self.lower = fold_three(self.place, *values)
        self.steps.leave(self.upper)

    def three_go(self):
        self.two_go(4, 2)

    def four(self, widths):
        values = self.steps.enter(self.upper, self.upper_got, self.lower, self.lower_got)
        res = fold_four(widths, *values)
        self.steps.leave(res[0])
        return res


def inverse(values):
    return lax.rsqrt(jnp.mean(values * values, axis=-1, keepdims=True) + EPS)


def tables(positions):
    cosine, sine = rope_tables(positions, HEAD_DIM)
    return jnp.concatenate([cosine, cosine], axis=1), jnp.concatenate([-sine, sine], axis=1)


def fast(
    hidden_in,
    block_order,
    seq_labels,
    exit_scales,
    attn_gain,
    w_query,
    w_key,
    w_value,
    w_out,
    mlp_gain,
    w_gate,
    w_up,
    w_down,
    d_out,
):
    loc, seqs, width = hidden_in.shape
    blocks = block_order.shape[0]
    rows = seqs * loc
    units = w_gate.shape[1]
    kv = w_key.shape[1] // HEAD_DIM
    group = w_query.shape[1] // w_key.shape[1]
    wide = group * HEAD_DIM
    me = lax.axis_index("blk")
    line = lax.axis_index("tp")
    middle = (line == 1) | (line == 2)
    index = jnp.arange(blocks, dtype=jnp.int32)
    at = jnp.sum(jnp.where(block_order[None, :] == index[:, None], index[None, :], 0), axis=1)
    mine = jnp.sum(jnp.where(index == me, block_order, 0)) * loc + jnp.arange(loc, dtype=jnp.int32)
    steps = Steps()
    enter, leave = steps.enter, steps.leave

    x = hidden_in.transpose(1, 0, 2)
    cosine, sine = tables(mine)
    messages, normed = project(x, attn_gain[None, :], cosine, sine, w_query, w_key, w_value)
    leave(messages)
    rec = lax.all_to_all(messages, "blk", 0, 0, tiled=True)
    scales = jnp.where(seq_labels == 1, exit_scales[1], exit_scales[0])
    cot = enter(d_out).transpose(1, 0, 2).astype(F32) * scales[:, None, None]
    g_down = leave(cot.astype(BF16).reshape(rows, width))
    d_hidden = leave(dot_rt(g_down, w_down).astype(BF16))
    mixed, full, lse = attend(at, enter(rec), group)
    leave(mixed)
    mixed = lax.all_to_all(mixed, "blk", 0, 0, tiled=True)
    all_cosine, all_sine = tables(enter(jnp.arange(blocks * loc, dtype=jnp.int32)))
    leave(all_cosine)
    mixed, parts = out_project(enter(mixed), w_out, seqs)
    leave(mixed)

    gain_m = mlp_gain.astype(F32)
    attn = Line(steps, middle, parts)
    back = Line(steps, middle, [None] * seqs)
    norms, hiddens, gates, ups, gains = ([None] * seqs for _ in range(5))

    def feed(s):
        total = attn.done[s]
        resid = x[s].astype(F32) + total.astype(F32)
        unit = resid * inverse(resid)
        norm = (unit * gain_m).astype(BF16)
        gate = dot(norm, w_gate)
        up = dot(norm, w_up)
        sig = jax.nn.sigmoid(gate)
        silu = gate * sig
        grad_h = d_hidden[s * loc:(s + 1) * loc].astype(F32)
        g_up = (grad_h * silu).astype(BF16)
        g_gate = (grad_h * up * (sig * (1.0 + gate * (1.0 - sig)))).astype(BF16)
        grad = dot_rt(g_gate, w_gate) + dot_rt(g_up, w_up)
        gains[s] = jnp.sum(grad * unit, axis=0)
        back.parts[s] = leave(grad.astype(BF16))
        norms[s], gates[s], ups[s] = norm, g_gate, g_up
        hiddens[s] = (silu * up).astype(BF16)

    d_resids, g_attns, sends = ([None] * seqs for _ in range(3))

    def norm_back(s):
        resid = x[s].astype(F32) + attn.done[s].astype(F32)
        inv = inverse(resid)
        unit = resid * inv
        scaled = back.done[s].astype(F32) * gain_m
        d_resids[s] = cot[s] + inv * (scaled - unit * jnp.mean(scaled * unit, axis=-1, keepdims=True))
        g_attns[s] = d_resids[s].astype(BF16)
        sends[s] = leave(dot_rt(g_attns[s], w_out).astype(BF16))

    def run(lines, *texts):
        for word in " ".join(texts).split():
            name, c = word[:-1], int(word[-1])
            if name == "F":
                feed(c)
            elif name == "N":
                norm_back(c)
            elif name == "O":
                hidden = jnp.concatenate(enter(hiddens[2 * c:2 * c + 2]), axis=0)
                outs.parts[c] = leave(dot(hidden, w_down).astype(BF16))
            else:
                obj = lines[name[0]]
                (obj.one, obj.two, obj.three, obj.four, obj.five)[int(name[1]) - 1](c)

    outs = Line(steps, middle, [None] * 2)
    lines = {"a": attn, "b": back, "c": outs}
    core = (me % 2).astype(jnp.int32)[None]
    place = jnp.stack([(me // 2) % 2, me // 4]).astype(jnp.int32)
    run(
        lines,
        "a10 a11 a12 a13",
        "a20 a21 a30 a22",
        "a31 a40 F0 b10",
        "a23 a32 a41 F1",
        "b11",
    )
    run(
        lines,
        "a33 a42 F2 b12",
        "b20 a43 F3 b13",
        "b21 b30",
    )
    run(
        lines,
        "O0 O1 b22 b31",
        "b40 N0 b23 b32",
        "b41 N1 b33 b42",
        "N2 b43 N3",
    )
    send = jnp.stack(enter(sends)).reshape(seqs, loc, kv, wide).transpose(0, 2, 1, 3).reshape(seqs * kv, loc, wide)
    grad = lax.all_to_all(send, "blk", 0, 0, tiled=True)
    made = leave(ffn_grads(core, *enter([gates, ups], norms), (), 3, blocks))
    run(lines, "c10 c11 c20")
    grads = leave(attend_back(at, rec, enter(grad), full, lse, all_cosine, all_sine, group))
    grads = lax.all_to_all(grads, "blk", 0, 0, tiled=True)
    send, keep = ffn_grads(core, *enter([hiddens], [g_down], made), 3, blocks)
    leave(keep)
    ffn_sum = Scatter(steps, place, send, keep)
    run(lines, "c21 c30")

    grads = enter(grads)
    parts = input_grads(grads, x, w_query, w_key, w_value, [g[None, :] for g in gains], 2)
    ins = Line(steps, middle, parts)
    leave(ins.parts[0])
    lines["d"] = ins
    run(lines, "d10 d11")
    ffn_sum.one_go()
    send, keep = attn_grads(*enter(core, grads, mixed, normed, g_attns), kv, blocks)
    leave(keep)
    attn_sum = Scatter(steps, place, send, keep)
    ffn_sum.two()
    ffn_sum.two_go()
    run(lines, "c31 c50 d20")
    attn_sum.one_go()
    run(lines, "d21 d30")
    attn_sum.two()
    attn_sum.two_go()
    ffn_sum.three()
    ffn_sum.three_go()
    run(lines, "c51")
    mid = middle.astype(jnp.int32)[None]
    block_out = leave(block_output(mid, x, attn.done, enter(outs.total), outs.third))
    attn_sum.three()
    run(lines, "d31")
    attn_sum.three_go()
    run(lines, "d40")
    extra = ins.done[0][2 * loc:2 * loc + 4].astype(F32)
    both = (extra[0::2] + extra[1::2]).reshape(2, 8, width // 8)
    both = leave(both + lax.ppermute(both, "blk", partner(1)))
    others = [lax.ppermute(enter(both), "blk", partner(bit)) for bit in (2, 4, 6)]
    d_w_gate, d_w_up, d_w_down = ffn_sum.four((units, units, units))
    run(lines, "d51")
    d_hidden_in = finish(
        mid,
        x,
        attn_gain[None, :],
        ins.total,
        ins.third,
        d_resids,
    )
    leave(d_hidden_in)
    d_w_query, d_w_key, d_w_value, d_w_out = attn_sum.four((kv * wide, kv * HEAD_DIM, kv * HEAD_DIM, kv * wide))
    others = enter(others)
    both = both + others[0] + others[1] + others[2]
    both = lax.dynamic_index_in_dim(both, me, 1, keepdims=False)
    return (
        block_out,
        d_hidden_in,
        both[0],
        d_w_query,
        d_w_key,
        d_w_value,
        d_w_out,
        both[1],
        d_w_gate,
        d_w_up,
        d_w_down,
    )


def per_device(*args):
    seqs = args[0].shape[1]
    kv_heads = args[6].shape[1] // HEAD_DIM
    fits = lax.axis_size("blk") == 8 and lax.axis_size("tp") == 4 and seqs * kv_heads == 8
    return (fast if fits else general)(*args)


def solution(mesh):
    return jax.shard_map(
        per_device,
        mesh=mesh,
        in_specs=(
            P("blk", None, None),
            P(),
            P(),
            P(),
            P(),
            P(None, "tp"),
            P(None, "tp"),
            P(None, "tp"),
            P("tp", None),
            P(),
            P(None, "tp"),
            P(None, "tp"),
            P("tp", None),
            P("blk", None, None),
        ),
        out_specs=(
            P("blk", None, None),
            P("blk", None, None),
            P("blk"),
            P("blk", "tp"),
            P("blk", "tp"),
            P("blk", "tp"),
            P("tp", "blk"),
            P("blk"),
            P("blk", "tp"),
            P("blk", "tp"),
            P("tp", "blk"),
        ),
        check_vma=False,
    )
```

```python
import functools
import math

import jax
import jax.numpy as jnp
from jax import lax
from jax.experimental import pallas as pl
from jax.experimental.pallas import tpu as pltpu
from jax.sharding import PartitionSpec as P

HEAD_DIM = 128
EPS = 1e-05
THETA = 10000.0
NEG = -1e30
F32 = jnp.float32
BF16 = jnp.bfloat16
MIB = 1024 * 1024


def dot(left, right):
    return lax.dot_general(left, right, (((1,), (0,)), ((), ())), preferred_element_type=F32)


def dot_rt(left, right):
    return lax.dot_general(left, right, (((1,), (1,)), ((), ())), preferred_element_type=F32)


def dot_lt(left, right):
    return lax.dot_general(left, right, (((0,), (0,)), ((), ())), preferred_element_type=F32)


def params(limit):
    return pltpu.CompilerParams(vmem_limit_bytes=limit * MIB)


def cost():
    return pl.CostEstimate(flops=10**9, bytes_accessed=10**6, transcendentals=0)


SMEM = pl.BlockSpec(memory_space=pltpu.SMEM)
VMEM = pl.BlockSpec(memory_space=pltpu.VMEM)


def project_kernel(heads, kv, x_ref, gain_ref, cos_ref, sin_ref, wq_ref, wk_ref, wv_ref, msg_ref, norm_ref):
    group = heads // kv
    seqs, loc, width = x_ref.shape
    gain = gain_ref[...].astype(F32)
    for s in range(seqs):
        x = x_ref[s].astype(F32)
        inv = lax.rsqrt(jnp.mean(x * x, axis=-1, keepdims=True) + EPS)
        norm_ref[s] = (x * inv * gain).astype(BF16)
    normed = norm_ref[...].reshape(seqs * loc, width)
    cosine, sine = cos_ref[...], sin_ref[...]

    def rot(t):
        return (t * cosine + pltpu.roll(t, HEAD_DIM // 2, 1) * sine).astype(BF16)

    def put(res, h, s, n, slot, turn):
        part = res[s * loc:(s + 1) * loc, h * HEAD_DIM:(h + 1) * HEAD_DIM]
        msg_ref[s * kv + n, :, slot * HEAD_DIM:(slot + 1) * HEAD_DIM] = rot(part) if turn else part.astype(BF16)

    query = dot(normed, wq_ref[...])
    for s in range(seqs):
        for h in range(heads):
            put(query, h, s, h // group, h % group, True)
    keys = dot(normed, wk_ref[...])
    for s in range(seqs):
        for n in range(kv):
            put(keys, n, s, n, group, True)
    vals = dot(normed, wv_ref[...])
    for s in range(seqs):
        for n in range(kv):
            put(vals, n, s, n, group + 1, False)


def project(x, gain, cosine, sine, wq, wk, wv):
    seqs, loc, width = x.shape
    heads, kv = wq.shape[1] // HEAD_DIM, wk.shape[1] // HEAD_DIM
    cols = (heads // kv + 2) * HEAD_DIM
    return pl.pallas_call(
        functools.partial(project_kernel, heads, kv),
        out_shape=(jax.ShapeDtypeStruct((seqs * kv, loc, cols), BF16), jax.ShapeDtypeStruct(x.shape, BF16)),
        in_specs=[VMEM] * 7,
        out_specs=(VMEM, VMEM),
        compiler_params=params(32),
        cost_estimate=cost(),
    )(x, gain, cosine, sine, wq, wk, wv)


def attend_kernel(group, at_ref, rec_ref, out_ref, full_ref, lse_ref, keys, vals):
    blocks, loc, _ = rec_ref.shape
    base = group * HEAD_DIM
    for p in range(blocks):
        i = at_ref[p]
        keys[p * loc:(p + 1) * loc, :] = rec_ref[i, :, base:base + HEAD_DIM]
        vals[p * loc:(p + 1) * loc, :] = rec_ref[i, :, base + HEAD_DIM:base + 2 * HEAD_DIM]
    rows = lax.broadcasted_iota(jnp.int32, (group * loc, loc), 0) % loc
    cols = lax.broadcasted_iota(jnp.int32, (group * loc, loc), 1)
    keep = cols <= rows
    for p in range(blocks):
        i = at_ref[p]
        count = (p + 1) * loc
        query = jnp.concatenate([rec_ref[i, :, g * HEAD_DIM:(g + 1) * HEAD_DIM] for g in range(group)], axis=0)
        scores = dot_rt(query, keys[:count, :]) * (HEAD_DIM ** -0.5)
        last = jnp.where(keep, scores[:, count - loc:], NEG)
        scores = jnp.concatenate([scores[:, :count - loc], last], axis=1) if p else last
        top = jnp.max(scores, axis=-1, keepdims=True)
        weights = jnp.exp(scores - top)
        total = jnp.sum(weights, axis=-1, keepdims=True)
        mixed = dot(weights.astype(BF16), vals[:count, :]) / total
        lse_ref[p] = jnp.broadcast_to(top + jnp.log(total), (group * loc, HEAD_DIM))
        full_ref[p] = mixed
        for g in range(group):
            out_ref[i, :, g * HEAD_DIM:(g + 1) * HEAD_DIM] = mixed[g * loc:(g + 1) * loc].astype(BF16)


def attend(at, rec, group):
    blocks, loc, _ = rec.shape
    total = blocks * loc
    return pl.pallas_call(
        functools.partial(attend_kernel, group),
        out_shape=(
            jax.ShapeDtypeStruct((blocks, loc, group * HEAD_DIM), BF16),
            jax.ShapeDtypeStruct((blocks, group * loc, HEAD_DIM), F32),
            jax.ShapeDtypeStruct((blocks, group * loc, HEAD_DIM), F32),
        ),
        in_specs=[SMEM, VMEM],
        out_specs=(VMEM,) * 3,
        scratch_shapes=[pltpu.VMEM((total, HEAD_DIM), BF16)] * 2,
        compiler_params=params(60),
        cost_estimate=cost(),
    )(at, rec)


def attend_back_kernel(group, at_ref, rec_ref, grad_ref, full_ref, lse_ref, cos_ref, sin_ref, out_ref, keys, vals, d_keys, d_vals):
    blocks, loc, _ = rec_ref.shape
    base = group * HEAD_DIM
    scale = HEAD_DIM ** -0.5
    for p in range(blocks):
        i = at_ref[p]
        keys[p * loc:(p + 1) * loc, :] = rec_ref[i, :, base:base + HEAD_DIM]
        vals[p * loc:(p + 1) * loc, :] = rec_ref[i, :, base + HEAD_DIM:base + 2 * HEAD_DIM]
    rows = lax.broadcasted_iota(jnp.int32, (group * loc, loc), 0) % loc
    cols = lax.broadcasted_iota(jnp.int32, (group * loc, loc), 1)
    keep = cols <= rows

    def unrot(t, cosine, sine):
        return (t * cosine - pltpu.roll(t, HEAD_DIM // 2, 1) * sine).astype(BF16)

    for p in reversed(range(blocks)):
        i = at_ref[p]
        count = (p + 1) * loc
        span = slice(p * loc, count)
        query = jnp.concatenate([rec_ref[i, :, g * HEAD_DIM:(g + 1) * HEAD_DIM] for g in range(group)], axis=0)
        grad = jnp.concatenate([grad_ref[i, :, g * HEAD_DIM:(g + 1) * HEAD_DIM] for g in range(group)], axis=0)
        lse = lse_ref[p][:, :1]
        delta = jnp.sum(grad.astype(F32) * full_ref[p], axis=-1, keepdims=True)
        probs = jnp.exp(dot_rt(query, keys[:count, :]) * scale - lse)
        last = jnp.where(keep, probs[:, count - loc:], 0.0)
        probs = jnp.concatenate([probs[:, :count - loc], last], axis=1) if p else last
        d_probs = dot_rt(grad, vals[:count, :])
        g_scores = (probs * (d_probs - delta) * scale).astype(BF16)
        d_query = dot(g_scores, keys[:count, :])
        dk = dot_lt(g_scores, query)
        dv = dot_lt(probs.astype(BF16), grad)
        if p == blocks - 1:
            d_keys[...] = dk
            d_vals[...] = dv
        else:
            d_keys[:count, :] += dk
            d_vals[:count, :] += dv
        cosine, sine = cos_ref[span, :], sin_ref[span, :]
        for g in range(group):
            out_ref[i, :, g * HEAD_DIM:(g + 1) * HEAD_DIM] = unrot(d_query[g * loc:(g + 1) * loc], cosine, sine)
        out_ref[i, :, base:base + HEAD_DIM] = unrot(d_keys[span, :], cosine, sine)
        out_ref[i, :, base + HEAD_DIM:base + 2 * HEAD_DIM] = d_vals[span, :].astype(BF16)


def attend_back(at, rec, grad, full, lse, cosine, sine, group):
    blocks, loc, cols = rec.shape
    total = blocks * loc
    return pl.pallas_call(
        functools.partial(attend_back_kernel, group),
        out_shape=jax.ShapeDtypeStruct((blocks, loc, cols), BF16),
        in_specs=[SMEM] + [VMEM] * 6,
        out_specs=VMEM,
        scratch_shapes=[pltpu.VMEM((total, HEAD_DIM), BF16)] * 2 + [pltpu.VMEM((total, HEAD_DIM), F32)] * 2,
        compiler_params=params(60),
        cost_estimate=cost(),
    )(at, rec, grad, full, lse, cosine, sine)


def out_kernel(kv, mix_ref, w_ref, cat_ref, *outs):
    cols = mix_ref.shape[2]
    for s, out in enumerate(outs):
        cat_ref[s] = jnp.concatenate([mix_ref[s * kv + n] for n in range(kv)], axis=1)
        out[...] = dot(cat_ref[s], w_ref[...]).astype(BF16)


def out_project(mixed, w_out, seqs):
    units, loc, cols = mixed.shape
    kv = units // seqs
    width = w_out.shape[1]
    res = pl.pallas_call(
        functools.partial(out_kernel, kv),
        out_shape=(jax.ShapeDtypeStruct((seqs, loc, kv * cols), BF16),)
        + (jax.ShapeDtypeStruct((loc, width), BF16),) * seqs,
        in_specs=[VMEM] * 2,
        out_specs=(VMEM,) * (seqs + 1),
        compiler_params=params(60),
        cost_estimate=cost(),
    )(mixed, w_out)
    return res[0], res[1:]


def input_grads_kernel(seqs, kv, groups, back_ref, x_ref, wq_ref, wk_ref, wv_ref, *refs):
    gain_refs, outs, (rows_ref, inv_ref, attn_ref) = refs[:seqs], refs[seqs:seqs + groups], refs[seqs + groups:]
    per = seqs // groups
    loc, width = x_ref.shape[1], x_ref.shape[2]
    group = wq_ref.shape[1] // (kv * HEAD_DIM)
    gather(back_ref, rows_ref, seqs, kv, group)
    at_k = kv * group * HEAD_DIM
    at_v = at_k + kv * HEAD_DIM
    for s in range(seqs):
        x = x_ref[s].astype(F32)
        inv = lax.rsqrt(jnp.mean(x * x, axis=-1, keepdims=True) + EPS)
        inv_ref[s * loc:(s + 1) * loc, :] = jnp.broadcast_to(inv, (loc, HEAD_DIM))
    tile = 512
    for t in range(width // tile):
        span = slice(t * tile, (t + 1) * tile)
        grad = dot_rt(rows_ref[:, :at_k], wq_ref[span, :])
        grad += dot_rt(rows_ref[:, at_k:at_v], wk_ref[span, :])
        grad += dot_rt(rows_ref[:, at_v:], wv_ref[span, :])
        total = 0.0
        for s in range(seqs):
            part = grad[s * loc:(s + 1) * loc]
            at = (s % per) * loc
            outs[s // per][at:at + loc, span] = part.astype(BF16)
            unit = x_ref[s, :, span].astype(F32) * inv_ref[s * loc:(s + 1) * loc, :1]
            total = total + jnp.sum(part * unit, axis=0, keepdims=True)
        attn_ref[:, span] = total
    mlp = sum(ref[...] for ref in gain_refs)
    lines = []
    for gain in (attn_ref[...], mlp):
        high = gain.astype(BF16).astype(F32)
        lines += [high, gain - high]
    row = lax.broadcasted_iota(jnp.int32, (16, width), 0)
    extra = jnp.zeros((16, width), F32)
    for i, gain in enumerate(lines):
        extra = jnp.where(row == i, gain, extra)
    outs[0][per * loc:, :] = extra.astype(BF16)


def gather(back_ref, rows_ref, seqs, kv, group):
    loc = back_ref.shape[1]
    wide = group * HEAD_DIM
    for s in range(seqs):
        for n in range(kv):
            span = slice(s * loc, (s + 1) * loc)
            rows_ref[span, n * wide:(n + 1) * wide] = back_ref[s * kv + n, :, :wide]
            for i in range(2):
                at = kv * wide + (i * kv + n) * HEAD_DIM
                rows_ref[span, at:at + HEAD_DIM] = back_ref[s * kv + n, :, wide + i * HEAD_DIM:wide + (i + 1) * HEAD_DIM]


def input_grads(back, x, wq, wk, wv, gains, groups):
    seqs, loc, width = x.shape
    kv = wk.shape[1] // HEAD_DIM
    cols = wq.shape[1] + 2 * wk.shape[1]
    rows = seqs * loc // groups
    return pl.pallas_call(
        functools.partial(input_grads_kernel, seqs, kv, groups),
        out_shape=(jax.ShapeDtypeStruct((rows + 16, width), BF16),) + (jax.ShapeDtypeStruct((rows, width), BF16),) * (groups - 1),
        in_specs=[VMEM] * (5 + seqs),
        out_specs=(VMEM,) * groups,
        scratch_shapes=[
            pltpu.VMEM((seqs * loc, cols), BF16),
            pltpu.VMEM((seqs * loc, HEAD_DIM), F32),
            pltpu.VMEM((1, width), F32),
        ],
        compiler_params=params(60),
        cost_estimate=cost(),
    )(back, x, wq, wk, wv, *gains)


def shares_call(body, fixed, tall, cols, scratch, core, shares):
    width = tall[0].shape[-1]
    tile = width // shares

    def mine(step, keep, core_ref):
        return 2 * step + jnp.where(keep == 0, 1 - core_ref[0], core_ref[0])

    def tall_spec(a):
        lead = (0,) * (a.ndim - 1)
        return pl.BlockSpec(a.shape[:-1] + (tile,), lambda i, k, c: lead + (mine(i, k, c),))

    out = pl.BlockSpec((1, tile, cols), lambda i, k, c: (i, 0, 0))
    return pl.pallas_call(
        body,
        grid_spec=pltpu.PrefetchScalarGridSpec(
            num_scalar_prefetch=1,
            grid=(shares // 2, 2),
            in_specs=[pl.BlockSpec(a.shape, lambda i, k, c, n=a.ndim: (0,) * n) for a in fixed] + [tall_spec(a) for a in tall],
            out_specs=(out, out),
            scratch_shapes=scratch,
        ),
        out_shape=(jax.ShapeDtypeStruct((shares // 2, tile, cols), BF16),) * 2,
        compiler_params=params(60),
        cost_estimate=cost(),
    )(core, *fixed, *tall)


def put_share(send_ref, keep_ref, pieces):
    def store(ref):
        at = 0
        for piece in pieces:
            ref[0, :, at:at + piece.shape[1]] = piece.astype(BF16)
            at += piece.shape[1]

    @pl.when(pl.program_id(1) == 0)
    def _():
        store(send_ref)

    @pl.when(pl.program_id(1) == 1)
    def _():
        store(keep_ref)


def attn_grads_kernel(seqs, kv, group, core_ref, back_ref, mix_ref, norm_ref, *refs):
    grad_refs, (send_ref, keep_ref, rows_ref) = refs[:seqs], refs[seqs:]

    @pl.when((pl.program_id(0) == 0) & (pl.program_id(1) == 0))
    def _():
        gather(back_ref, rows_ref, seqs, kv, group)

    rows = rows_ref.shape[0]
    left = norm_ref[...].reshape(rows, norm_ref.shape[2])
    grad = jnp.concatenate([ref[...] for ref in grad_refs], axis=0)
    mixed = mix_ref[...].reshape(rows, mix_ref.shape[2])
    put_share(send_ref, keep_ref, [dot_lt(left, rows_ref[...]), dot_lt(grad, mixed)])


def attn_grads(core, back, mixed, normed, g_attns, kv, shares):
    seqs, loc, width = normed.shape
    group = back.shape[2] // HEAD_DIM - 2
    cols = kv * back.shape[2]
    scratch = [pltpu.VMEM((seqs * loc, cols), BF16)]
    body = functools.partial(attn_grads_kernel, seqs, kv, group)
    return shares_call(body, (back, mixed), (normed,) + tuple(g_attns), cols + mixed.shape[2], scratch, core, shares)


def ffn_grads_kernel(seqs, count, core_ref, *refs):
    rights, lefts = refs[:count * seqs], refs[count * seqs:-3]
    send_ref, keep_ref, right_ref = refs[-3:]
    lefts = [ref for ref in lefts if len(ref.shape) == 2 and ref.shape[1] < right_ref.shape[2]]

    @pl.when((pl.program_id(0) == 0) & (pl.program_id(1) == 0))
    def _():
        loc = rights[0].shape[0]
        for i in range(count):
            for s in range(seqs):
                right_ref[i, s * loc:(s + 1) * loc, :] = rights[i * seqs + s][...]

    left = jnp.concatenate([ref[...] for ref in lefts], axis=0)
    put_share(send_ref, keep_ref, [dot_lt(left, right_ref[i]) for i in range(count)])


def ffn_grads(core, rights, lefts, before, total, shares):
    seqs, count = len(rights[0]), len(rights)
    loc, units = rights[0][0].shape
    width = lefts[0].shape[1]
    tile = width // shares
    start = total - count if before else 0
    fixed = sum((tuple(r) for r in rights), ())
    left = [pl.BlockSpec((a.shape[0], tile), lambda i, k, c: (0, 2 * i + jnp.where(k == 0, 1 - c[0], c[0]))) for a in lefts]
    out = pl.BlockSpec((1, tile, count * units), lambda i, k, c: (i, 0, start // count))
    args = fixed + tuple(lefts) + tuple(before)
    return pl.pallas_call(
        functools.partial(ffn_grads_kernel, seqs, count),
        grid_spec=pltpu.PrefetchScalarGridSpec(
            num_scalar_prefetch=1,
            grid=(shares // 2, 2),
            in_specs=[pl.BlockSpec((loc, units), lambda i, k, c: (0, 0))] * len(fixed)
            + left
            + [pl.BlockSpec(memory_space=pl.ANY)] * len(before),
            out_specs=(out, out),
            scratch_shapes=[pltpu.VMEM((count, seqs * loc, units), BF16)],
        ),
        out_shape=(jax.ShapeDtypeStruct((shares // 2, tile, total * units), BF16),) * 2,
        input_output_aliases={len(args) - 1: 0, len(args): 1} if before else {},
        compiler_params=params(60),
        cost_estimate=cost(),
    )(core, *args)


def fold_two_kernel(place_ref, *refs):
    keeps, gots, outs = refs[:4], refs[4:8], refs[8:]
    for keep, got, out in zip(keeps, gots, outs):
        out[0] = (keep[0, 0].astype(F32) + got[0, 0].astype(F32)).astype(BF16)


def fold_two(place, keep, got):
    _, rows, cols = keep.shape
    half = rows // 2
    keep, got = keep.reshape(2, 2, rows, cols), got.reshape(2, 2, rows, cols)
    tile = half // 2
    ins = []
    for own in (0, 1):
        ins.append(pl.BlockSpec((1, 1, tile, cols), lambda i, j, p, own=own: (i, jnp.where(own == 1, p[0], 1 - p[0]), j, 0)))
    for own in (0, 1):
        ins.append(pl.BlockSpec((1, 1, tile, cols), lambda i, j, p, own=own: (jnp.where(own == 1, p[1], 1 - p[1]), i, j + 2, 0)))
    return pl.pallas_call(
        fold_two_kernel,
        grid_spec=pltpu.PrefetchScalarGridSpec(
            num_scalar_prefetch=1,
            grid=(2, 2),
            in_specs=ins + ins,
            out_specs=(pl.BlockSpec((1, tile, cols), lambda i, j, p: (i, j, 0)),) * 4,
        ),
        out_shape=(jax.ShapeDtypeStruct((2, half, cols), BF16),) * 4,
        compiler_params=params(60),
        cost_estimate=cost(),
    )(place, keep, keep, keep, keep, got, got, got, got)


def fold_three(place, upper, upper_got, lower, lower_got):
    _, half, cols = upper.shape
    tile = half // 2
    ins = []
    for axis in (1, 0):
        for own in (0, 1):
            ins.append(pl.BlockSpec((1, 1, tile, cols), lambda j, p, own=own, axis=axis: (0, jnp.where(own == 1, p[axis], 1 - p[axis]), j, 0)))
    flat = pl.BlockSpec((1, tile, cols), lambda j, p: (0, j, 0))
    u, ug, l, lg = (a[None] for a in (upper, upper_got, lower, lower_got))
    res = pl.pallas_call(
        fold_two_kernel,
        grid_spec=pltpu.PrefetchScalarGridSpec(
            num_scalar_prefetch=1, grid=(2,), in_specs=ins + ins, out_specs=(flat,) * 4
        ),
        out_shape=(jax.ShapeDtypeStruct((1, half, cols), BF16),) * 4,
        compiler_params=params(60),
        cost_estimate=cost(),
    )(place, u, u, l, l, ug, ug, lg, lg)
    return [a[0] for a in res]


def fold_four_kernel(widths, upper, upper_got, lower, lower_got, *outs):
    half = upper.shape[0]
    for at, (one, two) in enumerate(((upper, upper_got), (lower, lower_got))):
        start = 0
        for out, width in zip(outs, widths):
            part = one[:, start:start + width].astype(F32) + two[:, start:start + width].astype(F32)
            if out is outs[-1]:
                out[:, at * half:(at + 1) * half] = part.T
            else:
                out[at * half:(at + 1) * half, :] = part
            start += width


def fold_four(widths, upper, upper_got, lower, lower_got):
    rows = 2 * upper.shape[0]
    shapes = [(rows, w) for w in widths[:-1]] + [(widths[-1], rows)]
    return pl.pallas_call(
        functools.partial(fold_four_kernel, widths),
        out_shape=tuple(jax.ShapeDtypeStruct(shape, F32) for shape in shapes),
        in_specs=[VMEM] * 4,
        out_specs=(VMEM,) * len(widths),
        compiler_params=params(40),
        cost_estimate=cost(),
    )(upper, upper_got, lower, lower_got)


def finish_kernel(seqs, mid_ref, x_ref, gain_ref, *refs):
    inner, ends, resids, out_ref = refs[:seqs], refs[seqs:2 * seqs], refs[2 * seqs:3 * seqs], refs[3 * seqs]
    gain = gain_ref[...].astype(F32)
    for s in range(seqs):
        grad = jnp.where(mid_ref[0] == 1, inner[s][...].astype(F32), ends[s][...].astype(F32))
        x = x_ref[s].astype(F32)
        inv = lax.rsqrt(jnp.mean(x * x, axis=-1, keepdims=True) + EPS)
        unit = x * inv
        scaled = grad * gain
        back = inv * (scaled - unit * jnp.mean(scaled * unit, axis=-1, keepdims=True))
        out_ref[:, s, :] = resids[s][...] + back


def by_seq(group, seqs, loc, tile):
    per = seqs // len(group)
    return [
        (group[s // per], pl.BlockSpec((tile, group[0].shape[1]), lambda i, at=(s % per) * (loc // tile): (i + at, 0)))
        for s in range(seqs)
    ]


def finish(mid, x, gain, inner, ends, resids):
    seqs, loc, width = x.shape
    tile = 32
    parts = by_seq(inner, seqs, loc, tile) + by_seq(ends, seqs, loc, tile) + by_seq(resids, seqs, loc, tile)
    return pl.pallas_call(
        functools.partial(finish_kernel, seqs),
        grid=(loc // tile,),
        out_shape=jax.ShapeDtypeStruct((loc, seqs, width), F32),
        in_specs=[SMEM, pl.BlockSpec((seqs, tile, width), lambda i: (0, i, 0)), pl.BlockSpec((1, width), lambda i: (0, 0))]
        + [spec for _, spec in parts],
        out_specs=pl.BlockSpec((tile, seqs, width), lambda i: (i, 0, 0)),
        compiler_params=params(60),
        cost_estimate=cost(),
    )(mid, x, gain, *(a for a, _ in parts))


def output_kernel(seqs, mid_ref, x_ref, *refs):
    attn, inner, ends, out_ref, wide = refs[:seqs], refs[seqs:2 * seqs], refs[2 * seqs:3 * seqs], refs[3 * seqs], refs[3 * seqs + 1]
    for s in range(seqs):
        down = jnp.where(mid_ref[0] == 1, inner[s][...].astype(F32), ends[s][...].astype(F32))
        wide[:, s, :] = x_ref[s].astype(F32) + attn[s][...].astype(F32) + down
    out_ref[...] = wide[...].astype(BF16)


def block_output(mid, x, attn, inner, ends):
    seqs, loc, width = x.shape
    tile = 32
    parts = by_seq(attn, seqs, loc, tile) + by_seq(inner, seqs, loc, tile) + by_seq(ends, seqs, loc, tile)
    return pl.pallas_call(
        functools.partial(output_kernel, seqs),
        grid=(loc // tile,),
        out_shape=jax.ShapeDtypeStruct((loc, seqs, width), BF16),
        in_specs=[SMEM, pl.BlockSpec((seqs, tile, width), lambda i: (0, i, 0))] + [spec for _, spec in parts],
        out_specs=pl.BlockSpec((tile, seqs, width), lambda i: (i, 0, 0)),
        scratch_shapes=[pltpu.VMEM((tile, seqs, width), F32)],
        compiler_params=params(60),
        cost_estimate=cost(),
    )(mid, x, *(a for a, _ in parts))


def add_kernel(left, right, out):
    out[...] = (left[...].astype(F32) + right[...].astype(F32)).astype(BF16)


def add(left, right):
    return pl.pallas_call(
        add_kernel,
        out_shape=jax.ShapeDtypeStruct(left.shape, BF16),
        in_specs=[VMEM, VMEM],
        out_specs=VMEM,
        compiler_params=params(16),
        cost_estimate=cost(),
    )(left, right)


def rope_tables(positions, head_dim):
    half = head_dim // 2
    freq = jnp.exp(jnp.arange(half, dtype=jnp.float32) * (-2.0 * math.log(THETA) / head_dim))
    angles = positions.astype(jnp.float32)[:, None] * freq[None, :]
    return (jnp.cos(angles), jnp.sin(angles))


def rotate(values, cosine, sine):
    half = values.shape[-1] // 2
    first = values[..., :half]
    second = values[..., half:]
    cosine = cosine[:, None, None, :]
    sine = sine[:, None, None, :]
    return jnp.concatenate(
        [first * cosine - second * sine, second * cosine + first * sine], axis=-1
    )


def inverse_rms(values):
    return lax.rsqrt(jnp.mean(values * values, axis=-1, keepdims=True) + EPS)


def norm_back(values, inverse, gain, grad):
    unit = values * inverse
    scaled = grad * gain
    back = inverse * (scaled - unit * jnp.mean(scaled * unit, axis=-1, keepdims=True))
    return (back, jnp.sum(grad * unit, axis=(0, 1)))


def matmul(values, weight):
    return jnp.einsum("lsd,de->lse", values, weight, preferred_element_type=jnp.float32)


def matmul_back(values, weight):
    return jnp.einsum("lse,de->lsd", values, weight, preferred_element_type=jnp.float32)


def weight_grad(left, right):
    return jnp.einsum("lsd,lse->de", left, right, preferred_element_type=jnp.float32)


def general(
    hidden_in,
    block_order,
    seq_labels,
    exit_scales,
    attn_gain,
    w_query,
    w_key,
    w_value,
    w_out,
    mlp_gain,
    w_gate,
    w_up,
    w_down,
    d_out,
):
    f32 = jnp.float32
    bf16 = jnp.bfloat16
    loc, seqs, width = hidden_in.shape
    head_dim = HEAD_DIM
    q_heads = w_query.shape[1] // head_dim
    kv_heads = w_key.shape[1] // head_dim
    group = q_heads // kv_heads
    scale = head_dim ** (-0.5)
    blocks_all = block_order.shape[0]
    total_rows = loc * lax.axis_size("blk")
    key_rows = math.gcd(512, total_rows)
    block_count = total_rows // key_rows
    kv_width = 2 * kv_heads * head_dim
    positions = block_order[lax.axis_index("blk")] * loc + jnp.arange(loc, dtype=jnp.int32)
    cosine, sine = rope_tables(positions, head_dim)

    def key_positions(start, count):
        index = start + jnp.arange(count, dtype=jnp.int32)
        owner = index // loc
        table = jnp.sum(
            jnp.where(
                owner[:, None] == jnp.arange(blocks_all, dtype=jnp.int32)[None, :],
                block_order[None, :],
                0,
            ),
            axis=1,
        )
        return table * loc + index % loc

    xin = hidden_in.astype(f32)
    inv_a = inverse_rms(xin)
    gain_a = attn_gain.astype(f32)
    normed = (xin * inv_a * gain_a).astype(bf16)
    query_bf = rotate(
        matmul(normed, w_query).reshape(loc, seqs, q_heads, head_dim), cosine, sine
    ).astype(bf16)
    keys_bf = (
        rotate(matmul(normed, w_key).reshape(loc, seqs, kv_heads, head_dim), cosine, sine)
        .astype(bf16)
        .reshape(loc, seqs, kv_heads * head_dim)
    )
    vals_bf = matmul(normed, w_value).astype(bf16)
    query_g = query_bf.reshape(loc, seqs, kv_heads, group, head_dim)
    starts = jnp.arange(block_count, dtype=jnp.int32) * key_rows
    top = jnp.full((seqs, kv_heads, group, loc), NEG, f32)
    key_part = lax.all_gather(keys_bf, "blk", axis=0, tiled=True)
    val_part = lax.all_gather(vals_bf, "blk", axis=0, tiled=True)
    count = key_part.shape[0]
    kk = key_part.reshape(count, seqs, kv_heads, head_dim)
    vv = val_part.reshape(count, seqs, kv_heads, head_dim)
    mask = key_positions(jnp.int32(0), count)[None, :] <= positions[:, None]
    raw = jnp.einsum("lsngd,msnd->snglm", query_g, kk, preferred_element_type=f32)
    scores = jnp.where(mask, raw * scale, NEG)
    new_top = jnp.maximum(top, jnp.max(scores, axis=-1))
    weights = jnp.where(mask, jnp.exp(scores - new_top[..., None]), 0.0)
    total = jnp.sum(weights, axis=-1)
    acc = jnp.einsum("snglm,msnd->sngld", weights.astype(bf16), vv, preferred_element_type=f32)
    top, total, acc = (new_top, total, acc)
    lse = top + jnp.log(total)
    mixed_raw = acc / total[..., None]
    mixed_bf = (
        mixed_raw.transpose(3, 0, 1, 2, 4).reshape(loc, seqs, q_heads * head_dim).astype(bf16)
    )
    resid = xin + lax.psum(matmul(mixed_bf, w_out).astype(jnp.bfloat16), "tp").astype(jnp.float32)
    inv_m = inverse_rms(resid)
    gain_m = mlp_gain.astype(f32)
    normed_m = (resid * inv_m * gain_m).astype(bf16)
    gate = matmul(normed_m, w_gate)
    up = matmul(normed_m, w_up)
    sig = jax.nn.sigmoid(gate)
    silu = gate * sig
    hidden = (silu * up).astype(bf16)
    output = resid + lax.psum(matmul(hidden, w_down).astype(jnp.bfloat16), "tp").astype(jnp.float32)
    block_out = output.astype(bf16)
    scale_rows = jnp.where(seq_labels == 1, exit_scales[1], exit_scales[0])
    cot = d_out.astype(f32) * scale_rows[None, :, None]
    g_down = cot.astype(bf16)
    d_w_down = weight_grad(hidden, g_down)
    d_hidden = matmul_back(g_down, w_down)
    g_up = (d_hidden * silu).astype(bf16)
    g_gate = (d_hidden * up * (sig * (1.0 + gate * (1.0 - sig)))).astype(bf16)
    d_w_gate = weight_grad(normed_m, g_gate)
    d_w_up = weight_grad(normed_m, g_up)
    d_nm = lax.psum(
        (matmul_back(g_gate, w_gate) + matmul_back(g_up, w_up)).astype(jnp.bfloat16), "tp"
    ).astype(jnp.float32)
    d_resid_norm, d_mlp_gain = norm_back(resid, inv_m, gain_m, d_nm)
    d_resid = cot + d_resid_norm
    g_attn = d_resid.astype(bf16)
    d_w_out = weight_grad(mixed_bf, g_attn)
    g_mixed = matmul_back(g_attn, w_out).astype(bf16)
    g_mixed_g = g_mixed.reshape(loc, seqs, kv_heads, group, head_dim)
    delta = jnp.sum(g_mixed_g.astype(f32).transpose(1, 2, 3, 0, 4) * mixed_raw, axis=-1)
    whole_keys, whole_vals = (
        lax.all_gather(keys_bf, "blk", axis=0, tiled=True),
        lax.all_gather(vals_bf, "blk", axis=0, tiled=True),
    )

    def probe(kk, vv, start, count):
        mask = key_positions(start, count)[None, :] <= positions[:, None]
        raw = jnp.einsum("lsngd,msnd->snglm", query_g, kk, preferred_element_type=f32)
        probs = jnp.where(mask, jnp.exp(raw * scale - lse[..., None]), 0.0)
        d_probs = jnp.einsum("lsngd,msnd->snglm", g_mixed_g, vv, preferred_element_type=f32)
        g_scores = (probs * (d_probs - delta[..., None]) * scale).astype(bf16)
        return (g_scores, probs)

    def kv_pair(g_scores, probs, count):
        d_keys = jnp.einsum("snglm,lsngd->msnd", g_scores, query_g, preferred_element_type=f32)
        d_vals = jnp.einsum(
            "snglm,lsngd->msnd", probs.astype(bf16), g_mixed_g, preferred_element_type=f32
        )
        return jnp.concatenate([d_keys, d_vals], axis=2).reshape(count, seqs, kv_width)

    scan_items = (
        whole_keys.reshape(block_count, key_rows, seqs, -1),
        whole_vals.reshape(block_count, key_rows, seqs, -1),
        starts,
    )
    zero_query = jnp.zeros((loc, seqs, kv_heads, group, head_dim), f32)

    def back_step(d_query, item):
        key_part, val_part, start = item
        kk = key_part.reshape(key_rows, seqs, kv_heads, head_dim)
        vv = val_part.reshape(key_rows, seqs, kv_heads, head_dim)
        g_scores, probs = probe(kk, vv, start, key_rows)
        d_query = d_query + jnp.einsum(
            "snglm,msnd->lsngd", g_scores, kk, preferred_element_type=f32
        )
        return (d_query, kv_pair(g_scores, probs, key_rows))

    d_query, kv_terms = lax.scan(back_step, zero_query, scan_items)
    kv_local = lax.psum_scatter(
        kv_terms.reshape(total_rows, seqs, kv_width).astype(jnp.bfloat16),
        "blk",
        scatter_dimension=0,
        tiled=True,
    ).astype(jnp.float32)
    kv_local = kv_local.reshape(loc, seqs, 2, kv_heads, head_dim)
    g_q = (
        rotate(d_query.reshape(loc, seqs, q_heads, head_dim), cosine, -sine)
        .astype(bf16)
        .reshape(loc, seqs, q_heads * head_dim)
    )
    g_k = (
        rotate(kv_local[:, :, 0], cosine, -sine)
        .astype(bf16)
        .reshape(loc, seqs, kv_heads * head_dim)
    )
    g_v = kv_local[:, :, 1].astype(bf16).reshape(loc, seqs, kv_heads * head_dim)
    d_w_query = weight_grad(normed, g_q)
    d_w_key = weight_grad(normed, g_k)
    d_w_value = weight_grad(normed, g_v)
    d_n = lax.psum(
        (matmul_back(g_q, w_query) + matmul_back(g_k, w_key) + matmul_back(g_v, w_value)).astype(
            jnp.bfloat16
        ),
        "tp",
    ).astype(jnp.float32)
    d_in_norm, d_attn_gain = norm_back(xin, inv_a, gain_a, d_n)
    d_hidden_in = d_resid + d_in_norm
    d_attn_gain, d_w_query, d_w_key, d_w_value, d_w_out, d_mlp_gain, d_w_gate, d_w_up, d_w_down = (
        lax.psum_scatter(
            d_attn_gain.astype(jnp.bfloat16), "blk", scatter_dimension=0, tiled=True
        ).astype(jnp.float32),
        lax.psum_scatter(
            d_w_query.astype(jnp.bfloat16), "blk", scatter_dimension=0, tiled=True
        ).astype(jnp.float32),
        lax.psum_scatter(
            d_w_key.astype(jnp.bfloat16), "blk", scatter_dimension=0, tiled=True
        ).astype(jnp.float32),
        lax.psum_scatter(
            d_w_value.astype(jnp.bfloat16), "blk", scatter_dimension=0, tiled=True
        ).astype(jnp.float32),
        lax.psum_scatter(
            d_w_out.astype(jnp.bfloat16), "blk", scatter_dimension=1, tiled=True
        ).astype(jnp.float32),
        lax.psum_scatter(
            d_mlp_gain.astype(jnp.bfloat16), "blk", scatter_dimension=0, tiled=True
        ).astype(jnp.float32),
        lax.psum_scatter(
            d_w_gate.astype(jnp.bfloat16), "blk", scatter_dimension=0, tiled=True
        ).astype(jnp.float32),
        lax.psum_scatter(
            d_w_up.astype(jnp.bfloat16), "blk", scatter_dimension=0, tiled=True
        ).astype(jnp.float32),
        lax.psum_scatter(
            d_w_down.astype(jnp.bfloat16), "blk", scatter_dimension=1, tiled=True
        ).astype(jnp.float32),
    )
    return (
        block_out,
        d_hidden_in,
        d_attn_gain,
        d_w_query,
        d_w_key,
        d_w_value,
        d_w_out,
        d_mlp_gain,
        d_w_gate,
        d_w_up,
        d_w_down,
    )


class Steps:
    def __init__(self):
        self.last = None

    def enter(self, *values):
        if self.last is not None:
            values, _ = lax.optimization_barrier((values, self.last))
        return values if len(values) > 1 else values[0]

    def leave(self, value):
        self.last = value
        return value


class Line:
    def __init__(self, steps, middle, parts):
        self.steps, self.middle, self.parts = steps, middle, list(parts)
        count = len(self.parts)
        self.first, self.half, self.second, self.total, self.third, self.done = ([None] * count for _ in range(6))

    def one(self, c):
        self.first[c] = lax.ppermute(self.parts[c], "tp", [(0, 1), (3, 2)])

    def two(self, c):
        part, got = self.steps.enter(self.parts[c], self.first[c])
        self.half[c] = self.steps.leave(add(part, got))
        self.second[c] = lax.ppermute(self.half[c], "tp", [(1, 2), (2, 1)])

    def three(self, c):
        half, got = self.steps.enter(self.half[c], self.second[c])
        self.total[c] = self.steps.leave(add(half, got))
        self.third[c] = lax.ppermute(self.total[c], "tp", [(1, 0), (2, 3)])

    def four(self, c):
        total, got = self.steps.enter(self.total[c], self.third[c])
        self.done[c] = self.steps.leave(jnp.where(self.middle, total, got))

    def five(self, c):
        self.third[c] = self.steps.leave(self.steps.enter(self.third[c]))


def partner(bit):
    return [(i, i ^ bit) for i in range(8)]


class Scatter:
    def __init__(self, steps, place, send, keep):
        self.steps, self.place, self.send, self.keep = steps, place, send, keep

    def one_go(self):
        self.got = lax.ppermute(self.steps.enter(self.send), "blk", partner(1))

    def two(self):
        keep, got = self.steps.enter(self.keep, self.got)
        self.away, self.upper, self.off, self.lower = fold_two(self.place, keep, got)
        self.steps.leave(self.upper)

    def two_go(self, first=2, second=4):
        away, off = self.steps.enter(self.away, self.off)
        self.upper_got = lax.ppermute(away, "blk", partner(first))
        self.lower_got = lax.ppermute(off, "blk", partner(second))

    def three(self):
        values = self.steps.enter(self.upper, self.upper_got, self.lower, self.lower_got)
        self.away, self.upper, self.off, self.lower = fold_three(self.place, *values)
        self.steps.leave(self.upper)

    def three_go(self):
        self.two_go(4, 2)

    def four(self, widths):
        values = self.steps.enter(self.upper, self.upper_got, self.lower, self.lower_got)
        res = fold_four(widths, *values)
        self.steps.leave(res[0])
        return res


def inverse(values):
    return lax.rsqrt(jnp.mean(values * values, axis=-1, keepdims=True) + EPS)


def tables(positions):
    cosine, sine = rope_tables(positions, HEAD_DIM)
    return jnp.concatenate([cosine, cosine], axis=1), jnp.concatenate([-sine, sine], axis=1)


def fast(
    hidden_in,
    block_order,
    seq_labels,
    exit_scales,
    attn_gain,
    w_query,
    w_key,
    w_value,
    w_out,
    mlp_gain,
    w_gate,
    w_up,
    w_down,
    d_out,
):
    loc, seqs, width = hidden_in.shape
    blocks = block_order.shape[0]
    rows = seqs * loc
    units = w_gate.shape[1]
    kv = w_key.shape[1] // HEAD_DIM
    group = w_query.shape[1] // w_key.shape[1]
    wide = group * HEAD_DIM
    me = lax.axis_index("blk")
    line = lax.axis_index("tp")
    middle = (line == 1) | (line == 2)
    index = jnp.arange(blocks, dtype=jnp.int32)
    at = jnp.sum(jnp.where(block_order[None, :] == index[:, None], index[None, :], 0), axis=1)
    mine = jnp.sum(jnp.where(index == me, block_order, 0)) * loc + jnp.arange(loc, dtype=jnp.int32)
    steps = Steps()
    enter, leave = steps.enter, steps.leave

    x = hidden_in.transpose(1, 0, 2)
    cosine, sine = tables(mine)
    messages, normed = project(x, attn_gain[None, :], cosine, sine, w_query, w_key, w_value)
    leave(messages)
    rec = lax.all_to_all(messages, "blk", 0, 0, tiled=True)
    scales = jnp.where(seq_labels == 1, exit_scales[1], exit_scales[0])
    cot = enter(d_out).transpose(1, 0, 2).astype(F32) * scales[:, None, None]
    g_down = leave(cot.astype(BF16).reshape(rows, width))
    d_hidden = leave(dot_rt(g_down, w_down).astype(BF16))
    mixed, full, lse = attend(at, enter(rec), group)
    leave(mixed)
    mixed = lax.all_to_all(mixed, "blk", 0, 0, tiled=True)
    all_cosine, all_sine = tables(enter(jnp.arange(blocks * loc, dtype=jnp.int32)))
    leave(all_cosine)
    mixed, parts = out_project(enter(mixed), w_out, seqs)
    leave(mixed)

    gain_m = mlp_gain.astype(F32)
    attn = Line(steps, middle, parts)
    back = Line(steps, middle, [None] * seqs)
    norms, hiddens, gates, ups, gains = ([None] * seqs for _ in range(5))

    def feed(s):
        total = attn.done[s]
        resid = x[s].astype(F32) + total.astype(F32)
        unit = resid * inverse(resid)
        norm = (unit * gain_m).astype(BF16)
        gate = dot(norm, w_gate)
        up = dot(norm, w_up)
        sig = jax.nn.sigmoid(gate)
        silu = gate * sig
        grad_h = d_hidden[s * loc:(s + 1) * loc].astype(F32)
        g_up = (grad_h * silu).astype(BF16)
        g_gate = (grad_h * up * (sig * (1.0 + gate * (1.0 - sig)))).astype(BF16)
        grad = dot_rt(g_gate, w_gate) + dot_rt(g_up, w_up)
        gains[s] = jnp.sum(grad * unit, axis=0)
        back.parts[s] = leave(grad.astype(BF16))
        norms[s], gates[s], ups[s] = norm, g_gate, g_up
        hiddens[s] = (silu * up).astype(BF16)

    d_resids, g_attns, sends = ([None] * seqs for _ in range(3))

    def norm_back(s):
        resid = x[s].astype(F32) + attn.done[s].astype(F32)
        inv = inverse(resid)
        unit = resid * inv
        scaled = back.done[s].astype(F32) * gain_m
        d_resids[s] = cot[s] + inv * (scaled - unit * jnp.mean(scaled * unit, axis=-1, keepdims=True))
        g_attns[s] = d_resids[s].astype(BF16)
        sends[s] = leave(dot_rt(g_attns[s], w_out).astype(BF16))

    def run(lines, *texts):
        for word in " ".join(texts).split():
            name, c = word[:-1], int(word[-1])
            if name == "F":
                feed(c)
            elif name == "N":
                norm_back(c)
            elif name == "O":
                hidden = jnp.concatenate(enter(hiddens[2 * c:2 * c + 2]), axis=0)
                outs.parts[c] = leave(dot(hidden, w_down).astype(BF16))
            else:
                obj = lines[name[0]]
                (obj.one, obj.two, obj.three, obj.four, obj.five)[int(name[1]) - 1](c)

    outs = Line(steps, middle, [None] * 2)
    lines = {"a": attn, "b": back, "c": outs}
    core = (me % 2).astype(jnp.int32)[None]
    place = jnp.stack([(me // 2) % 2, me // 4]).astype(jnp.int32)
    run(
        lines,
        "a10 a11 a12 a13",
        "a20 a21 a30 a22",
        "a31 a40 F0 b10",
        "a23 a32 a41 F1",
        "b11",
    )
    run(
        lines,
        "a33 a42 F2 b12",
        "b20 a43 F3 b13",
        "b21 b30",
    )
    run(
        lines,
        "O0 O1 b22 b31",
        "b40 N0 b23 b32",
        "b41 N1 b33 b42",
        "N2 b43 N3",
    )
    send = jnp.stack(enter(sends)).reshape(seqs, loc, kv, wide).transpose(0, 2, 1, 3).reshape(seqs * kv, loc, wide)
    grad = lax.all_to_all(send, "blk", 0, 0, tiled=True)
    made = leave(ffn_grads(core, *enter([gates, ups], norms), (), 3, blocks))
    run(lines, "c10 c11 c20")
    grads = leave(attend_back(at, rec, enter(grad), full, lse, all_cosine, all_sine, group))
    grads = lax.all_to_all(grads, "blk", 0, 0, tiled=True)
    send, keep = ffn_grads(core, *enter([hiddens], [g_down], made), 3, blocks)
    leave(keep)
    ffn_sum = Scatter(steps, place, send, keep)
    run(lines, "c21 c30")

    grads = enter(grads)
    parts = input_grads(grads, x, w_query, w_key, w_value, [g[None, :] for g in gains], 2)
    ins = Line(steps, middle, parts)
    leave(ins.parts[0])
    lines["d"] = ins
    run(lines, "d10 d11")
    ffn_sum.one_go()
    send, keep = attn_grads(*enter(core, grads, mixed, normed, g_attns), kv, blocks)
    leave(keep)
    attn_sum = Scatter(steps, place, send, keep)
    ffn_sum.two()
    ffn_sum.two_go()
    run(lines, "c31 c50 d20")
    attn_sum.one_go()
    run(lines, "d21 d30")
    attn_sum.two()
    attn_sum.two_go()
    ffn_sum.three()
    ffn_sum.three_go()
    run(lines, "c51")
    mid = middle.astype(jnp.int32)[None]
    block_out = leave(block_output(mid, x, attn.done, enter(outs.total), outs.third))
    attn_sum.three()
    run(lines, "d31")
    attn_sum.three_go()
    run(lines, "d40")
    extra = ins.done[0][2 * loc:2 * loc + 4].astype(F32)
    both = (extra[0::2] + extra[1::2]).reshape(2, 8, width // 8)
    both = leave(both + lax.ppermute(both, "blk", partner(1)))
    others = [lax.ppermute(enter(both), "blk", partner(bit)) for bit in (2, 4, 6)]
    d_w_gate, d_w_up, d_w_down = ffn_sum.four((units, units, units))
    run(lines, "d51")
    d_hidden_in = finish(
        mid,
        x,
        attn_gain[None, :],
        ins.total,
        ins.third,
        d_resids,
    )
    leave(d_hidden_in)
    d_w_query, d_w_key, d_w_value, d_w_out = attn_sum.four((kv * wide, kv * HEAD_DIM, kv * HEAD_DIM, kv * wide))
    others = enter(others)
    both = both + others[0] + others[1] + others[2]
    both = lax.dynamic_index_in_dim(both, me, 1, keepdims=False)
    return (
        block_out,
        d_hidden_in,
        both[0],
        d_w_query,
        d_w_key,
        d_w_value,
        d_w_out,
        both[1],
        d_w_gate,
        d_w_up,
        d_w_down,
    )


def per_device(*args):
    seqs = args[0].shape[1]
    kv_heads = args[6].shape[1] // HEAD_DIM
    fits = lax.axis_size("blk") == 8 and lax.axis_size("tp") == 4 and seqs * kv_heads == 8
    return (fast if fits else general)(*args)


def solution(mesh):
    return jax.shard_map(
        per_device,
        mesh=mesh,
        in_specs=(
            P("blk", None, None),
            P(),
            P(),
            P(),
            P(),
            P(None, "tp"),
            P(None, "tp"),
            P(None, "tp"),
            P("tp", None),
            P(),
            P(None, "tp"),
            P(None, "tp"),
            P("tp", None),
            P("blk", None, None),
        ),
        out_specs=(
            P("blk", None, None),
            P("blk", None, None),
            P("blk"),
            P("blk", "tp"),
            P("blk", "tp"),
            P("blk", "tp"),
            P("tp", "blk"),
            P("blk"),
            P("blk", "tp"),
            P("blk", "tp"),
            P("tp", "blk"),
        ),
        check_vma=False,
    )
```
